32 devices in a mesh: dap: 32 (over z, y, x, core), grp: 1.
Axes of the slice: x: 2, y: 2, z: 4, core: 2. Of those that a mesh axis runs over, the one named last changes fastest.
Arguments:
- pair_rep: bfloat16 [256, 256, 128], P('dap', 'grp'), may hold values from -6 to 6
- chain_ids: int32 [256], replicated, may hold values from 0 to 7, never falling along the last dimension, each value on 1 to 64 neighbouring positions
- crop_lengths: int32 [8], replicated, may hold values from 16 to 64
- ln_in_gain: float32 [2, 128], replicated, may hold values from 0.1 to 1.9
- w_proj: bfloat16 [2, 128, 512], replicated, may hold values from -0.5 to 0.5
- w_gate: bfloat16 [2, 128, 128], replicated, may hold values from -0.5 to 0.5
- ln_out_gain: float32 [2, 128], replicated, may hold values from 0.1 to 1.9
- w_out: bfloat16 [2, 128, 128], replicated, may hold values from -0.5 to 0.5
Outputs:
- pair_out: bfloat16 [256, 256, 128], P('dap', 'grp')
The draws below stay inside these ranges and needn't reach their ends.
Inputs may be any that keep to these rules, and one draw needn't show every extreme that they name: `chain_ids`: chain ids never fall along the residues; each chain holds 1 to 64 residues, and some chain exactly 64.
All inputs are finite; a program needn't handle non-finite values.
Results may differ from the reference program's by a relative error of at most 0.0095.
Values may be sent and summed in bfloat16 or wider, within the bound.
No kernel may reach another device: no remote copies, remote signals or barrier semaphores. Data moves between devices by JAX's collectives and lax.ppermute only.
A program may use at most 64 MiB of HBM per device.

```python
import math
import jax
import jax.numpy as jnp
import numpy as np
from jax import lax

D = 128
H = 128
NCHAIN = 8
N = 256
CHAIN_MOST = 64
CROP_LO = 16
CROP_HI = 65


def touch_ends(drawn, rng, smallest, top_value):
    spot = [jax.random.randint(jax.random.fold_in(rng, axis), (), 0, length) for axis, length in enumerate(drawn.shape)]
    main_axis = drawn.shape.index(max(drawn.shape))
    neighbour = spot[:main_axis] + [(spot[main_axis] + 1) % drawn.shape[main_axis]] + spot[main_axis + 1:]
    return drawn.at[tuple(spot)].set(smallest).at[tuple(neighbour)].set(top_value)


def block_scale(stream_key, dims, shards, smallest, top_value):
    loudness, own = 1.0, jax.random.fold_in(stream_key, 6)
    for position, parts in shards:
        heights = jnp.exp(jax.random.uniform(jax.random.fold_in(own, position), (parts,), jnp.float32, smallest / len(shards), top_value / len(shards)))
        loudness = loudness * jnp.repeat(heights, dims[position] // parts).reshape([-1 if axis == position else 1 for axis in range(len(dims))])
    return loudness


def length_profile(number_of, total, most, slope):
    portions = [(1 << 20) // math.isqrt(rank ** slope) + 1 for rank in range(2, number_of + 1)]
    spare, given = total - most - (number_of - 1), [1] * (number_of - 1)
    while spare > 0:
        free = [i for i in range(number_of - 1) if given[i] < most]
        whole, left = sum([portions[i] for i in free]), spare
        for i in free:
            addition = min(most - given[i], max(1, left * portions[i] // whole), spare)
            given[i] = given[i] + addition
            spare = spare - addition
    return np.array([most] + given)


def uneven(own_key, number_of, total, reach, slope):
    if number_of == 2:
        one = jax.random.randint(own_key, (), max(1, total - reach), min(reach, total - 1) + 1)
        return jnp.stack([one, total - one])
    lengths = jnp.asarray(length_profile(number_of, total, reach, slope), jnp.int32)
    twos = (number_of - 1) // 2
    donor, receiver = lengths[1:1 + 2 * twos:2], lengths[2:2 + 2 * twos:2]
    room = jnp.minimum(donor - 1, reach - receiver)
    passed = jax.random.randint(jax.random.fold_in(own_key, 1), (twos,), 0, 1 << 20) % (room + 1)
    lengths = lengths.at[1:1 + 2 * twos:2].set(donor - passed).at[2:2 + 2 * twos:2].set(receiver + passed)
    return lengths[jax.random.permutation(jax.random.fold_in(own_key, 2), number_of)]


def bell_draw(rng, shape, scale, most, split=(), kind=jnp.bfloat16):
    values = scale * jax.random.normal(rng, shape, jnp.float32)
    if split:
        values = values * block_scale(rng, shape, split, -0.22, 0.18)
    return jnp.clip(values, -most, most).astype(kind)


def setup_inputs(seed: int = 0) -> dict:
    splits = jax.random.split(jax.random.key(seed), 9)
    pair_rep = bell_draw(splits[0], (N, N, D), 1.0, 6.0, ((0, 32),))
    chain_ids = jnp.searchsorted(jnp.cumsum(uneven(splits[1], NCHAIN, N, CHAIN_MOST, 0)), jnp.arange(N), side="right").astype(jnp.int32)
    crop_lengths = touch_ends(jax.random.randint(splits[2], (NCHAIN,), CROP_LO, CROP_HI), jax.random.fold_in(splits[2], 1), CROP_LO, CROP_HI - 1).astype(jnp.int32)
    ln_in_gain = jnp.clip(1.0 + 0.18 * jax.random.normal(splits[3], (2, D), jnp.float32), 0.1, 1.9)
    w_proj = bell_draw(splits[4], (2, D, 4 * H), D ** -0.5, 0.5)
    w_gate = bell_draw(splits[5], (2, D, D), D ** -0.5, 0.5)
    ln_out_gain = jnp.clip(1.0 + 0.18 * jax.random.normal(splits[6], (2, H), jnp.float32), 0.1, 1.9)
    w_out = bell_draw(splits[7], (2, H, D), H ** -0.5, 0.5)
    return dict(pair_rep=pair_rep, chain_ids=chain_ids, crop_lengths=crop_lengths, ln_in_gain=ln_in_gain, w_proj=w_proj, w_gate=w_gate, ln_out_gain=ln_out_gain, w_out=w_out)


epsilon_norm = 1e-05

def residue_valid(chain_ids, crop_lengths):
    count = chain_ids.shape[0]
    chains = jnp.arange(crop_lengths.shape[0], dtype=jnp.int32)
    member = (chain_ids[:, None] == chains[None, :]).astype(jnp.int32)
    counts = lax.optimization_barrier(jnp.sum(member, axis=0))
    starts = jnp.cumsum(counts) - counts
    first = lax.optimization_barrier(jnp.sum(member * starts[None, :], axis=1))
    limit = lax.optimization_barrier(jnp.sum(member * crop_lengths[None, :], axis=1))
    place = jnp.arange(count, dtype=jnp.int32) - first
    return (place < limit).astype(jnp.float32)

def layer_norm(values, gain, axis):
    centre = lax.optimization_barrier(jnp.mean(values, axis=axis, keepdims=True))
    spread = lax.optimization_barrier(jnp.mean((values - centre) ** 2, axis=axis, keepdims=True))
    return (values - centre) * lax.rsqrt(spread + epsilon_norm) * gain

def update(pair_tile, kept, ln_in, w_proj, w_gate, ln_out, w_out, outgoing):
    count = pair_tile.shape[0]
    width = pair_tile.shape[2]
    hidden = w_out.shape[0]
    block = math.gcd(count, 64)
    blocks = count // block
    pair_blocks = pair_tile.reshape(blocks, block, count, width)
    kept_blocks = kept.reshape(blocks, block)

    def project(items):
        row_block, kept_rows = items
        normed = layer_norm(row_block.astype(jnp.float32), ln_in, 2).astype(jnp.bfloat16)
        projected = jnp.einsum('rqc,cf->frq', normed.astype(jnp.float32), w_proj.astype(jnp.float32))
        pair_mask = kept_rows[:, None] * kept[None, :]
        left_op = (jax.nn.sigmoid(projected[:hidden]) * projected[hidden:2 * hidden] * pair_mask).astype(jnp.bfloat16)
        right_op = (jax.nn.sigmoid(projected[2 * hidden:3 * hidden]) * projected[3 * hidden:] * pair_mask).astype(jnp.bfloat16)
        return (left_op, right_op)
    left_op, right_op = lax.map(project, (pair_blocks, kept_blocks))
    left_op = left_op.transpose(1, 0, 2, 3).reshape(hidden, count, count)
    right_op = right_op.transpose(1, 0, 2, 3).reshape(hidden, count, count)

    def contract(items):
        left_chan = items[0].astype(jnp.float32)
        right_chan = items[1].astype(jnp.float32)
        if outgoing:
            product = jnp.dot(left_chan, right_chan.T)
        else:
            product = jnp.dot(left_chan.T, right_chan)
        return product.astype(jnp.bfloat16)
    triangle = lax.map(contract, (left_op, right_op))
    triangle = lax.optimization_barrier(triangle)
    triangle = triangle.reshape(hidden, blocks, block, count).transpose(1, 0, 2, 3)

    def finish(items):
        row_block, tri_block = items
        normed = layer_norm(row_block.astype(jnp.float32), ln_in, 2).astype(jnp.bfloat16)
        gate_value = jax.nn.sigmoid(jnp.einsum('rqc,cd->rqd', normed.astype(jnp.float32), w_gate.astype(jnp.float32)))
        normed_product = layer_norm(tri_block.astype(jnp.float32), ln_out[:, None, None], 0).astype(jnp.bfloat16)
        update_term = jnp.einsum('hrq,hd->rqd', normed_product.astype(jnp.float32), w_out.astype(jnp.float32))
        return (row_block.astype(jnp.float32) + gate_value * update_term).astype(jnp.bfloat16)
    result = lax.map(finish, (pair_blocks, triangle))
    return result.reshape(count, count, width)

def reference(pair_rep, chain_ids, crop_lengths, ln_in_gain, w_proj, w_gate, ln_out_gain, w_out):
    kept = residue_valid(chain_ids, crop_lengths)
    pair_tile = pair_rep
    for layer_index, outgoing in ((0, True), (1, False)):
        pair_tile = update(pair_tile, kept, ln_in_gain[layer_index], w_proj[layer_index], w_gate[layer_index], ln_out_gain[layer_index], w_out[layer_index], outgoing)
    return pair_tile
```

```python
import functools

import jax
import jax.numpy as jnp
from jax import lax
from jax.experimental import pallas as pl
from jax.experimental.pallas import tpu as pltpu
from jax.sharding import PartitionSpec as P

epsilon_norm = 1e-05
F32 = jnp.float32
BF16 = jnp.bfloat16


def residue_valid(chain_ids, crop_lengths):
    count = chain_ids.shape[0]
    chains = jnp.arange(crop_lengths.shape[0], dtype=jnp.int32)
    member = (chain_ids[:, None] == chains[None, :]).astype(jnp.int32)
    counts = jnp.sum(member, axis=0)
    starts = jnp.cumsum(counts) - counts
    first = jnp.sum(member * starts[None, :], axis=1)
    limit = jnp.sum(member * crop_lengths[None, :], axis=1)
    place = jnp.arange(count, dtype=jnp.int32) - first
    return (place < limit).astype(jnp.float32)


def layer_norm(values, gain, axis):
    centre = jnp.mean(values, axis=axis, keepdims=True)
    spread = jnp.mean((values - centre) ** 2, axis=axis, keepdims=True)
    return (values - centre) * lax.rsqrt(spread + epsilon_norm) * gain


def column_rows(right_chan):
    return lax.all_to_all(right_chan, "grp", split_axis=1, concat_axis=2, tiled=True)


def update(pair_tile, pair_mask, ln_in, w_proj, w_gate, ln_out, w_out, outgoing):
    hidden = w_out.shape[0]
    normed = layer_norm(pair_tile.astype(jnp.float32), ln_in, 2).astype(jnp.bfloat16)
    projected = jnp.einsum("rqc,cf->frq", normed, w_proj, preferred_element_type=jnp.float32)
    gate_value = jax.nn.sigmoid(
        jnp.einsum("rqc,cd->rqd", normed, w_gate, preferred_element_type=jnp.float32)
    )
    left_op = (
        jax.nn.sigmoid(projected[:hidden]) * projected[hidden : 2 * hidden] * pair_mask
    ).astype(jnp.bfloat16)
    right_op = (
        jax.nn.sigmoid(projected[2 * hidden : 3 * hidden]) * projected[3 * hidden :] * pair_mask
    ).astype(jnp.bfloat16)
    left_chan, right_chan = (
        lax.all_to_all(left_op, "dap", split_axis=0, concat_axis=1, tiled=True),
        lax.all_to_all(right_op, "dap", split_axis=0, concat_axis=1, tiled=True),
    )
    if outgoing:
        right_rows = column_rows(right_chan)
        triangle = jnp.einsum(
            "hik,hjk->hij",
            lax.all_gather(left_chan, "grp", axis=2, tiled=True),
            right_rows,
            preferred_element_type=jnp.float32,
        )
    else:
        triangle = jnp.einsum(
            "hki,hkj->hij",
            lax.all_gather(left_chan, "grp", axis=2, tiled=True),
            right_chan,
            preferred_element_type=jnp.float32,
        )
    returned = lax.all_to_all(
        triangle.astype(jnp.bfloat16), "dap", split_axis=1, concat_axis=0, tiled=True
    )
    normed_product = layer_norm(returned.astype(jnp.float32), ln_out[:, None, None], 0).astype(
        jnp.bfloat16
    )
    update_term = jnp.einsum(
        "hrq,hd->rqd", normed_product, w_out, preferred_element_type=jnp.float32
    )
    return (pair_tile.astype(jnp.float32) + gate_value * update_term).astype(jnp.bfloat16)


def shards(pair_rep, chain_ids, crop_lengths, ln_in_gain, w_proj, w_gate, ln_out_gain, w_out):
    row_count = pair_rep.shape[0]
    column_count = pair_rep.shape[1]
    kept = residue_valid(chain_ids, crop_lengths)
    row_start = lax.axis_index("dap") * row_count
    column_start = lax.axis_index("grp") * column_count
    kept_rows = lax.dynamic_slice_in_dim(kept, row_start, row_count, 0)
    kept_columns = lax.dynamic_slice_in_dim(kept, column_start, column_count, 0)
    pair_mask = kept_rows[:, None] * kept_columns[None, :]
    pair_tile = pair_rep
    for layer_index, outgoing in ((0, True), (1, False)):
        pair_tile = update(
            pair_tile,
            pair_mask,
            ln_in_gain[layer_index],
            w_proj[layer_index],
            w_gate[layer_index],
            ln_out_gain[layer_index],
            w_out[layer_index],
            outgoing,
        )
    return pair_tile


def dot_nn(a, b):
    return lax.dot_general(a, b, (((1,), (0,)), ((), ())), preferred_element_type=F32)


def dot_nt(a, b):
    return lax.dot_general(a, b, (((1,), (1,)), ((), ())), preferred_element_type=F32)


def dot_tn(a, b):
    return lax.dot_general(a, b, (((0,), (0,)), ((), ())), preferred_element_type=F32)


def sigmoid(v):
    return 0.5 * jnp.tanh(0.5 * v) + 0.5


def one_hot(source, columns):
    place = lax.broadcasted_iota(jnp.int32, (source.shape[0], columns), 1)
    return jnp.where(place == source, 1.0, 0.0).astype(BF16)


def interleave(outer, inner):
    row = lax.broadcasted_iota(jnp.int32, (outer * inner, 1), 0)
    return one_hot((row % inner) * outer + row // inner, outer * inner)


def move(matrix, rows):
    return dot_nn(matrix, rows).astype(BF16)


def kept_residues(ids, crop_ref):
    place = lax.broadcasted_iota(jnp.int32, ids.shape, 1).astype(F32)
    kept = jnp.zeros(ids.shape, F32)
    for chain in range(crop_ref.shape[0]):
        first = jnp.sum(jnp.where(ids < chain, 1.0, 0.0), axis=1, keepdims=True)
        limit = crop_ref[chain].astype(F32)
        inside = jnp.where(ids == chain, 1.0, 0.0) * jnp.where(place - first < limit, 1.0, 0.0)
        kept = kept + inside
    return kept


def norm_rows(values, gain):
    centre = jnp.mean(values, axis=1, keepdims=True)
    apart = values - centre
    spread = jnp.mean(apart * apart, axis=1, keepdims=True)
    return (apart * lax.rsqrt(spread + epsilon_norm) * gain).astype(BF16)


def sorted_projection(w_proj, devices):
    total = w_proj.shape[1]
    hidden = total // 4
    own = hidden // devices
    row = lax.broadcasted_iota(jnp.int32, (total, 1), 0)
    kind = row // (2 * hidden)
    rest = row % (2 * hidden)
    device = rest // (2 * own)
    side = (rest % (2 * own)) // own
    channel = rest % own
    source = (side * 2 + kind) * hidden + device * own + channel
    return dot_nt(one_hot(source, total), w_proj).astype(BF16)


def project_row(normed, weights, mask, send_ref, row):
    count = normed.shape[0]
    half = weights.shape[0] // 2
    projected = dot_nt(weights, normed)
    operand = sigmoid(projected[:half]) * projected[half:] * mask
    shape = send_ref.shape[:2] + (count,)
    send_ref[:, :, row * count : (row + 1) * count] = operand.astype(BF16).reshape(shape)


def row_masks(ids_ref, crop_ref, me_ref, rows):
    kept = kept_residues(ids_ref[...], crop_ref)
    place = lax.broadcasted_iota(jnp.int32, kept.shape, 1)
    masks = []
    for row in range(rows):
        own = jnp.where(place == me_ref[0] * rows + row, kept, 0.0)
        masks.append(kept * jnp.sum(own, axis=1, keepdims=True))
    return masks


def first_kernel(devices, me_ref, crop_ref, ids_ref, pair_ref, gain_ref, w_proj_ref, send_ref):
    rows = pair_ref.shape[0]
    masks = row_masks(ids_ref, crop_ref, me_ref, rows)
    weights = sorted_projection(w_proj_ref[...], devices)
    for row in range(rows):
        normed = norm_rows(pair_ref[row].astype(F32), gain_ref[...])
        project_row(normed, weights, masks[row], send_ref, row)


def gate_kernel(pair_ref, gain_ref, w_gate_ref, gate_ref):
    for row in range(pair_ref.shape[0]):
        normed = norm_rows(pair_ref[row].astype(F32), gain_ref[...])
        gate_ref[row] = sigmoid(dot_nn(normed, w_gate_ref[...]))


def triangle_kernel(outgoing, rows, came_ref, send_ref):
    devices, both, width = came_ref.shape
    own = both // 2
    count = width // rows
    by_channel = interleave(both, devices)
    by_source = interleave(devices, rows)
    came = came_ref[...].reshape(devices * both, width)
    blocks = [
        move(by_channel, came[:, row * count : (row + 1) * count]) for row in range(rows)
    ]

    def channel_rows(channel):
        span = slice(channel * devices, (channel + 1) * devices)
        return jnp.concatenate([block[span] for block in blocks], axis=0)

    products = []
    for channel in range(own):
        left = channel_rows(channel)
        right = channel_rows(own + channel)
        if outgoing:
            product = dot_nt(left, move(by_source, right)).astype(BF16)
        else:
            product = dot_tn(left, right).astype(BF16)
            product = dot_tn(by_source, product).astype(BF16)
        products.append(product)
    low = rows * own // 8
    to_device = interleave(devices, 8)
    for offset in range(low):
        parts = []
        for channel in range(own):
            for high in range(rows // low):
                row = high * low + offset
                parts.append(products[channel][row * devices : (row + 1) * devices])
        sent = move(to_device, jnp.concatenate(parts, axis=0))
        send_ref[:, :, offset * count : (offset + 1) * count] = sent.reshape(devices, 8, count)


def finish_rows(came_ref, pair_ref, gate_ref, gain_ref, w_out_ref):
    devices, eight, width = came_ref.shape
    rows, count, _ = pair_ref.shape
    own = w_out_ref.shape[0] // devices
    hidden = w_out_ref.shape[0]
    low = width // count
    high = rows // low
    came = move(interleave(high, hidden), came_ref[...].reshape(devices * eight, width))
    gain = gain_ref[...]
    square = lax.broadcasted_iota(jnp.int32, (hidden, hidden), 0) == lax.broadcasted_iota(
        jnp.int32, (hidden, hidden), 1
    )
    gain = jnp.sum(jnp.where(square, gain, 0.0), axis=1, keepdims=True)
    for row in range(rows):
        offset = (row % low) * count
        span = (row // low) * hidden
        block = came[span : span + hidden, offset : offset + count].astype(F32)
        centre = jnp.mean(block, axis=0, keepdims=True)
        apart = block - centre
        spread = jnp.mean(apart * apart, axis=0, keepdims=True)
        normed = (apart * lax.rsqrt(spread + epsilon_norm) * gain).astype(BF16)
        term = dot_tn(normed, w_out_ref[...])
        yield row, (pair_ref[row].astype(F32) + gate_ref[row] * term).astype(BF16)


def middle_kernel(
    devices,
    me_ref,
    crop_ref,
    ids_ref,
    came_ref,
    pair_ref,
    gate_ref,
    gain_out_ref,
    w_out_ref,
    gain_in_ref,
    w_proj_ref,
    next_ref,
    send_ref,
):
    masks = row_masks(ids_ref, crop_ref, me_ref, pair_ref.shape[0])
    weights = sorted_projection(w_proj_ref[...], devices)
    for row, fresh in finish_rows(came_ref, pair_ref, gate_ref, gain_out_ref, w_out_ref):
        next_ref[row] = fresh
        normed = norm_rows(fresh.astype(F32), gain_in_ref[...])
        project_row(normed, weights, masks[row], send_ref, row)


def last_kernel(came_ref, pair_ref, gate_ref, gain_out_ref, w_out_ref, next_ref):
    for row, fresh in finish_rows(came_ref, pair_ref, gate_ref, gain_out_ref, w_out_ref):
        next_ref[row] = fresh


VMEM = pl.BlockSpec(memory_space=pltpu.VMEM)
SMEM = pl.BlockSpec(memory_space=pltpu.SMEM)


def layer_of(shape, layer):
    return pl.BlockSpec((None,) + shape[1:], lambda i: (layer,) + (0,) * (len(shape) - 1))


def whole(shape):
    return pl.BlockSpec(shape, lambda i: (0,) * len(shape))


def call(body, name, out, specs, operands):
    single = not isinstance(out, (list, tuple))
    outs = [out] if single else list(out)
    result = pl.pallas_call(
        body,
        out_shape=outs,
        grid=(1,),
        in_specs=specs,
        out_specs=[whole(o.shape) for o in outs],
        compiler_params=pltpu.CompilerParams(vmem_limit_bytes=48 * 1024 * 1024),
        name=name,
    )(*operands)
    return result[0] if single else result


def row_shards(pair_rep, chain_ids, crop_lengths, ln_in_gain, w_proj, w_gate, ln_out_gain, w_out):
    devices = lax.axis_size("dap")
    rows, count, width = pair_rep.shape
    hidden = w_out.shape[1]
    own = hidden // devices
    me = lax.axis_index("dap").reshape(1).astype(jnp.int32)
    ids = chain_ids.reshape(1, count)
    ln_in = ln_in_gain.reshape(2, 1, width)
    ln_out = ln_out_gain.reshape(2, 1, hidden)
    send_shape = jax.ShapeDtypeStruct((devices, 2 * own, rows * count), BF16)
    back_shape = jax.ShapeDtypeStruct((devices, 8, rows * own * count // 8), BF16)
    pair_shape = jax.ShapeDtypeStruct(pair_rep.shape, BF16)
    gate_shape = jax.ShapeDtypeStruct(pair_rep.shape, F32)
    head = [SMEM, SMEM, whole(ids.shape)]

    def exchange(sent):
        return lax.all_to_all(sent, "dap", split_axis=0, concat_axis=0, tiled=True)

    def gates(pair, layer):
        return call(
            gate_kernel,
            "gates",
            gate_shape,
            [whole(pair.shape), layer_of(ln_in.shape, layer), layer_of(w_gate.shape, layer)],
            (pair, ln_in, w_gate),
        )

    sent = call(
        functools.partial(first_kernel, devices),
        "first_operands",
        send_shape,
        head + [whole(pair_rep.shape), layer_of(ln_in.shape, 0), layer_of(w_proj.shape, 0)],
        (me, crop_lengths, ids, pair_rep, ln_in, w_proj),
    )
    gate = gates(pair_rep, 0)
    came = exchange(sent)
    sent = call(
        functools.partial(triangle_kernel, True, rows),
        "outgoing",
        back_shape,
        [whole(came.shape)],
        (came,),
    )
    came = exchange(sent)
    pair, sent = call(
        functools.partial(middle_kernel, devices),
        "finish_and_operands",
        (pair_shape, send_shape),
        head
        + [
            whole(came.shape),
            whole(pair_rep.shape),
            whole(gate.shape),
            layer_of(ln_out.shape, 0),
            layer_of(w_out.shape, 0),
            layer_of(ln_in.shape, 1),
            layer_of(w_proj.shape, 1),
        ],
        (me, crop_lengths, ids, came, pair_rep, gate, ln_out, w_out, ln_in, w_proj),
    )
    gate = gates(pair, 1)
    came = exchange(sent)
    sent = call(
        functools.partial(triangle_kernel, False, rows),
        "incoming",
        back_shape,
        [whole(came.shape)],
        (came,),
    )
    came = exchange(sent)
    return call(
        last_kernel,
        "finish",
        pair_shape,
        [
            whole(came.shape),
            whole(pair_rep.shape),
            whole(gate.shape),
            layer_of(ln_out.shape, 1),
            layer_of(w_out.shape, 1),
        ],
        (came, pair, gate, ln_out, w_out),
    )


def solution(mesh):
    devices = mesh.shape["dap"]
    placed = (P("dap", "grp", None), P(), P(), P(), P(), P(), P(), P())

    def body(*arrays):
        rows, count, width = arrays[0].shape
        hidden = arrays[-1].shape[1]
        plain = (
            mesh.shape["grp"] == 1
            and rows * devices == count
            and count % 128 == 0
            and rows == 8
            and hidden == 4 * devices
        )
        return (row_shards if plain else shards)(*arrays)

    return jax.shard_map(
        body, mesh=mesh, in_specs=placed, out_specs=P("dap", "grp", None), check_vma=False
    )
```

```python
import functools

import jax
import jax.numpy as jnp
from jax import lax
from jax.experimental import pallas as pl
from jax.experimental.pallas import tpu as pltpu
from jax.sharding import PartitionSpec as P

epsilon_norm = 1e-05
F32 = jnp.float32
BF16 = jnp.bfloat16


def residue_valid(chain_ids, crop_lengths):
    count = chain_ids.shape[0]
    chains = jnp.arange(crop_lengths.shape[0], dtype=jnp.int32)
    member = (chain_ids[:, None] == chains[None, :]).astype(jnp.int32)
    counts = jnp.sum(member, axis=0)
    starts = jnp.cumsum(counts) - counts
    first = jnp.sum(member * starts[None, :], axis=1)
    limit = jnp.sum(member * crop_lengths[None, :], axis=1)
    place = jnp.arange(count, dtype=jnp.int32) - first
    return (place < limit).astype(jnp.float32)


def layer_norm(values, gain, axis):
    centre = jnp.mean(values, axis=axis, keepdims=True)
    spread = jnp.mean((values - centre) ** 2, axis=axis, keepdims=True)
    return (values - centre) * lax.rsqrt(spread + epsilon_norm) * gain


def column_rows(right_chan):
    return lax.all_to_all(right_chan, "grp", split_axis=1, concat_axis=2, tiled=True)


def update(pair_tile, pair_mask, ln_in, w_proj, w_gate, ln_out, w_out, outgoing):
    hidden = w_out.shape[0]
    normed = layer_norm(pair_tile.astype(jnp.float32), ln_in, 2).astype(jnp.bfloat16)
    projected = jnp.einsum("rqc,cf->frq", normed, w_proj, preferred_element_type=jnp.float32)
    gate_value = jax.nn.sigmoid(
        jnp.einsum("rqc,cd->rqd", normed, w_gate, preferred_element_type=jnp.float32)
    )
    left_op = (
        jax.nn.sigmoid(projected[:hidden]) * projected[hidden : 2 * hidden] * pair_mask
    ).astype(jnp.bfloat16)
    right_op = (
        jax.nn.sigmoid(projected[2 * hidden : 3 * hidden]) * projected[3 * hidden :] * pair_mask
    ).astype(jnp.bfloat16)
    left_chan, right_chan = (
        lax.all_to_all(left_op, "dap", split_axis=0, concat_axis=1, tiled=True),
        lax.all_to_all(right_op, "dap", split_axis=0, concat_axis=1, tiled=True),
    )
    if outgoing:
        right_rows = column_rows(right_chan)
        triangle = jnp.einsum(
            "hik,hjk->hij",
            lax.all_gather(left_chan, "grp", axis=2, tiled=True),
            right_rows,
            preferred_element_type=jnp.float32,
        )
    else:
        triangle = jnp.einsum(
            "hki,hkj->hij",
            lax.all_gather(left_chan, "grp", axis=2, tiled=True),
            right_chan,
            preferred_element_type=jnp.float32,
        )
    returned = lax.all_to_all(
        triangle.astype(jnp.bfloat16), "dap", split_axis=1, concat_axis=0, tiled=True
    )
    normed_product = layer_norm(returned.astype(jnp.float32), ln_out[:, None, None], 0).astype(
        jnp.bfloat16
    )
    update_term = jnp.einsum(
        "hrq,hd->rqd", normed_product, w_out, preferred_element_type=jnp.float32
    )
    return (pair_tile.astype(jnp.float32) + gate_value * update_term).astype(jnp.bfloat16)


def shards(pair_rep, chain_ids, crop_lengths, ln_in_gain, w_proj, w_gate, ln_out_gain, w_out):
    row_count = pair_rep.shape[0]
    column_count = pair_rep.shape[1]
    kept = residue_valid(chain_ids, crop_lengths)
    row_start = lax.axis_index("dap") * row_count
    column_start = lax.axis_index("grp") * column_count
    kept_rows = lax.dynamic_slice_in_dim(kept, row_start, row_count, 0)
    kept_columns = lax.dynamic_slice_in_dim(kept, column_start, column_count, 0)
    pair_mask = kept_rows[:, None] * kept_columns[None, :]
    pair_tile = pair_rep
    for layer_index, outgoing in ((0, True), (1, False)):
        pair_tile = update(
            pair_tile,
            pair_mask,
            ln_in_gain[layer_index],
            w_proj[layer_index],
            w_gate[layer_index],
            ln_out_gain[layer_index],
            w_out[layer_index],
            outgoing,
        )
    return pair_tile


def dot_nn(a, b):
    return lax.dot_general(a, b, (((1,), (0,)), ((), ())), preferred_element_type=F32)


def dot_nt(a, b):
    return lax.dot_general(a, b, (((1,), (1,)), ((), ())), preferred_element_type=F32)


def dot_tn(a, b):
    return lax.dot_general(a, b, (((0,), (0,)), ((), ())), preferred_element_type=F32)


def sigmoid(v):
    return 0.5 * jnp.tanh(0.5 * v) + 0.5


def one_hot(source, columns):
    place = lax.broadcasted_iota(jnp.int32, (source.shape[0], columns), 1)
    return jnp.where(place == source, 1.0, 0.0).astype(BF16)


def interleave(outer, inner):
    row = lax.broadcasted_iota(jnp.int32, (outer * inner, 1), 0)
    return one_hot((row % inner) * outer + row // inner, outer * inner)


def move(matrix, rows):
    return dot_nn(matrix, rows).astype(BF16)


def selection(slots, width):
    row = lax.broadcasted_iota(jnp.int32, (width, slots.shape[1]), 0).astype(F32)
    return jnp.where(row == slots, 1.0, 0.0).astype(BF16)


def kept_residues(ids, crop_ref):
    place = lax.broadcasted_iota(jnp.int32, ids.shape, 1).astype(F32)
    kept = jnp.zeros(ids.shape, F32)
    for chain in range(crop_ref.shape[0]):
        first = jnp.sum(jnp.where(ids < chain, 1.0, 0.0), axis=1, keepdims=True)
        limit = crop_ref[chain].astype(F32)
        inside = jnp.where(ids == chain, 1.0, 0.0) * jnp.where(place - first < limit, 1.0, 0.0)
        kept = kept + inside
    return kept


def norm_rows(values, gain):
    centre = jnp.mean(values, axis=1, keepdims=True)
    apart = values - centre
    spread = jnp.mean(apart * apart, axis=1, keepdims=True)
    return (apart * lax.rsqrt(spread + epsilon_norm) * gain).astype(BF16)


def sorted_projection(w_proj, devices):
    total = w_proj.shape[1]
    hidden = total // 4
    own = hidden // devices
    row = lax.broadcasted_iota(jnp.int32, (total, 1), 0)
    kind = row // (2 * hidden)
    rest = row % (2 * hidden)
    device = rest // (2 * own)
    side = (rest % (2 * own)) // own
    channel = rest % own
    source = (side * 2 + kind) * hidden + device * own + channel
    return dot_nt(one_hot(source, total), w_proj).astype(BF16)


def project(flat, gain, weights, info_ref, send_ref, rows, start):
    span = flat.shape[0]
    width = send_ref.shape[2] // rows
    half = weights.shape[0] // 2
    place = start + lax.broadcasted_iota(jnp.int32, (1, span), 1)
    mask = jnp.zeros((1, span), F32)
    for row in range(rows):
        if row * width < start + span and (row + 1) * width > start:
            inside = jnp.where(place >= row * width, 1.0, 0.0)
            inside = inside * jnp.where(place < (row + 1) * width, 1.0, 0.0)
            mask = mask + inside * info_ref[8 + row : 9 + row, 0:1]
    projected = dot_nt(weights, norm_rows(flat, gain))
    operand = sigmoid(projected[:half]) * projected[half:] * mask
    shape = send_ref.shape[:2] + (span,)
    send_ref[:, :, start : start + span] = operand.astype(BF16).reshape(shape)


def spans(total):
    start = 0
    while start < total:
        span = min(256, total - start)
        yield start, span
        start += span


def compact_kernel(
    devices, widths, me_ref, crop_ref, ids_ref, pair_ref, choice_ref, info_ref, packed_ref
):
    rows, count, width = pair_ref.shape
    kept = kept_residues(ids_ref[...], crop_ref)
    total = jnp.sum(kept)
    choice = jnp.int32(0)
    for some in widths[:-1]:
        choice = choice + jnp.where(total > some, 1, 0).astype(jnp.int32)
    choice_ref[0] = choice
    square = (count, count)
    up = lax.broadcasted_iota(jnp.int32, square, 0) < lax.broadcasted_iota(jnp.int32, square, 1)
    rank = dot_nn(
        jnp.broadcast_to(kept, (8, count)).astype(BF16), jnp.where(up, 1.0, 0.0).astype(BF16)
    )[0:1]
    slots = jnp.where(kept > 0.0, rank, -1.0)
    by_row = dot_nt(
        jnp.broadcast_to(slots, (8, count)).astype(BF16), interleave(rows, devices)
    )[0:1]
    info_ref[0:1] = slots
    info_ref[1:2] = by_row
    place = lax.broadcasted_iota(jnp.int32, kept.shape, 1)
    for row in range(rows):
        own = jnp.where(place == me_ref[0] * rows + row, kept, 0.0)
        info_ref[8 + row : 9 + row] = jnp.broadcast_to(
            jnp.sum(own, axis=1, keepdims=True), kept.shape
        )
    pick = selection(slots, count)
    lanes = jnp.concatenate([pair_ref[row] for row in range(rows)], axis=1)
    packed = move(pick, lanes)
    for row in range(rows):
        packed_ref[row] = packed[:, row * width : (row + 1) * width]


def first_kernel(devices, info_ref, packed_ref, gain_ref, w_proj_ref, flat_ref, send_ref):
    rows = packed_ref.shape[0]
    width = send_ref.shape[2] // rows
    weights = sorted_projection(w_proj_ref[...], devices)
    flat = jnp.concatenate([packed_ref[row, :width] for row in range(rows)], axis=0)
    flat_ref[...] = flat
    for start, span in spans(rows * width):
        part = flat[start : start + span].astype(F32)
        project(part, gain_ref[...], weights, info_ref, send_ref, rows, start)


def gate_kernel(flat_ref, gain_ref, w_gate_ref, gate_ref):
    for start, span in spans(flat_ref.shape[0]):
        normed = norm_rows(flat_ref[start : start + span].astype(F32), gain_ref[...])
        gate_ref[start : start + span] = sigmoid(dot_nn(normed, w_gate_ref[...]))


def triangle_kernel(outgoing, rows, info_ref, came_ref, send_ref):
    devices, both, total = came_ref.shape
    own = both // 2
    width = total // rows
    by_channel = interleave(both, devices)
    pick = selection(info_ref[1:2], width)
    came = move(by_channel, came_ref[...].reshape(devices * both, total))

    def channel_rows(channel):
        span = slice(channel * devices, (channel + 1) * devices)
        return jnp.concatenate(
            [came[span, row * width : (row + 1) * width] for row in range(rows)], axis=0
        )

    products = []
    for channel in range(own):
        left = channel_rows(channel)
        right = channel_rows(own + channel)
        if outgoing:
            product = dot_nt(left, move(pick, right)).astype(BF16)
        else:
            product = dot_tn(left, right).astype(BF16)
            product = dot_tn(pick, product).astype(BF16)
        products.append(product)
    low = rows * own // 8
    to_device = interleave(devices, 8)
    for offset in range(low):
        parts = []
        for channel in range(own):
            for high in range(rows // low):
                row = high * low + offset
                parts.append(products[channel][row * devices : (row + 1) * devices])
        sent = move(to_device, jnp.concatenate(parts, axis=0))
        send_ref[:, :, offset * width : (offset + 1) * width] = sent.reshape(devices, 8, width)


def finish_parts(came_ref, flat_ref, gate_ref, gain_ref, w_out_ref):
    devices, eight, lanes = came_ref.shape
    hidden = w_out_ref.shape[0]
    high = flat_ref.shape[0] // lanes
    came = move(interleave(high, hidden), came_ref[...].reshape(devices * eight, lanes))
    gain = gain_ref[...]
    square = lax.broadcasted_iota(jnp.int32, (hidden, hidden), 0) == lax.broadcasted_iota(
        jnp.int32, (hidden, hidden), 1
    )
    gain = jnp.sum(jnp.where(square, gain, 0.0), axis=1, keepdims=True)
    for part in range(high):
        for offset, span in spans(lanes):
            block = came[part * hidden : (part + 1) * hidden, offset : offset + span].astype(F32)
            centre = jnp.mean(block, axis=0, keepdims=True)
            apart = block - centre
            spread = jnp.mean(apart * apart, axis=0, keepdims=True)
            normed = (apart * lax.rsqrt(spread + epsilon_norm) * gain).astype(BF16)
            term = dot_tn(normed, w_out_ref[...])
            start = part * lanes + offset
            here = slice(start, start + span)
            yield start, (flat_ref[here].astype(F32) + gate_ref[here] * term).astype(BF16)


def middle_kernel(
    devices,
    rows,
    info_ref,
    came_ref,
    flat_ref,
    gate_ref,
    gain_out_ref,
    w_out_ref,
    gain_in_ref,
    w_proj_ref,
    next_ref,
    send_ref,
):
    weights = sorted_projection(w_proj_ref[...], devices)
    for start, fresh in finish_parts(came_ref, flat_ref, gate_ref, gain_out_ref, w_out_ref):
        next_ref[start : start + fresh.shape[0]] = fresh
        project(fresh.astype(F32), gain_in_ref[...], weights, info_ref, send_ref, rows, start)


def last_kernel(
    info_ref, pair_ref, came_ref, flat_ref, gate_ref, gain_out_ref, w_out_ref, out_ref, next_ref
):
    rows = out_ref.shape[0]
    depth = out_ref.shape[2]
    width = flat_ref.shape[0] // rows
    for start, fresh in finish_parts(came_ref, flat_ref, gate_ref, gain_out_ref, w_out_ref):
        next_ref[start : start + fresh.shape[0]] = fresh
    pick = selection(info_ref[0:1], width)
    lanes = [next_ref[row * width : (row + 1) * width] for row in range(rows)]
    lanes.append(jnp.ones((width, depth), BF16))
    spread = dot_tn(pick, jnp.concatenate(lanes, axis=1))
    kept = spread[:, rows * depth :] > 0.5
    for row in range(rows):
        fresh = spread[:, row * depth : (row + 1) * depth]
        out_ref[row] = jnp.where(kept, fresh, pair_ref[row].astype(F32)).astype(BF16)


VMEM = pl.BlockSpec(memory_space=pltpu.VMEM)
SMEM = pl.BlockSpec(memory_space=pltpu.SMEM)


def layer_of(array, layer):
    shape = array.shape
    return pl.BlockSpec((None,) + shape[1:], lambda i: (layer,) + (0,) * (len(shape) - 1))


def whole(array):
    return pl.BlockSpec(array.shape, lambda i: (0,) * len(array.shape))


def call(body, name, outs, specs, operands, out_specs=None, scratch=()):
    return pl.pallas_call(
        body,
        out_shape=list(outs),
        grid=(1,),
        in_specs=specs,
        out_specs=out_specs or [whole(o) for o in outs],
        scratch_shapes=list(scratch),
        compiler_params=pltpu.CompilerParams(vmem_limit_bytes=48 * 1024 * 1024),
        name=name,
    )(*operands)


def kept_columns(width, pair_rep, info, packed, ln_in, w_proj, w_gate, ln_out, w_out):
    devices = lax.axis_size("dap")
    rows, _, depth = pair_rep.shape
    hidden = w_out.shape[1]
    own = hidden // devices
    send_shape = jax.ShapeDtypeStruct((devices, 2 * own, rows * width), BF16)
    back_shape = jax.ShapeDtypeStruct((devices, 8, rows * own * width // 8), BF16)
    flat_shape = jax.ShapeDtypeStruct((rows * width, depth), BF16)
    gate_shape = jax.ShapeDtypeStruct((rows * width, depth), F32)

    def exchange(sent):
        return lax.all_to_all(sent, "dap", split_axis=0, concat_axis=0, tiled=True)

    def gates(flat, layer):
        return call(
            gate_kernel,
            "gates",
            [gate_shape],
            [whole(flat), layer_of(ln_in, layer), layer_of(w_gate, layer)],
            (flat, ln_in, w_gate),
        )[0]

    def triangle(came, outgoing):
        return call(
            functools.partial(triangle_kernel, outgoing, rows),
            "outgoing" if outgoing else "incoming",
            [back_shape],
            [whole(info), whole(came)],
            (info, came),
        )[0]

    flat, sent = call(
        functools.partial(first_kernel, devices),
        "first_operands",
        [flat_shape, send_shape],
        [whole(info), whole(packed), layer_of(ln_in, 0), layer_of(w_proj, 0)],
        (info, packed, ln_in, w_proj),
    )
    gate = gates(flat, 0)
    came = exchange(triangle(exchange(sent), True))
    flat, sent = call(
        functools.partial(middle_kernel, devices, rows),
        "finish_and_operands",
        [flat_shape, send_shape],
        [
            whole(info),
            whole(came),
            whole(flat),
            whole(gate),
            layer_of(ln_out, 0),
            layer_of(w_out, 0),
            layer_of(ln_in, 1),
            layer_of(w_proj, 1),
        ],
        (info, came, flat, gate, ln_out, w_out, ln_in, w_proj),
    )
    gate = gates(flat, 1)
    came = exchange(triangle(exchange(sent), False))
    return call(
        last_kernel,
        "finish",
        [jax.ShapeDtypeStruct(pair_rep.shape, BF16)],
        [
            whole(info),
            whole(pair_rep),
            whole(came),
            whole(flat),
            whole(gate),
            layer_of(ln_out, 1),
            layer_of(w_out, 1),
        ],
        (info, pair_rep, came, flat, gate, ln_out, w_out),
        scratch=[pltpu.VMEM(flat_shape.shape, BF16)],
    )[0]


def row_shards(pair_rep, chain_ids, crop_lengths, ln_in_gain, w_proj, w_gate, ln_out_gain, w_out):
    devices = lax.axis_size("dap")
    rows, count, width = pair_rep.shape
    me = lax.axis_index("dap").reshape(1).astype(jnp.int32)
    ids = chain_ids.reshape(1, count)
    ln_in = ln_in_gain.reshape(2, 1, width)
    ln_out = ln_out_gain.reshape(2, 1, w_out.shape[1])
    widths = [some for some in range(STEP, count, STEP) if 2 * some >= count] + [count]
    info_shape = jax.ShapeDtypeStruct((16, count), F32)
    packed_shape = jax.ShapeDtypeStruct(pair_rep.shape, BF16)
    choice, info, packed = call(
        functools.partial(compact_kernel, devices, widths),
        "keep_columns",
        [jax.ShapeDtypeStruct((1,), jnp.int32), info_shape, packed_shape],
        [SMEM, SMEM, whole(ids), whole(pair_rep)],
        (me, crop_lengths, ids, pair_rep),
        out_specs=[SMEM, whole(info_shape), whole(packed_shape)],
    )
    return lax.switch(
        choice[0],
        [functools.partial(kept_columns, some) for some in widths],
        pair_rep,
        info,
        packed,
        ln_in,
        w_proj,
        w_gate,
        ln_out,
        w_out,
    )


STEP = 32


def solution(mesh):
    devices = mesh.shape["dap"]
    placed = (P("dap", "grp", None), P(), P(), P(), P(), P(), P(), P())

    def body(*arrays):
        rows, count, width = arrays[0].shape
        hidden = arrays[-1].shape[1]
        plain = (
            mesh.shape["grp"] == 1
            and rows * devices == count
            and count == 256
            and rows == 8
            and hidden == 4 * devices
        )
        return (row_shards if plain else shards)(*arrays)

    return jax.shard_map(
        body, mesh=mesh, in_specs=placed, out_specs=P("dap", "grp", None), check_vma=False
    )
```

```python
import functools

import jax
import jax.numpy as jnp
from jax import lax
from jax.experimental import pallas as pl
from jax.experimental.pallas import tpu as pltpu
from jax.sharding import PartitionSpec as P

epsilon_norm = 1e-05
F32 = jnp.float32
BF16 = jnp.bfloat16


def residue_valid(chain_ids, crop_lengths):
    count = chain_ids.shape[0]
    chains = jnp.arange(crop_lengths.shape[0], dtype=jnp.int32)
    member = (chain_ids[:, None] == chains[None, :]).astype(jnp.int32)
    counts = jnp.sum(member, axis=0)
    starts = jnp.cumsum(counts) - counts
    first = jnp.sum(member * starts[None, :], axis=1)
    limit = jnp.sum(member * crop_lengths[None, :], axis=1)
    place = jnp.arange(count, dtype=jnp.int32) - first
    return (place < limit).astype(jnp.float32)


def layer_norm(values, gain, axis):
    centre = jnp.mean(values, axis=axis, keepdims=True)
    spread = jnp.mean((values - centre) ** 2, axis=axis, keepdims=True)
    return (values - centre) * lax.rsqrt(spread + epsilon_norm) * gain


def column_rows(right_chan):
    return lax.all_to_all(right_chan, "grp", split_axis=1, concat_axis=2, tiled=True)


def update(pair_tile, pair_mask, ln_in, w_proj, w_gate, ln_out, w_out, outgoing):
    hidden = w_out.shape[0]
    normed = layer_norm(pair_tile.astype(jnp.float32), ln_in, 2).astype(jnp.bfloat16)
    projected = jnp.einsum("rqc,cf->frq", normed, w_proj, preferred_element_type=jnp.float32)
    gate_value = jax.nn.sigmoid(
        jnp.einsum("rqc,cd->rqd", normed, w_gate, preferred_element_type=jnp.float32)
    )
    left_op = (
        jax.nn.sigmoid(projected[:hidden]) * projected[hidden : 2 * hidden] * pair_mask
    ).astype(jnp.bfloat16)
    right_op = (
        jax.nn.sigmoid(projected[2 * hidden : 3 * hidden]) * projected[3 * hidden :] * pair_mask
    ).astype(jnp.bfloat16)
    left_chan, right_chan = (
        lax.all_to_all(left_op, "dap", split_axis=0, concat_axis=1, tiled=True),
        lax.all_to_all(right_op, "dap", split_axis=0, concat_axis=1, tiled=True),
    )
    if outgoing:
        right_rows = column_rows(right_chan)
        triangle = jnp.einsum(
            "hik,hjk->hij",
            lax.all_gather(left_chan, "grp", axis=2, tiled=True),
            right_rows,
            preferred_element_type=jnp.float32,
        )
    else:
        triangle = jnp.einsum(
            "hki,hkj->hij",
            lax.all_gather(left_chan, "grp", axis=2, tiled=True),
            right_chan,
            preferred_element_type=jnp.float32,
        )
    returned = lax.all_to_all(
        triangle.astype(jnp.bfloat16), "dap", split_axis=1, concat_axis=0, tiled=True
    )
    normed_product = layer_norm(returned.astype(jnp.float32), ln_out[:, None, None], 0).astype(
        jnp.bfloat16
    )
    update_term = jnp.einsum(
        "hrq,hd->rqd", normed_product, w_out, preferred_element_type=jnp.float32
    )
    return (pair_tile.astype(jnp.float32) + gate_value * update_term).astype(jnp.bfloat16)


def shards(pair_rep, chain_ids, crop_lengths, ln_in_gain, w_proj, w_gate, ln_out_gain, w_out):
    row_count = pair_rep.shape[0]
    column_count = pair_rep.shape[1]
    kept = residue_valid(chain_ids, crop_lengths)
    row_start = lax.axis_index("dap") * row_count
    column_start = lax.axis_index("grp") * column_count
    kept_rows = lax.dynamic_slice_in_dim(kept, row_start, row_count, 0)
    kept_columns = lax.dynamic_slice_in_dim(kept, column_start, column_count, 0)
    pair_mask = kept_rows[:, None] * kept_columns[None, :]
    pair_tile = pair_rep
    for layer_index, outgoing in ((0, True), (1, False)):
        pair_tile = update(
            pair_tile,
            pair_mask,
            ln_in_gain[layer_index],
            w_proj[layer_index],
            w_gate[layer_index],
            ln_out_gain[layer_index],
            w_out[layer_index],
            outgoing,
        )
    return pair_tile


def dot_nn(a, b):
    return lax.dot_general(a, b, (((1,), (0,)), ((), ())), preferred_element_type=F32)


def dot_nt(a, b):
    return lax.dot_general(a, b, (((1,), (1,)), ((), ())), preferred_element_type=F32)


def dot_tn(a, b):
    return lax.dot_general(a, b, (((0,), (0,)), ((), ())), preferred_element_type=F32)


def sigmoid(v):
    return 0.5 * jnp.tanh(0.5 * v) + 0.5


def one_hot(source, columns):
    place = lax.broadcasted_iota(jnp.int32, (source.shape[0], columns), 1)
    return jnp.where(place == source, 1.0, 0.0).astype(BF16)


def interleave(outer, inner):
    row = lax.broadcasted_iota(jnp.int32, (outer * inner, 1), 0)
    return one_hot((row % inner) * outer + row // inner, outer * inner)


def move(matrix, rows):
    return dot_nn(matrix, rows).astype(BF16)


def selection(slots, width):
    row = lax.broadcasted_iota(jnp.int32, (width, slots.shape[1]), 0).astype(F32)
    return jnp.where(row == slots, 1.0, 0.0).astype(BF16)


def kept_residues(ids, crop_ref):
    place = lax.broadcasted_iota(jnp.int32, ids.shape, 1).astype(F32)
    kept = jnp.zeros(ids.shape, F32)
    for chain in range(crop_ref.shape[0]):
        first = jnp.sum(jnp.where(ids < chain, 1.0, 0.0), axis=1, keepdims=True)
        limit = crop_ref[chain].astype(F32)
        inside = jnp.where(ids == chain, 1.0, 0.0) * jnp.where(place - first < limit, 1.0, 0.0)
        kept = kept + inside
    return kept


def norm_rows(values, gain):
    centre = jnp.mean(values, axis=1, keepdims=True)
    apart = values - centre
    spread = jnp.mean(apart * apart, axis=1, keepdims=True)
    return (apart * lax.rsqrt(spread + epsilon_norm) * gain).astype(BF16)


def sort_projection(w_proj_ref, devices, sorted_ref):
    total = w_proj_ref.shape[1]
    hidden = total // 4
    own = hidden // devices

    def block(index, carry):
        first = pl.multiple_of(index * 128, 128)
        row = first + lax.broadcasted_iota(jnp.int32, (128, 1), 0)
        kind = row // (2 * hidden)
        rest = row % (2 * hidden)
        device = rest // (2 * own)
        side = (rest % (2 * own)) // own
        channel = rest % own
        source = (side * 2 + kind) * hidden + device * own + channel
        rows = dot_nt(one_hot(source, total), w_proj_ref[...])
        sorted_ref[pl.ds(first, 128)] = rows.astype(BF16)
        return carry

    lax.fori_loop(0, total // 128, block, 0)


def project(flat, gain, weights, info_ref, send_ref, rows, start):
    span = flat.shape[0]
    width = send_ref.shape[2] // rows
    half = weights.shape[0] // 2
    place = start + lax.broadcasted_iota(jnp.int32, (1, span), 1)
    mask = jnp.zeros((1, span), F32)
    for row in range(rows):
        inside = jnp.where(place >= row * width, 1.0, 0.0)
        inside = inside * jnp.where(place < (row + 1) * width, 1.0, 0.0)
        mask = mask + inside * info_ref[8 + row : 9 + row, 0:1]
    projected = dot_nt(weights, norm_rows(flat, gain))
    operand = sigmoid(projected[:half]) * projected[half:] * mask
    shape = send_ref.shape[:2] + (span,)
    send_ref[:, :, pl.ds(start, span)] = operand.astype(BF16).reshape(shape)


def each_span(total, body):
    span = 256 if total % 256 == 0 else 128

    def step(index, carry):
        body(pl.multiple_of(index * span, span), span)
        return carry

    lax.fori_loop(0, total // span, step, 0)


LN_IN, LN_OUT, ROWS = 2, 4, 8


def gain_of(info_ref, row, width):
    return info_ref[row : row + 1, :width]


def compact_kernel(
    devices,
    widths,
    me_ref,
    crop_ref,
    ids_ref,
    ln_in_ref,
    ln_out_ref,
    pair_hbm,
    choice_ref,
    info_ref,
    packed_ref,
    pair_ref,
    arrived,
):
    copy = pltpu.make_async_copy(pair_hbm, pair_ref, arrived)
    copy.start()
    rows, count, width = pair_ref.shape
    kept = kept_residues(ids_ref[...], crop_ref)
    total = jnp.sum(kept)
    choice = jnp.int32(0)
    for some in widths[:-1]:
        choice = choice + jnp.where(total > some, 1, 0).astype(jnp.int32)
    choice_ref[0] = choice
    square = (count, count)
    up = lax.broadcasted_iota(jnp.int32, square, 0) < lax.broadcasted_iota(jnp.int32, square, 1)
    rank = dot_nn(
        jnp.broadcast_to(kept, (8, count)).astype(BF16), jnp.where(up, 1.0, 0.0).astype(BF16)
    )[0:1]
    slots = jnp.where(kept > 0.0, rank, -1.0)
    by_row = dot_nt(
        jnp.broadcast_to(slots, (8, count)).astype(BF16), interleave(rows, devices)
    )[0:1]
    info_ref[...] = jnp.zeros(info_ref.shape, F32)
    info_ref[0:1] = slots
    info_ref[1:2] = by_row
    info_ref[LN_IN : LN_IN + 2, :width] = ln_in_ref[...]
    info_ref[LN_OUT : LN_OUT + 2, : ln_out_ref.shape[1]] = ln_out_ref[...]
    place = lax.broadcasted_iota(jnp.int32, kept.shape, 1)
    for row in range(rows):
        own = jnp.where(place == me_ref[0] * rows + row, kept, 0.0)
        info_ref[ROWS + row : ROWS + row + 1] = jnp.broadcast_to(
            jnp.sum(own, axis=1, keepdims=True), kept.shape
        )
    pick = selection(slots, count)
    copy.wait()
    lanes = jnp.concatenate([pair_ref[row] for row in range(rows)], axis=1)
    packed = move(pick, lanes)
    for row in range(rows):
        packed_ref[row] = packed[:, row * width : (row + 1) * width]


def first_kernel(devices, info_ref, packed_ref, w_proj_ref, flat_ref, send_ref, weights_ref):
    rows, _, depth = packed_ref.shape
    width = send_ref.shape[2] // rows
    gain = gain_of(info_ref, LN_IN, depth)
    sort_projection(w_proj_ref, devices, weights_ref)
    for row in range(rows):
        flat_ref[row * width : (row + 1) * width] = packed_ref[row, :width]

    def body(start, span):
        part = flat_ref[pl.ds(start, span)].astype(F32)
        project(part, gain, weights_ref[...], info_ref, send_ref, rows, start)

    each_span(rows * width, body)


def gate_kernel(layer, info_ref, flat_ref, w_gate_ref, gate_ref):
    gain = gain_of(info_ref, LN_IN + layer, flat_ref.shape[1])

    def body(start, span):
        normed = norm_rows(flat_ref[pl.ds(start, span)].astype(F32), gain)
        gate_ref[pl.ds(start, span)] = sigmoid(dot_nn(normed, w_gate_ref[...]))

    each_span(flat_ref.shape[0], body)


def triangle_kernel(outgoing, rows, info_ref, came_ref, send_ref, sorted_ref, product_ref):
    devices, both, total = came_ref.shape
    own = both // 2
    width = total // rows
    by_channel = interleave(both, devices)
    pick = selection(info_ref[1:2], width)

    def sort(start, span):
        here = pl.ds(start, span)
        sorted_ref[:, here] = move(by_channel, came_ref[:, :, here].reshape(devices * both, span))

    each_span(total, sort)

    def channel_rows(channel):
        came = sorted_ref[pl.ds(pl.multiple_of(channel * devices, devices), devices)]
        return jnp.concatenate(
            [came[:, row * width : (row + 1) * width] for row in range(rows)], axis=0
        )

    def multiply(channel, carry):
        left = channel_rows(channel)
        right = channel_rows(own + channel)
        if outgoing:
            product = dot_nt(left, move(pick, right)).astype(BF16)
        else:
            product = dot_tn(left, right).astype(BF16)
            product = dot_tn(pick, product).astype(BF16)
        product_ref[channel] = product
        return carry

    lax.fori_loop(0, own, multiply, 0)
    low = rows * own // 8
    to_device = interleave(devices, 8)
    for offset in range(low):
        parts = []
        for channel in range(own):
            for high in range(rows // low):
                row = high * low + offset
                parts.append(product_ref[channel, row * devices : (row + 1) * devices])
        sent = move(to_device, jnp.concatenate(parts, axis=0))
        send_ref[:, :, offset * width : (offset + 1) * width] = sent.reshape(devices, 8, width)


def finish_parts(layer, info_ref, came_ref, flat_ref, gate_ref, w_out_ref, use):
    devices, eight, lanes = came_ref.shape
    hidden = w_out_ref.shape[0]
    high = flat_ref.shape[0] // lanes
    by_part = interleave(high, hidden)
    square = lax.broadcasted_iota(jnp.int32, (hidden, hidden), 0) == lax.broadcasted_iota(
        jnp.int32, (hidden, hidden), 1
    )
    gain = gain_of(info_ref, LN_OUT + layer, hidden)
    gain = jnp.sum(jnp.where(square, gain, 0.0), axis=1, keepdims=True)

    def body(offset, span):
        came = dot_nn(by_part, came_ref[:, :, pl.ds(offset, span)].reshape(devices * eight, span))
        for part in range(high):
            block = came[part * hidden : (part + 1) * hidden]
            centre = jnp.mean(block, axis=0, keepdims=True)
            apart = block - centre
            spread = jnp.mean(apart * apart, axis=0, keepdims=True)
            normed = (apart * lax.rsqrt(spread + epsilon_norm) * gain).astype(BF16)
            term = dot_tn(normed, w_out_ref[...])
            start = pl.multiple_of(part * lanes + offset, 128)
            here = pl.ds(start, span)
            use(start, (flat_ref[here].astype(F32) + gate_ref[here] * term).astype(BF16))

    each_span(lanes, body)


def middle_kernel(
    devices,
    rows,
    info_ref,
    came_ref,
    flat_ref,
    gate_ref,
    w_out_ref,
    w_proj_ref,
    next_ref,
    send_ref,
    weights_ref,
):
    sort_projection(w_proj_ref, devices, weights_ref)
    gain = gain_of(info_ref, LN_IN + 1, flat_ref.shape[1])

    def use(start, fresh):
        next_ref[pl.ds(start, fresh.shape[0])] = fresh
        project(fresh.astype(F32), gain, weights_ref[...], info_ref, send_ref, rows, start)

    finish_parts(0, info_ref, came_ref, flat_ref, gate_ref, w_out_ref, use)


def last_kernel(info_ref, pair_ref, came_ref, flat_ref, gate_ref, w_out_ref, out_ref, next_ref):
    rows, _, depth = out_ref.shape
    width = flat_ref.shape[0] // rows

    def use(start, fresh):
        next_ref[pl.ds(start, fresh.shape[0])] = fresh

    finish_parts(1, info_ref, came_ref, flat_ref, gate_ref, w_out_ref, use)
    pick = selection(info_ref[0:1], width)
    kept = dot_tn(pick, jnp.ones((width, depth), BF16)) > 0.5

    def spread(row, carry):
        fresh = next_ref[pl.ds(pl.multiple_of(row * width, 16), width)]
        out_ref[row] = jnp.where(
            kept, dot_tn(pick, fresh), pair_ref[row].astype(F32)
        ).astype(BF16)
        return carry

    lax.fori_loop(0, rows, spread, 0)


SMEM = pl.BlockSpec(memory_space=pltpu.SMEM)


def layer_of(array, layer):
    shape = array.shape
    return pl.BlockSpec((None,) + shape[1:], lambda i: (layer,) + (0,) * (len(shape) - 1))


def whole(array):
    return pl.BlockSpec(array.shape, lambda i: (0,) * len(array.shape))


def call(body, name, outs, specs, operands, out_specs=None, scratch=()):
    return pl.pallas_call(
        body,
        out_shape=list(outs),
        grid=(1,),
        in_specs=specs,
        out_specs=out_specs or [whole(o) for o in outs],
        scratch_shapes=list(scratch),
        compiler_params=pltpu.CompilerParams(vmem_limit_bytes=48 * 1024 * 1024),
        name=name,
    )(*operands)


def kept_columns(width, pair_rep, info, packed, w_proj, w_gate, w_out):
    devices = lax.axis_size("dap")
    rows, _, depth = pair_rep.shape
    hidden = w_out.shape[1]
    own = hidden // devices
    send_shape = jax.ShapeDtypeStruct((devices, 2 * own, rows * width), BF16)
    back_shape = jax.ShapeDtypeStruct((devices, 8, rows * own * width // 8), BF16)
    flat_shape = jax.ShapeDtypeStruct((rows * width, depth), BF16)
    gate_shape = jax.ShapeDtypeStruct((rows * width, depth), F32)
    weights_scratch = pltpu.VMEM((4 * hidden, depth), BF16)

    def exchange(sent):
        return lax.all_to_all(sent, "dap", split_axis=0, concat_axis=0, tiled=True)

    def gates(flat, layer):
        return call(
            functools.partial(gate_kernel, layer),
            "gates",
            [gate_shape],
            [whole(info), whole(flat), layer_of(w_gate, layer)],
            (info, flat, w_gate),
        )[0]

    def triangle(came, outgoing):
        return call(
            functools.partial(triangle_kernel, outgoing, rows),
            "outgoing" if outgoing else "incoming",
            [back_shape],
            [whole(info), whole(came)],
            (info, came),
            scratch=[
                pltpu.VMEM((devices * 2 * own, rows * width), BF16),
                pltpu.VMEM((own, rows * devices, width), BF16),
            ],
        )[0]

    flat, sent = call(
        functools.partial(first_kernel, devices),
        "first_operands",
        [flat_shape, send_shape],
        [whole(info), whole(packed), layer_of(w_proj, 0)],
        (info, packed, w_proj),
        scratch=[weights_scratch],
    )
    gate = gates(flat, 0)
    came = exchange(triangle(exchange(sent), True))
    flat, sent = call(
        functools.partial(middle_kernel, devices, rows),
        "finish_and_operands",
        [flat_shape, send_shape],
        [
            whole(info),
            whole(came),
            whole(flat),
            whole(gate),
            layer_of(w_out, 0),
            layer_of(w_proj, 1),
        ],
        (info, came, flat, gate, w_out, w_proj),
        scratch=[weights_scratch],
    )
    gate = gates(flat, 1)
    came = exchange(triangle(exchange(sent), False))
    return call(
        last_kernel,
        "finish",
        [jax.ShapeDtypeStruct(pair_rep.shape, BF16)],
        [
            whole(info),
            whole(pair_rep),
            whole(came),
            whole(flat),
            whole(gate),
            layer_of(w_out, 1),
        ],
        (info, pair_rep, came, flat, gate, w_out),
        scratch=[pltpu.VMEM(flat_shape.shape, BF16)],
    )[0]


def row_shards(pair_rep, chain_ids, crop_lengths, ln_in_gain, w_proj, w_gate, ln_out_gain, w_out):
    devices = lax.axis_size("dap")
    count = pair_rep.shape[1]
    me = lax.axis_index("dap").reshape(1).astype(jnp.int32)
    ids = chain_ids.reshape(1, count)
    widths = [some for some in range(STEP, count, STEP) if 2 * some >= count] + [count]
    info_shape = jax.ShapeDtypeStruct((16, count), F32)
    packed_shape = jax.ShapeDtypeStruct(pair_rep.shape, BF16)
    choice, info, packed = call(
        functools.partial(compact_kernel, devices, widths),
        "keep_columns",
        [jax.ShapeDtypeStruct((1,), jnp.int32), info_shape, packed_shape],
        [
            SMEM,
            SMEM,
            whole(ids),
            whole(ln_in_gain),
            whole(ln_out_gain),
            pl.BlockSpec(memory_space=pltpu.HBM),
        ],
        (me, crop_lengths, ids, ln_in_gain, ln_out_gain, pair_rep),
        out_specs=[SMEM, whole(info_shape), whole(packed_shape)],
        scratch=[pltpu.VMEM(pair_rep.shape, BF16), pltpu.SemaphoreType.DMA],
    )
    return lax.switch(
        choice[0],
        [functools.partial(kept_columns, some) for some in widths],
        pair_rep,
        info,
        packed,
        w_proj,
        w_gate,
        w_out,
    )


STEP = 32


def solution(mesh):
    devices = mesh.shape["dap"]
    placed = (P("dap", "grp", None), P(), P(), P(), P(), P(), P(), P())

    def body(*arrays):
        rows, count, width = arrays[0].shape
        hidden = arrays[-1].shape[1]
        plain = (
            mesh.shape["grp"] == 1
            and rows * devices == count
            and count == 256
            and rows == 8
            and hidden == 4 * devices
        )
        return (row_shards if plain else shards)(*arrays)

    return jax.shard_map(
        body, mesh=mesh, in_specs=placed, out_specs=P("dap", "grp", None), check_vma=False
    )
```

```python
import functools

import jax
import jax.numpy as jnp
from jax import lax
from jax.experimental import pallas as pl
from jax.experimental.pallas import tpu as pltpu
from jax.sharding import PartitionSpec as P

epsilon_norm = 1e-05
F32 = jnp.float32
BF16 = jnp.bfloat16


def residue_valid(chain_ids, crop_lengths):
    count = chain_ids.shape[0]
    chains = jnp.arange(crop_lengths.shape[0], dtype=jnp.int32)
    member = (chain_ids[:, None] == chains[None, :]).astype(jnp.int32)
    counts = jnp.sum(member, axis=0)
    starts = jnp.cumsum(counts) - counts
    first = jnp.sum(member * starts[None, :], axis=1)
    limit = jnp.sum(member * crop_lengths[None, :], axis=1)
    place = jnp.arange(count, dtype=jnp.int32) - first
    return (place < limit).astype(jnp.float32)


def layer_norm(values, gain, axis):
    centre = jnp.mean(values, axis=axis, keepdims=True)
    spread = jnp.mean((values - centre) ** 2, axis=axis, keepdims=True)
    return (values - centre) * lax.rsqrt(spread + epsilon_norm) * gain


def column_rows(right_chan):
    return lax.all_to_all(right_chan, "grp", split_axis=1, concat_axis=2, tiled=True)


def update(pair_tile, pair_mask, ln_in, w_proj, w_gate, ln_out, w_out, outgoing):
    hidden = w_out.shape[0]
    normed = layer_norm(pair_tile.astype(jnp.float32), ln_in, 2).astype(jnp.bfloat16)
    projected = jnp.einsum("rqc,cf->frq", normed, w_proj, preferred_element_type=jnp.float32)
    gate_value = jax.nn.sigmoid(
        jnp.einsum("rqc,cd->rqd", normed, w_gate, preferred_element_type=jnp.float32)
    )
    left_op = (
        jax.nn.sigmoid(projected[:hidden]) * projected[hidden : 2 * hidden] * pair_mask
    ).astype(jnp.bfloat16)
    right_op = (
        jax.nn.sigmoid(projected[2 * hidden : 3 * hidden]) * projected[3 * hidden :] * pair_mask
    ).astype(jnp.bfloat16)
    left_chan, right_chan = (
        lax.all_to_all(left_op, "dap", split_axis=0, concat_axis=1, tiled=True),
        lax.all_to_all(right_op, "dap", split_axis=0, concat_axis=1, tiled=True),
    )
    if outgoing:
        right_rows = column_rows(right_chan)
        triangle = jnp.einsum(
            "hik,hjk->hij",
            lax.all_gather(left_chan, "grp", axis=2, tiled=True),
            right_rows,
            preferred_element_type=jnp.float32,
        )
    else:
        triangle = jnp.einsum(
            "hki,hkj->hij",
            lax.all_gather(left_chan, "grp", axis=2, tiled=True),
            right_chan,
            preferred_element_type=jnp.float32,
        )
    returned = lax.all_to_all(
        triangle.astype(jnp.bfloat16), "dap", split_axis=1, concat_axis=0, tiled=True
    )
    normed_product = layer_norm(returned.astype(jnp.float32), ln_out[:, None, None], 0).astype(
        jnp.bfloat16
    )
    update_term = jnp.einsum(
        "hrq,hd->rqd", normed_product, w_out, preferred_element_type=jnp.float32
    )
    return (pair_tile.astype(jnp.float32) + gate_value * update_term).astype(jnp.bfloat16)


def shards(pair_rep, chain_ids, crop_lengths, ln_in_gain, w_proj, w_gate, ln_out_gain, w_out):
    row_count = pair_rep.shape[0]
    column_count = pair_rep.shape[1]
    kept = residue_valid(chain_ids, crop_lengths)
    row_start = lax.axis_index("dap") * row_count
    column_start = lax.axis_index("grp") * column_count
    kept_rows = lax.dynamic_slice_in_dim(kept, row_start, row_count, 0)
    kept_columns = lax.dynamic_slice_in_dim(kept, column_start, column_count, 0)
    pair_mask = kept_rows[:, None] * kept_columns[None, :]
    pair_tile = pair_rep
    for layer_index, outgoing in ((0, True), (1, False)):
        pair_tile = update(
            pair_tile,
            pair_mask,
            ln_in_gain[layer_index],
            w_proj[layer_index],
            w_gate[layer_index],
            ln_out_gain[layer_index],
            w_out[layer_index],
            outgoing,
        )
    return pair_tile


def dot_nn(a, b):
    return lax.dot_general(a, b, (((1,), (0,)), ((), ())), preferred_element_type=F32)


def dot_nt(a, b):
    return lax.dot_general(a, b, (((1,), (1,)), ((), ())), preferred_element_type=F32)


def dot_tn(a, b):
    return lax.dot_general(a, b, (((0,), (0,)), ((), ())), preferred_element_type=F32)


def sigmoid(v):
    return 0.5 * jnp.tanh(0.5 * v) + 0.5


def one_hot(source, columns):
    place = lax.broadcasted_iota(jnp.int32, (source.shape[0], columns), 1)
    return jnp.where(place == source, 1.0, 0.0).astype(BF16)


def interleave(outer, inner):
    row = lax.broadcasted_iota(jnp.int32, (outer * inner, 1), 0)
    return one_hot((row % inner) * outer + row // inner, outer * inner)


def move(matrix, rows):
    return dot_nn(matrix, rows).astype(BF16)


def selection(slots, width):
    row = lax.broadcasted_iota(jnp.int32, (width, slots.shape[1]), 0).astype(F32)
    return jnp.where(row == slots, 1.0, 0.0).astype(BF16)


def kept_residues(ids, limits):
    place = lax.broadcasted_iota(jnp.int32, ids.shape, 1).astype(F32)
    kept = jnp.zeros(ids.shape, F32)
    for chain in range(limits.shape[1]):
        first = jnp.sum(jnp.where(ids < chain, 1.0, 0.0), axis=1, keepdims=True)
        limit = limits[:, chain : chain + 1].astype(F32)
        inside = jnp.where(ids == chain, 1.0, 0.0) * jnp.where(place - first < limit, 1.0, 0.0)
        kept = kept + inside
    return kept


def norm_rows(values, gain):
    centre = jnp.mean(values, axis=1, keepdims=True)
    apart = values - centre
    spread = jnp.mean(apart * apart, axis=1, keepdims=True)
    return (apart * lax.rsqrt(spread + epsilon_norm) * gain).astype(BF16)


def sort_projection(w_proj_ref, devices, sorted_ref):
    total = w_proj_ref.shape[1]
    hidden = total // 4
    own = hidden // devices
    for first in range(0, total, 128):
        row = first + lax.broadcasted_iota(jnp.int32, (128, 1), 0)
        kind = row // (2 * hidden)
        rest = row % (2 * hidden)
        device = rest // (2 * own)
        side = (rest % (2 * own)) // own
        channel = rest % own
        source = (side * 2 + kind) * hidden + device * own + channel
        rows = dot_nt(one_hot(source, total), w_proj_ref[...])
        sorted_ref[first : first + 128] = rows.astype(BF16)


def project(flat, gain, weights, info_ref, send_ref, rows, width, start):
    span = flat.shape[0]
    half = weights.shape[0] // 2
    place = start + lax.broadcasted_iota(jnp.int32, (1, span), 1)
    mask = jnp.zeros((1, span), F32)
    for row in range(rows):
        inside = jnp.where(place >= row * width, 1.0, 0.0)
        inside = inside * jnp.where(place < (row + 1) * width, 1.0, 0.0)
        mask = mask + inside * info_ref[ROWS + row : ROWS + row + 1, 0:1]
    projected = dot_nt(weights, norm_rows(flat, gain))
    operand = sigmoid(projected[:half]) * projected[half:] * mask
    shape = send_ref.shape[:2] + (span,)
    send_ref[:, :, start : start + span] = operand.astype(BF16).reshape(shape)


def spans(total):
    start = 0
    while start < total:
        span = min(256, total - start)
        yield start, span
        start += span


LN_IN, LN_OUT, ROWS = 2, 4, 8


def gain_of(info_ref, row, width):
    return info_ref[row : row + 1, :width]


def first_kernel(
    devices,
    widths,
    me_ref,
    ids_hbm,
    crop_hbm,
    ln_in_hbm,
    ln_out_hbm,
    w_proj_hbm,
    pair_hbm,
    choice_ref,
    info_ref,
    flat_ref,
    send_ref,
    ids_ref,
    crop_ref,
    ln_in_ref,
    ln_out_ref,
    w_proj_ref,
    pair_ref,
    weights_ref,
    arrived,
):
    moves = (
        (ids_hbm, ids_ref),
        (crop_hbm, crop_ref),
        (ln_in_hbm, ln_in_ref),
        (ln_out_hbm, ln_out_ref),
        (w_proj_hbm.at[0], w_proj_ref),
        (pair_hbm, pair_ref),
    )
    copies = [
        pltpu.make_async_copy(source, target, arrived.at[index])
        for index, (source, target) in enumerate(moves)
    ]
    for copy in copies:
        copy.start()
    rows, count, depth = pair_ref.shape
    flat_ref[...] = jnp.zeros(flat_ref.shape, BF16)
    info_ref[...] = jnp.zeros(info_ref.shape, F32)
    for copy in copies[:4]:
        copy.wait()
    kept = kept_residues(ids_ref[...], crop_ref[...])
    total = jnp.sum(kept)
    choice = jnp.int32(0)
    for some in widths[:-1]:
        choice = choice + jnp.where(total > some, 1, 0).astype(jnp.int32)
    choice_ref[0] = choice
    width = widths[0] + STEP * choice
    square = (count, count)
    up = lax.broadcasted_iota(jnp.int32, square, 0) < lax.broadcasted_iota(jnp.int32, square, 1)
    rank = dot_nn(
        jnp.broadcast_to(kept, (8, count)).astype(BF16), jnp.where(up, 1.0, 0.0).astype(BF16)
    )[0:1]
    slots = jnp.where(kept > 0.0, rank, -1.0)
    by_row = dot_nt(
        jnp.broadcast_to(slots, (8, count)).astype(BF16), interleave(rows, devices)
    )[0:1]
    info_ref[0:1] = slots
    info_ref[1:2] = by_row
    info_ref[LN_IN : LN_IN + 2, :depth] = ln_in_ref[...]
    info_ref[LN_OUT : LN_OUT + 2, : ln_out_ref.shape[1]] = ln_out_ref[...]
    place = lax.broadcasted_iota(jnp.int32, kept.shape, 1)
    for row in range(rows):
        own = jnp.where(place == me_ref[0] * rows + row, kept, 0.0)
        info_ref[ROWS + row : ROWS + row + 1] = jnp.broadcast_to(
            jnp.sum(own, axis=1, keepdims=True), kept.shape
        )
    pick = selection(slots, count)
    copies[4].wait()
    sort_projection(w_proj_ref, devices, weights_ref)
    copies[5].wait()
    lanes = jnp.concatenate([pair_ref[row] for row in range(rows)], axis=1)
    packed = move(pick, lanes)
    for row in range(rows):
        start = pl.multiple_of(row * width, 16)
        flat_ref[pl.ds(start, count)] = packed[:, row * depth : (row + 1) * depth]
    gain = gain_of(info_ref, LN_IN, depth)
    for start, span in spans(rows * count):
        part = flat_ref[start : start + span].astype(F32)
        project(part, gain, weights_ref[...], info_ref, send_ref, rows, width, start)


def gate_kernel(layer, info_ref, flat_ref, w_gate_ref, gate_ref):
    gain = gain_of(info_ref, LN_IN + layer, flat_ref.shape[1])
    total = flat_ref.shape[0]
    span = 256 if total % 256 == 0 else 128

    def step(index, carry):
        here = pl.ds(pl.multiple_of(index * span, span), span)
        normed = norm_rows(flat_ref[here].astype(F32), gain)
        gate_ref[here] = sigmoid(dot_nn(normed, w_gate_ref[...]))
        return carry

    lax.fori_loop(0, total // span, step, 0)


def gate_and_sort_kernel(
    layer, devices, info_ref, flat_ref, w_gate_ref, w_proj_ref, gate_ref, sorted_ref
):
    gate_kernel(layer, info_ref, flat_ref, w_gate_ref, gate_ref)
    sort_projection(w_proj_ref, devices, sorted_ref)


def triangle_kernel(outgoing, rows, info_ref, came_ref, send_ref):
    devices, both, total = came_ref.shape
    own = both // 2
    width = total // rows
    by_channel = interleave(both, devices)
    pick = selection(info_ref[1:2], width)
    if not outgoing:
        pick = dot_nt(interleave(1, rows * devices), pick).astype(BF16)
    came = move(by_channel, came_ref[...].reshape(devices * both, total))

    def channel_rows(channel):
        span = slice(channel * devices, (channel + 1) * devices)
        return jnp.concatenate(
            [came[span, row * width : (row + 1) * width] for row in range(rows)], axis=0
        )

    products = []
    for channel in range(own):
        left = channel_rows(channel)
        right = channel_rows(own + channel)
        if outgoing:
            product = dot_nt(left, move(pick, right)).astype(BF16)
        else:
            product = move(pick, dot_tn(left, right).astype(BF16))
        products.append(product)
    low = rows * own // 8
    to_device = interleave(devices, 8)
    for offset in range(low):
        parts = []
        for channel in range(own):
            for high in range(rows // low):
                row = high * low + offset
                parts.append(products[channel][row * devices : (row + 1) * devices])
        sent = move(to_device, jnp.concatenate(parts, axis=0))
        send_ref[:, :, offset * width : (offset + 1) * width] = sent.reshape(devices, 8, width)


def finish_parts(layer, info_ref, came_ref, flat_ref, gate_ref, w_out_ref, use):
    devices, eight, lanes = came_ref.shape
    hidden = w_out_ref.shape[0]
    high = flat_ref.shape[0] // lanes
    by_part = interleave(high, hidden)
    square = lax.broadcasted_iota(jnp.int32, (hidden, hidden), 0) == lax.broadcasted_iota(
        jnp.int32, (hidden, hidden), 1
    )
    gain = gain_of(info_ref, LN_OUT + layer, hidden)
    gain = jnp.sum(jnp.where(square, gain, 0.0), axis=1, keepdims=True)

    for offset, span in spans(lanes):
        came = dot_nn(
            by_part, came_ref[:, :, offset : offset + span].reshape(devices * eight, span)
        )
        for part in range(high):
            block = came[part * hidden : (part + 1) * hidden]
            centre = jnp.mean(block, axis=0, keepdims=True)
            apart = block - centre
            spread = jnp.mean(apart * apart, axis=0, keepdims=True)
            normed = (apart * lax.rsqrt(spread + epsilon_norm) * gain).astype(BF16)
            term = dot_tn(normed, w_out_ref[...])
            start = part * lanes + offset
            here = slice(start, start + span)
            use(start, (flat_ref[here].astype(F32) + gate_ref[here] * term).astype(BF16))


def middle_kernel(
    rows, info_ref, came_ref, flat_ref, gate_ref, w_out_ref, weights_ref, next_ref, send_ref
):
    gain = gain_of(info_ref, LN_IN + 1, flat_ref.shape[1])
    width = flat_ref.shape[0] // rows

    def use(start, fresh):
        next_ref[start : start + fresh.shape[0]] = fresh
        part = fresh.astype(F32)
        project(part, gain, weights_ref[...], info_ref, send_ref, rows, width, start)

    finish_parts(0, info_ref, came_ref, flat_ref, gate_ref, w_out_ref, use)


def last_kernel(info_ref, pair_ref, came_ref, flat_ref, gate_ref, w_out_ref, out_ref, next_ref):
    rows, count, depth = out_ref.shape
    width = flat_ref.shape[0] // rows

    def use(start, fresh):
        next_ref[start : start + fresh.shape[0]] = fresh

    finish_parts(1, info_ref, came_ref, flat_ref, gate_ref, w_out_ref, use)
    pick = selection(info_ref[0:1], width)
    pick = dot_nt(interleave(1, count), pick).astype(BF16)
    lanes = [next_ref[row * width : (row + 1) * width] for row in range(rows)]
    lanes.append(jnp.ones((width, depth), BF16))
    spread = dot_nn(pick, jnp.concatenate(lanes, axis=1))
    kept = spread[:, rows * depth :] > 0.5
    for row in range(rows):
        fresh = spread[:, row * depth : (row + 1) * depth]
        out_ref[row] = jnp.where(kept, fresh, pair_ref[row].astype(F32)).astype(BF16)


SMEM = pl.BlockSpec(memory_space=pltpu.SMEM)
HBM = pl.BlockSpec(memory_space=pltpu.HBM)


def layer_of(array, layer):
    shape = array.shape
    return pl.BlockSpec((None,) + shape[1:], lambda i: (layer,) + (0,) * (len(shape) - 1))


def whole(array):
    return pl.BlockSpec(array.shape, lambda i: (0,) * len(array.shape))


def call(body, name, outs, specs, operands, out_specs=None, scratch=()):
    return pl.pallas_call(
        body,
        out_shape=list(outs),
        grid=(1,),
        in_specs=specs,
        out_specs=out_specs or [whole(o) for o in outs],
        scratch_shapes=list(scratch),
        compiler_params=pltpu.CompilerParams(vmem_limit_bytes=48 * 1024 * 1024),
        name=name,
    )(*operands)


def kept_columns(width, pair_rep, info, flat, sent, w_proj, w_gate, w_out):
    devices = lax.axis_size("dap")
    rows, _, depth = pair_rep.shape
    hidden = w_out.shape[1]
    own = hidden // devices
    send_shape = jax.ShapeDtypeStruct((devices, 2 * own, rows * width), BF16)
    back_shape = jax.ShapeDtypeStruct((devices, 8, rows * own * width // 8), BF16)
    flat_shape = jax.ShapeDtypeStruct((rows * width, depth), BF16)
    gate_shape = jax.ShapeDtypeStruct((rows * width, depth), F32)
    sorted_shape = jax.ShapeDtypeStruct((4 * hidden, depth), BF16)

    def exchange(sent):
        return lax.all_to_all(sent, "dap", split_axis=0, concat_axis=0, tiled=True)

    def triangle(came, outgoing):
        return call(
            functools.partial(triangle_kernel, outgoing, rows),
            "outgoing" if outgoing else "incoming",
            [back_shape],
            [whole(info), whole(came)],
            (info, came),
        )[0]

    sent = sent[:, :, : rows * width]
    gate, weights = call(
        functools.partial(gate_and_sort_kernel, 0, devices),
        "gates_and_weights",
        [gate_shape, sorted_shape],
        [whole(info), whole(flat_shape), layer_of(w_gate, 0), layer_of(w_proj, 1)],
        (info, flat, w_gate, w_proj),
    )
    came = exchange(triangle(exchange(sent), True))
    flat, sent = call(
        functools.partial(middle_kernel, rows),
        "finish_and_operands",
        [flat_shape, send_shape],
        [
            whole(info),
            whole(came),
            whole(flat_shape),
            whole(gate),
            layer_of(w_out, 0),
            whole(weights),
        ],
        (info, came, flat, gate, w_out, weights),
    )
    gate = call(
        functools.partial(gate_kernel, 1),
        "gates",
        [gate_shape],
        [whole(info), whole(flat), layer_of(w_gate, 1)],
        (info, flat, w_gate),
    )[0]
    came = exchange(triangle(exchange(sent), False))
    return call(
        last_kernel,
        "finish",
        [jax.ShapeDtypeStruct(pair_rep.shape, BF16)],
        [
            whole(info),
            whole(pair_rep),
            whole(came),
            whole(flat),
            whole(gate),
            layer_of(w_out, 1),
        ],
        (info, pair_rep, came, flat, gate, w_out),
        scratch=[pltpu.VMEM(flat_shape.shape, BF16)],
    )[0]


def row_shards(pair_rep, chain_ids, crop_lengths, ln_in_gain, w_proj, w_gate, ln_out_gain, w_out):
    devices = lax.axis_size("dap")
    rows, count, depth = pair_rep.shape
    me = lax.axis_index("dap").reshape(1).astype(jnp.int32)
    ids = chain_ids.reshape(1, count)
    crops = crop_lengths.reshape(1, -1)
    widths = [some for some in range(STEP, count + 1, STEP) if 2 * some >= count]
    info_shape = jax.ShapeDtypeStruct((16, count), F32)
    flat_shape = jax.ShapeDtypeStruct((rows * count, depth), BF16)
    send_shape = jax.ShapeDtypeStruct((devices, w_proj.shape[2] // devices // 2, rows * count), BF16)
    choice, info, flat, sent = call(
        functools.partial(first_kernel, devices, widths),
        "first_operands",
        [jax.ShapeDtypeStruct((1,), jnp.int32), info_shape, flat_shape, send_shape],
        [SMEM, HBM, HBM, HBM, HBM, HBM, HBM],
        (me, ids, crops, ln_in_gain, ln_out_gain, w_proj, pair_rep),
        out_specs=[SMEM, whole(info_shape), whole(flat_shape), whole(send_shape)],
        scratch=[
            pltpu.VMEM(ids.shape, jnp.int32),
            pltpu.VMEM(crops.shape, jnp.int32),
            pltpu.VMEM(ln_in_gain.shape, F32),
            pltpu.VMEM(ln_out_gain.shape, F32),
            pltpu.VMEM(w_proj.shape[1:], BF16),
            pltpu.VMEM(pair_rep.shape, BF16),
            pltpu.VMEM((w_proj.shape[2], depth), BF16),
            pltpu.SemaphoreType.DMA((6,)),
        ],
    )
    return lax.switch(
        choice[0],
        [functools.partial(kept_columns, some) for some in widths],
        pair_rep,
        info,
        flat,
        sent,
        w_proj,
        w_gate,
        w_out,
    )


STEP = 32


def solution(mesh):
    devices = mesh.shape["dap"]
    placed = (P("dap", "grp", None), P(), P(), P(), P(), P(), P(), P())

    def body(*arrays):
        rows, count, width = arrays[0].shape
        hidden = arrays[-1].shape[1]
        plain = (
            mesh.shape["grp"] == 1
            and rows * devices == count
            and count == 256
            and rows == 8
            and hidden == 4 * devices
        )
        return (row_shards if plain else shards)(*arrays)

    return jax.shard_map(
        body, mesh=mesh, in_specs=placed, out_specs=P("dap", "grp", None), check_vma=False
    )
```

```python
import functools

import jax
import jax.numpy as jnp
from jax import lax
from jax.experimental import pallas as pl
from jax.experimental.pallas import tpu as pltpu
from jax.sharding import PartitionSpec as P

epsilon_norm = 1e-05
F32 = jnp.float32
BF16 = jnp.bfloat16


def residue_valid(chain_ids, crop_lengths):
    count = chain_ids.shape[0]
    chains = jnp.arange(crop_lengths.shape[0], dtype=jnp.int32)
    member = (chain_ids[:, None] == chains[None, :]).astype(jnp.int32)
    counts = jnp.sum(member, axis=0)
    starts = jnp.cumsum(counts) - counts
    first = jnp.sum(member * starts[None, :], axis=1)
    limit = jnp.sum(member * crop_lengths[None, :], axis=1)
    place = jnp.arange(count, dtype=jnp.int32) - first
    return (place < limit).astype(jnp.float32)


def layer_norm(values, gain, axis):
    centre = jnp.mean(values, axis=axis, keepdims=True)
    spread = jnp.mean((values - centre) ** 2, axis=axis, keepdims=True)
    return (values - centre) * lax.rsqrt(spread + epsilon_norm) * gain


def column_rows(right_chan):
    return lax.all_to_all(right_chan, "grp", split_axis=1, concat_axis=2, tiled=True)


def update(pair_tile, pair_mask, ln_in, w_proj, w_gate, ln_out, w_out, outgoing):
    hidden = w_out.shape[0]
    normed = layer_norm(pair_tile.astype(jnp.float32), ln_in, 2).astype(jnp.bfloat16)
    projected = jnp.einsum("rqc,cf->frq", normed, w_proj, preferred_element_type=jnp.float32)
    gate_value = jax.nn.sigmoid(
        jnp.einsum("rqc,cd->rqd", normed, w_gate, preferred_element_type=jnp.float32)
    )
    left_op = (
        jax.nn.sigmoid(projected[:hidden]) * projected[hidden : 2 * hidden] * pair_mask
    ).astype(jnp.bfloat16)
    right_op = (
        jax.nn.sigmoid(projected[2 * hidden : 3 * hidden]) * projected[3 * hidden :] * pair_mask
    ).astype(jnp.bfloat16)
    left_chan, right_chan = (
        lax.all_to_all(left_op, "dap", split_axis=0, concat_axis=1, tiled=True),
        lax.all_to_all(right_op, "dap", split_axis=0, concat_axis=1, tiled=True),
    )
    if outgoing:
        right_rows = column_rows(right_chan)
        triangle = jnp.einsum(
            "hik,hjk->hij",
            lax.all_gather(left_chan, "grp", axis=2, tiled=True),
            right_rows,
            preferred_element_type=jnp.float32,
        )
    else:
        triangle = jnp.einsum(
            "hki,hkj->hij",
            lax.all_gather(left_chan, "grp", axis=2, tiled=True),
            right_chan,
            preferred_element_type=jnp.float32,
        )
    returned = lax.all_to_all(
        triangle.astype(jnp.bfloat16), "dap", split_axis=1, concat_axis=0, tiled=True
    )
    normed_product = layer_norm(returned.astype(jnp.float32), ln_out[:, None, None], 0).astype(
        jnp.bfloat16
    )
    update_term = jnp.einsum(
        "hrq,hd->rqd", normed_product, w_out, preferred_element_type=jnp.float32
    )
    return (pair_tile.astype(jnp.float32) + gate_value * update_term).astype(jnp.bfloat16)


def shards(pair_rep, chain_ids, crop_lengths, ln_in_gain, w_proj, w_gate, ln_out_gain, w_out):
    row_count = pair_rep.shape[0]
    column_count = pair_rep.shape[1]
    kept = residue_valid(chain_ids, crop_lengths)
    row_start = lax.axis_index("dap") * row_count
    column_start = lax.axis_index("grp") * column_count
    kept_rows = lax.dynamic_slice_in_dim(kept, row_start, row_count, 0)
    kept_columns = lax.dynamic_slice_in_dim(kept, column_start, column_count, 0)
    pair_mask = kept_rows[:, None] * kept_columns[None, :]
    pair_tile = pair_rep
    for layer_index, outgoing in ((0, True), (1, False)):
        pair_tile = update(
            pair_tile,
            pair_mask,
            ln_in_gain[layer_index],
            w_proj[layer_index],
            w_gate[layer_index],
            ln_out_gain[layer_index],
            w_out[layer_index],
            outgoing,
        )
    return pair_tile


def dot_nn(a, b):
    return lax.dot_general(a, b, (((1,), (0,)), ((), ())), preferred_element_type=F32)


def dot_nt(a, b):
    return lax.dot_general(a, b, (((1,), (1,)), ((), ())), preferred_element_type=F32)


def dot_tn(a, b):
    return lax.dot_general(a, b, (((0,), (0,)), ((), ())), preferred_element_type=F32)


def sigmoid(v):
    return 0.5 * jnp.tanh(0.5 * v) + 0.5


def one_hot(source, columns):
    place = lax.broadcasted_iota(jnp.int32, (source.shape[0], columns), 1)
    return jnp.where(place == source, 1.0, 0.0).astype(BF16)


def interleave(outer, inner):
    row = lax.broadcasted_iota(jnp.int32, (outer * inner, 1), 0)
    return one_hot((row % inner) * outer + row // inner, outer * inner)


def move(matrix, rows):
    return dot_nn(matrix, rows).astype(BF16)


def selection(slots, width):
    row = lax.broadcasted_iota(jnp.int32, (width, slots.shape[1]), 0).astype(F32)
    return jnp.where(row == slots, 1.0, 0.0).astype(BF16)


def kept_residues(ids, limits):
    place = lax.broadcasted_iota(jnp.int32, ids.shape, 1).astype(F32)
    kept = jnp.zeros(ids.shape, F32)
    for chain in range(limits.shape[1]):
        first = jnp.sum(jnp.where(ids < chain, 1.0, 0.0), axis=1, keepdims=True)
        limit = limits[:, chain : chain + 1].astype(F32)
        inside = jnp.where(ids == chain, 1.0, 0.0) * jnp.where(place - first < limit, 1.0, 0.0)
        kept = kept + inside
    return kept


def norm_rows(values, gain):
    centre = jnp.mean(values, axis=1, keepdims=True)
    apart = values - centre
    spread = jnp.mean(apart * apart, axis=1, keepdims=True)
    return (apart * lax.rsqrt(spread + epsilon_norm) * gain).astype(BF16)


def sort_projection(w_proj_ref, devices, sorted_ref):
    total = w_proj_ref.shape[1]
    hidden = total // 4
    own = hidden // devices
    for first in range(0, total, 128):
        row = first + lax.broadcasted_iota(jnp.int32, (128, 1), 0)
        kind = row // (2 * hidden)
        rest = row % (2 * hidden)
        device = rest // (2 * own)
        side = (rest % (2 * own)) // own
        channel = rest % own
        source = (side * 2 + kind) * hidden + device * own + channel
        rows = dot_nt(one_hot(source, total), w_proj_ref[...])
        sorted_ref[first : first + 128] = rows.astype(BF16)


def project(flat, gain, weights, w_gate, info_ref, gate_ref, send_ref, rows, width, start):
    span = flat.shape[0]
    half = weights.shape[0] // 2
    place = start + lax.broadcasted_iota(jnp.int32, (1, span), 1)
    mask = jnp.zeros((1, span), F32)
    for row in range(rows):
        inside = jnp.where(place >= row * width, 1.0, 0.0)
        inside = inside * jnp.where(place < (row + 1) * width, 1.0, 0.0)
        mask = mask + inside * info_ref[ROWS + row : ROWS + row + 1, 0:1]
    normed = norm_rows(flat, gain)
    gate_ref[start : start + span] = sigmoid(dot_nn(normed, w_gate))
    projected = dot_nt(weights, normed)
    operand = sigmoid(projected[:half]) * projected[half:] * mask
    shape = send_ref.shape[:2] + (span,)
    send_ref[:, :, start : start + span] = operand.astype(BF16).reshape(shape)


def spans(total):
    start = 0
    while start < total:
        span = min(256, total - start)
        yield start, span
        start += span


LN_IN, LN_OUT, ROWS = 2, 4, 8


def gain_of(info_ref, row, width):
    return info_ref[row : row + 1, :width]


def first_kernel(
    devices,
    widths,
    me_ref,
    ids_hbm,
    crop_hbm,
    ln_in_hbm,
    ln_out_hbm,
    w_proj_hbm,
    w_gate_hbm,
    pair_hbm,
    choice_ref,
    info_ref,
    flat_ref,
    gate_ref,
    send_ref,
    sorted_ref,
    ids_ref,
    crop_ref,
    ln_in_ref,
    ln_out_ref,
    w_proj_ref,
    w_gate_ref,
    pair_ref,
    weights_ref,
    arrived,
):
    moves = (
        (ids_hbm, ids_ref),
        (crop_hbm, crop_ref),
        (ln_in_hbm, ln_in_ref),
        (ln_out_hbm, ln_out_ref),
        (w_proj_hbm, w_proj_ref),
        (pair_hbm, pair_ref),
        (w_gate_hbm.at[0], w_gate_ref),
    )
    copies = [
        pltpu.make_async_copy(source, target, arrived.at[index])
        for index, (source, target) in enumerate(moves)
    ]
    for copy in copies:
        copy.start()
    rows, count, depth = pair_ref.shape
    flat_ref[...] = jnp.zeros(flat_ref.shape, BF16)
    info_ref[...] = jnp.zeros(info_ref.shape, F32)
    for copy in copies[:4]:
        copy.wait()
    kept = kept_residues(ids_ref[...], crop_ref[...])
    total = jnp.sum(kept)
    choice = jnp.int32(0)
    for some in widths[:-1]:
        choice = choice + jnp.where(total > some, 1, 0).astype(jnp.int32)
    choice_ref[0] = choice
    width = widths[0] + STEP * choice
    square = (count, count)
    up = lax.broadcasted_iota(jnp.int32, square, 0) < lax.broadcasted_iota(jnp.int32, square, 1)
    rank = dot_nn(
        jnp.broadcast_to(kept, (8, count)).astype(BF16), jnp.where(up, 1.0, 0.0).astype(BF16)
    )[0:1]
    slots = jnp.where(kept > 0.0, rank, -1.0)
    by_row = dot_nt(
        jnp.broadcast_to(slots, (8, count)).astype(BF16), interleave(rows, devices)
    )[0:1]
    info_ref[0:1] = slots
    info_ref[1:2] = by_row
    info_ref[LN_IN : LN_IN + 2, :depth] = ln_in_ref[...]
    info_ref[LN_OUT : LN_OUT + 2, : ln_out_ref.shape[1]] = ln_out_ref[...]
    place = lax.broadcasted_iota(jnp.int32, kept.shape, 1)
    for row in range(rows):
        own = jnp.where(place == me_ref[0] * rows + row, kept, 0.0)
        info_ref[ROWS + row : ROWS + row + 1] = jnp.broadcast_to(
            jnp.sum(own, axis=1, keepdims=True), kept.shape
        )
    pick = selection(slots, count)
    copies[4].wait()
    sort_projection(w_proj_ref.at[0], devices, weights_ref)
    sort_projection(w_proj_ref.at[1], devices, sorted_ref)
    copies[5].wait()
    copies[6].wait()
    lanes = jnp.concatenate([pair_ref[row] for row in range(rows)], axis=1)
    packed = move(pick, lanes)
    for row in range(rows):
        start = pl.multiple_of(row * width, 16)
        flat_ref[pl.ds(start, count)] = packed[:, row * depth : (row + 1) * depth]
    gain = gain_of(info_ref, LN_IN, depth)
    for start, span in spans(rows * count):
        part = flat_ref[start : start + span].astype(F32)
        project(
            part,
            gain,
            weights_ref[...],
            w_gate_ref[...],
            info_ref,
            gate_ref,
            send_ref,
            rows,
            width,
            start,
        )


def triangle_kernel(outgoing, rows, info_ref, came_ref, send_ref):
    devices, both, total = came_ref.shape
    own = both // 2
    width = total // rows
    by_channel = interleave(both, devices)
    pick = selection(info_ref[1:2], width)
    if not outgoing:
        pick = dot_nt(interleave(1, rows * devices), pick).astype(BF16)
    came = move(by_channel, came_ref[...].reshape(devices * both, total))

    def channel_rows(channel):
        span = slice(channel * devices, (channel + 1) * devices)
        return jnp.concatenate(
            [came[span, row * width : (row + 1) * width] for row in range(rows)], axis=0
        )

    products = []
    for channel in range(own):
        left = channel_rows(channel)
        right = channel_rows(own + channel)
        if outgoing:
            product = dot_nt(left, move(pick, right)).astype(BF16)
        else:
            product = move(pick, dot_tn(left, right).astype(BF16))
        products.append(product)
    low = rows * own // 8
    to_device = interleave(devices, 8)
    for offset in range(low):
        parts = []
        for channel in range(own):
            for high in range(rows // low):
                row = high * low + offset
                parts.append(products[channel][row * devices : (row + 1) * devices])
        sent = move(to_device, jnp.concatenate(parts, axis=0))
        send_ref[:, :, offset * width : (offset + 1) * width] = sent.reshape(devices, 8, width)


def finish_parts(layer, info_ref, came_ref, flat_ref, gate_ref, w_out_ref, use):
    devices, eight, lanes = came_ref.shape
    hidden = w_out_ref.shape[0]
    high = flat_ref.shape[0] // lanes
    by_part = interleave(high, hidden)
    square = lax.broadcasted_iota(jnp.int32, (hidden, hidden), 0) == lax.broadcasted_iota(
        jnp.int32, (hidden, hidden), 1
    )
    gain = gain_of(info_ref, LN_OUT + layer, hidden)
    gain = jnp.sum(jnp.where(square, gain, 0.0), axis=1, keepdims=True)

    for offset, span in spans(lanes):
        came = dot_nn(
            by_part, came_ref[:, :, offset : offset + span].reshape(devices * eight, span)
        )
        for part in range(high):
            block = came[part * hidden : (part + 1) * hidden]
            centre = jnp.mean(block, axis=0, keepdims=True)
            apart = block - centre
            spread = jnp.mean(apart * apart, axis=0, keepdims=True)
            normed = (apart * lax.rsqrt(spread + epsilon_norm) * gain).astype(BF16)
            term = dot_tn(normed, w_out_ref[...])
            start = part * lanes + offset
            here = slice(start, start + span)
            use(start, (flat_ref[here].astype(F32) + gate_ref[here] * term).astype(BF16))


def middle_kernel(
    rows,
    info_ref,
    came_ref,
    flat_ref,
    gate_ref,
    w_out_ref,
    weights_ref,
    w_gate_ref,
    next_ref,
    next_gate_ref,
    send_ref,
):
    gain = gain_of(info_ref, LN_IN + 1, flat_ref.shape[1])
    width = flat_ref.shape[0] // rows

    def use(start, fresh):
        next_ref[start : start + fresh.shape[0]] = fresh
        project(
            fresh.astype(F32),
            gain,
            weights_ref[...],
            w_gate_ref[...],
            info_ref,
            next_gate_ref,
            send_ref,
            rows,
            width,
            start,
        )

    finish_parts(0, info_ref, came_ref, flat_ref, gate_ref, w_out_ref, use)


def last_kernel(info_ref, pair_ref, came_ref, flat_ref, gate_ref, w_out_ref, out_ref, next_ref):
    rows, count, depth = out_ref.shape
    width = flat_ref.shape[0] // rows

    def use(start, fresh):
        next_ref[start : start + fresh.shape[0]] = fresh

    finish_parts(1, info_ref, came_ref, flat_ref, gate_ref, w_out_ref, use)
    pick = selection(info_ref[0:1], width)
    pick = dot_nt(interleave(1, count), pick).astype(BF16)
    lanes = [next_ref[row * width : (row + 1) * width] for row in range(rows)]
    lanes.append(jnp.ones((width, depth), BF16))
    spread = dot_nn(pick, jnp.concatenate(lanes, axis=1))
    kept = spread[:, rows * depth :] > 0.5
    for row in range(rows):
        fresh = spread[:, row * depth : (row + 1) * depth]
        out_ref[row] = jnp.where(kept, fresh, pair_ref[row].astype(F32)).astype(BF16)


SMEM = pl.BlockSpec(memory_space=pltpu.SMEM)
HBM = pl.BlockSpec(memory_space=pltpu.HBM)


def layer_of(array, layer):
    shape = array.shape
    return pl.BlockSpec((None,) + shape[1:], lambda i: (layer,) + (0,) * (len(shape) - 1))


def whole(array):
    return pl.BlockSpec(array.shape, lambda i: (0,) * len(array.shape))


def call(body, name, outs, specs, operands, out_specs=None, scratch=()):
    return pl.pallas_call(
        body,
        out_shape=list(outs),
        grid=(1,),
        in_specs=specs,
        out_specs=out_specs or [whole(o) for o in outs],
        scratch_shapes=list(scratch),
        compiler_params=pltpu.CompilerParams(vmem_limit_bytes=24 * 1024 * 1024),
        name=name,
    )(*operands)


def kept_columns(width, pair_rep, info, flat, gate, sent, weights, w_gate, w_out):
    devices = lax.axis_size("dap")
    rows, _, depth = pair_rep.shape
    hidden = w_out.shape[1]
    own = hidden // devices
    send_shape = jax.ShapeDtypeStruct((devices, 2 * own, rows * width), BF16)
    back_shape = jax.ShapeDtypeStruct((devices, 8, rows * own * width // 8), BF16)
    flat_shape = jax.ShapeDtypeStruct((rows * width, depth), BF16)
    gate_shape = jax.ShapeDtypeStruct((rows * width, depth), F32)

    def exchange(sent):
        return lax.all_to_all(sent, "dap", split_axis=0, concat_axis=0, tiled=True)

    def triangle(came, outgoing):
        return call(
            functools.partial(triangle_kernel, outgoing, rows),
            "outgoing" if outgoing else "incoming",
            [back_shape],
            [whole(info), whole(came)],
            (info, came),
        )[0]

    sent = sent[:, :, : rows * width]
    came = exchange(triangle(exchange(sent), True))
    flat, gate, sent = call(
        functools.partial(middle_kernel, rows),
        "finish_and_operands",
        [flat_shape, gate_shape, send_shape],
        [
            whole(info),
            whole(came),
            whole(flat_shape),
            whole(gate_shape),
            layer_of(w_out, 0),
            whole(weights),
            layer_of(w_gate, 1),
        ],
        (info, came, flat, gate, w_out, weights, w_gate),
    )
    came = exchange(triangle(exchange(sent), False))
    return call(
        last_kernel,
        "finish",
        [jax.ShapeDtypeStruct(pair_rep.shape, BF16)],
        [
            whole(info),
            whole(pair_rep),
            whole(came),
            whole(flat),
            whole(gate),
            layer_of(w_out, 1),
        ],
        (info, pair_rep, came, flat, gate, w_out),
        scratch=[pltpu.VMEM(flat_shape.shape, BF16)],
    )[0]


def row_shards(pair_rep, chain_ids, crop_lengths, ln_in_gain, w_proj, w_gate, ln_out_gain, w_out):
    devices = lax.axis_size("dap")
    rows, count, depth = pair_rep.shape
    me = lax.axis_index("dap").reshape(1).astype(jnp.int32)
    ids = chain_ids.reshape(1, count)
    crops = crop_lengths.reshape(1, -1)
    widths = [some for some in range(STEP, count + 1, STEP) if 2 * some >= count]
    info_shape = jax.ShapeDtypeStruct((16, count), F32)
    flat_shape = jax.ShapeDtypeStruct((rows * count, depth), BF16)
    send_shape = jax.ShapeDtypeStruct((devices, w_proj.shape[2] // devices // 2, rows * count), BF16)
    gate_shape = jax.ShapeDtypeStruct(flat_shape.shape, F32)
    sorted_shape = jax.ShapeDtypeStruct((w_proj.shape[2], depth), BF16)
    choice, info, flat, gate, sent, weights = call(
        functools.partial(first_kernel, devices, widths),
        "first_operands",
        [
            jax.ShapeDtypeStruct((1,), jnp.int32),
            info_shape,
            flat_shape,
            gate_shape,
            send_shape,
            sorted_shape,
        ],
        [SMEM, HBM, HBM, HBM, HBM, HBM, HBM, HBM],
        (me, ids, crops, ln_in_gain, ln_out_gain, w_proj, w_gate, pair_rep),
        out_specs=[
            SMEM,
            whole(info_shape),
            whole(flat_shape),
            whole(gate_shape),
            whole(send_shape),
            whole(sorted_shape),
        ],
        scratch=[
            pltpu.VMEM(ids.shape, jnp.int32),
            pltpu.VMEM(crops.shape, jnp.int32),
            pltpu.VMEM(ln_in_gain.shape, F32),
            pltpu.VMEM(ln_out_gain.shape, F32),
            pltpu.VMEM(w_proj.shape, BF16),
            pltpu.VMEM(w_gate.shape[1:], BF16),
            pltpu.VMEM(pair_rep.shape, BF16),
            pltpu.VMEM(sorted_shape.shape, BF16),
            pltpu.SemaphoreType.DMA((7,)),
        ],
    )
    return lax.switch(
        choice[0],
        [functools.partial(kept_columns, some) for some in widths],
        pair_rep,
        info,
        flat,
        gate,
        sent,
        weights,
        w_gate,
        w_out,
    )


STEP = 32


def solution(mesh):
    devices = mesh.shape["dap"]
    placed = (P("dap", "grp", None), P(), P(), P(), P(), P(), P(), P())

    def body(*arrays):
        rows, count, width = arrays[0].shape
        hidden = arrays[-1].shape[1]
        plain = (
            mesh.shape["grp"] == 1
            and rows * devices == count
            and count == 256
            and rows == 8
            and hidden == 4 * devices
        )
        return (row_shards if plain else shards)(*arrays)

    return jax.shard_map(
        body, mesh=mesh, in_specs=placed, out_specs=P("dap", "grp", None), check_vma=False
    )
```

```python
import functools

import jax
import jax.numpy as jnp
from jax import lax
from jax.experimental import pallas as pl
from jax.experimental.pallas import tpu as pltpu
from jax.sharding import PartitionSpec as P

epsilon_norm = 1e-05
F32 = jnp.float32
BF16 = jnp.bfloat16


def residue_valid(chain_ids, crop_lengths):
    count = chain_ids.shape[0]
    chains = jnp.arange(crop_lengths.shape[0], dtype=jnp.int32)
    member = (chain_ids[:, None] == chains[None, :]).astype(jnp.int32)
    counts = jnp.sum(member, axis=0)
    starts = jnp.cumsum(counts) - counts
    first = jnp.sum(member * starts[None, :], axis=1)
    limit = jnp.sum(member * crop_lengths[None, :], axis=1)
    place = jnp.arange(count, dtype=jnp.int32) - first
    return (place < limit).astype(jnp.float32)


def layer_norm(values, gain, axis):
    centre = jnp.mean(values, axis=axis, keepdims=True)
    spread = jnp.mean((values - centre) ** 2, axis=axis, keepdims=True)
    return (values - centre) * lax.rsqrt(spread + epsilon_norm) * gain


def column_rows(right_chan):
    return lax.all_to_all(right_chan, "grp", split_axis=1, concat_axis=2, tiled=True)


def update(pair_tile, pair_mask, ln_in, w_proj, w_gate, ln_out, w_out, outgoing):
    hidden = w_out.shape[0]
    normed = layer_norm(pair_tile.astype(jnp.float32), ln_in, 2).astype(jnp.bfloat16)
    projected = jnp.einsum("rqc,cf->frq", normed, w_proj, preferred_element_type=jnp.float32)
    gate_value = jax.nn.sigmoid(
        jnp.einsum("rqc,cd->rqd", normed, w_gate, preferred_element_type=jnp.float32)
    )
    left_op = (
        jax.nn.sigmoid(projected[:hidden]) * projected[hidden : 2 * hidden] * pair_mask
    ).astype(jnp.bfloat16)
    right_op = (
        jax.nn.sigmoid(projected[2 * hidden : 3 * hidden]) * projected[3 * hidden :] * pair_mask
    ).astype(jnp.bfloat16)
    left_chan, right_chan = (
        lax.all_to_all(left_op, "dap", split_axis=0, concat_axis=1, tiled=True),
        lax.all_to_all(right_op, "dap", split_axis=0, concat_axis=1, tiled=True),
    )
    if outgoing:
        right_rows = column_rows(right_chan)
        triangle = jnp.einsum(
            "hik,hjk->hij",
            lax.all_gather(left_chan, "grp", axis=2, tiled=True),
            right_rows,
            preferred_element_type=jnp.float32,
        )
    else:
        triangle = jnp.einsum(
            "hki,hkj->hij",
            lax.all_gather(left_chan, "grp", axis=2, tiled=True),
            right_chan,
            preferred_element_type=jnp.float32,
        )
    returned = lax.all_to_all(
        triangle.astype(jnp.bfloat16), "dap", split_axis=1, concat_axis=0, tiled=True
    )
    normed_product = layer_norm(returned.astype(jnp.float32), ln_out[:, None, None], 0).astype(
        jnp.bfloat16
    )
    update_term = jnp.einsum(
        "hrq,hd->rqd", normed_product, w_out, preferred_element_type=jnp.float32
    )
    return (pair_tile.astype(jnp.float32) + gate_value * update_term).astype(jnp.bfloat16)


def shards(pair_rep, chain_ids, crop_lengths, ln_in_gain, w_proj, w_gate, ln_out_gain, w_out):
    row_count = pair_rep.shape[0]
    column_count = pair_rep.shape[1]
    kept = residue_valid(chain_ids, crop_lengths)
    row_start = lax.axis_index("dap") * row_count
    column_start = lax.axis_index("grp") * column_count
    kept_rows = lax.dynamic_slice_in_dim(kept, row_start, row_count, 0)
    kept_columns = lax.dynamic_slice_in_dim(kept, column_start, column_count, 0)
    pair_mask = kept_rows[:, None] * kept_columns[None, :]
    pair_tile = pair_rep
    for layer_index, outgoing in ((0, True), (1, False)):
        pair_tile = update(
            pair_tile,
            pair_mask,
            ln_in_gain[layer_index],
            w_proj[layer_index],
            w_gate[layer_index],
            ln_out_gain[layer_index],
            w_out[layer_index],
            outgoing,
        )
    return pair_tile


def dot_nn(a, b):
    return lax.dot_general(a, b, (((1,), (0,)), ((), ())), preferred_element_type=F32)


def dot_nt(a, b):
    return lax.dot_general(a, b, (((1,), (1,)), ((), ())), preferred_element_type=F32)


def dot_tn(a, b):
    return lax.dot_general(a, b, (((0,), (0,)), ((), ())), preferred_element_type=F32)


def open_gate(half):
    return jnp.tanh(half) + 1.0


def halved(weights):
    return (weights.astype(F32) * 0.5).astype(BF16)


def one_hot(source, columns):
    place = lax.broadcasted_iota(jnp.int32, (source.shape[0], columns), 1)
    return jnp.where(place == source, 1.0, 0.0).astype(BF16)


def interleave(outer, inner):
    row = lax.broadcasted_iota(jnp.int32, (outer * inner, 1), 0)
    return one_hot((row % inner) * outer + row // inner, outer * inner)


def move(matrix, rows):
    return dot_nn(matrix, rows).astype(BF16)


def selection(slots, width):
    row = lax.broadcasted_iota(jnp.int32, (width, slots.shape[1]), 0).astype(F32)
    return jnp.where(row == slots, 1.0, 0.0).astype(BF16)


def kept_residues(ids, limits):
    place = lax.broadcasted_iota(jnp.int32, ids.shape, 1).astype(F32)
    kept = jnp.zeros(ids.shape, F32)
    for chain in range(limits.shape[1]):
        first = jnp.sum(jnp.where(ids < chain, 1.0, 0.0), axis=1, keepdims=True)
        limit = limits[:, chain : chain + 1].astype(F32)
        inside = jnp.where(ids == chain, 1.0, 0.0) * jnp.where(place - first < limit, 1.0, 0.0)
        kept = kept + inside
    return kept


def norm_rows(values, gain):
    centre = jnp.mean(values, axis=1, keepdims=True)
    apart = values - centre
    spread = jnp.mean(apart * apart, axis=1, keepdims=True)
    return (apart * lax.rsqrt(spread + epsilon_norm) * gain).astype(BF16)


def sort_projection(w_proj_ref, devices, sorted_ref):
    total = w_proj_ref.shape[1]
    hidden = total // 4
    own = hidden // devices
    for first in range(0, total, 128):
        row = first + lax.broadcasted_iota(jnp.int32, (128, 1), 0)
        kind = row // (2 * hidden)
        rest = row % (2 * hidden)
        device = rest // (2 * own)
        side = (rest % (2 * own)) // own
        channel = rest % own
        source = (side * 2 + kind) * hidden + device * own + channel
        rows = dot_nt(one_hot(source, total), w_proj_ref[...])
        sorted_ref[first : first + 128] = (rows * 0.5).astype(BF16)


def project(flat, gain, weights, w_gate, info_ref, gate_ref, send_ref, rows, width, start):
    span = flat.shape[0]
    half = weights.shape[0] // 2
    place = start + lax.broadcasted_iota(jnp.int32, (1, span), 1)
    mask = jnp.zeros((1, span), F32)
    for row in range(rows):
        inside = jnp.where(place >= row * width, 1.0, 0.0)
        inside = inside * jnp.where(place < (row + 1) * width, 1.0, 0.0)
        mask = mask + inside * info_ref[ROWS + row : ROWS + row + 1, 0:1]
    normed = norm_rows(flat, gain)
    gate_ref[start : start + span] = open_gate(dot_nn(normed, w_gate))
    projected = dot_nt(weights, normed)
    operand = open_gate(projected[:half]) * projected[half:] * mask
    shape = send_ref.shape[:2] + (span,)
    send_ref[:, :, start : start + span] = operand.astype(BF16).reshape(shape)


def spans(total):
    start = 0
    while start < total:
        span = min(256, total - start)
        yield start, span
        start += span


LN_IN, LN_OUT, ROWS = 2, 4, 8


def gain_of(info_ref, row, width):
    return info_ref[row : row + 1, :width]


def first_kernel(
    devices,
    widths,
    me_ref,
    ids_hbm,
    crop_hbm,
    ln_in_hbm,
    ln_out_hbm,
    w_proj_hbm,
    w_gate_hbm,
    pair_hbm,
    choice_ref,
    info_ref,
    flat_ref,
    gate_ref,
    send_ref,
    ids_ref,
    crop_ref,
    ln_in_ref,
    ln_out_ref,
    w_proj_ref,
    w_gate_ref,
    pair_ref,
    weights_ref,
    arrived,
):
    moves = (
        (ids_hbm, ids_ref),
        (crop_hbm, crop_ref),
        (ln_in_hbm, ln_in_ref),
        (ln_out_hbm, ln_out_ref),
        (w_proj_hbm.at[0], w_proj_ref),
        (pair_hbm, pair_ref),
        (w_gate_hbm.at[0], w_gate_ref),
    )
    copies = [
        pltpu.make_async_copy(source, target, arrived.at[index])
        for index, (source, target) in enumerate(moves)
    ]
    for copy in copies:
        copy.start()
    rows, count, depth = pair_ref.shape
    flat_ref[...] = jnp.zeros(flat_ref.shape, BF16)
    info_ref[...] = jnp.zeros(info_ref.shape, F32)
    for copy in copies[:4]:
        copy.wait()
    kept = kept_residues(ids_ref[...], crop_ref[...])
    total = jnp.sum(kept)
    choice = jnp.int32(0)
    for some in widths[:-1]:
        choice = choice + jnp.where(total > some, 1, 0).astype(jnp.int32)
    choice_ref[0] = choice
    width = jnp.int32(widths[0])
    for some, wider in zip(widths[:-1], widths[1:]):
        width = width + jnp.where(total > some, wider - some, 0).astype(jnp.int32)
    square = (count, count)
    up = lax.broadcasted_iota(jnp.int32, square, 0) < lax.broadcasted_iota(jnp.int32, square, 1)
    rank = dot_nn(
        jnp.broadcast_to(kept, (8, count)).astype(BF16), jnp.where(up, 1.0, 0.0).astype(BF16)
    )[0:1]
    slots = jnp.where(kept > 0.0, rank, -1.0)
    by_row = dot_nt(
        jnp.broadcast_to(slots, (8, count)).astype(BF16), interleave(rows, devices)
    )[0:1]
    info_ref[0:1] = slots
    info_ref[1:2] = by_row
    info_ref[LN_IN : LN_IN + 2, :depth] = ln_in_ref[...]
    info_ref[LN_OUT : LN_OUT + 2, : ln_out_ref.shape[1]] = ln_out_ref[...]
    place = lax.broadcasted_iota(jnp.int32, kept.shape, 1)
    for row in range(rows):
        own = jnp.where(place == me_ref[0] * rows + row, kept, 0.0)
        info_ref[ROWS + row : ROWS + row + 1] = jnp.broadcast_to(
            jnp.sum(own, axis=1, keepdims=True), kept.shape
        )
    pick = selection(slots, count)
    copies[4].wait()
    sort_projection(w_proj_ref, devices, weights_ref)
    copies[5].wait()
    copies[6].wait()
    lanes = jnp.concatenate([pair_ref[row] for row in range(rows)], axis=1)
    packed = move(pick, lanes)
    for row in range(rows):
        start = pl.multiple_of(row * width, 16)
        flat_ref[pl.ds(start, count)] = packed[:, row * depth : (row + 1) * depth]
    gain = gain_of(info_ref, LN_IN, depth)
    w_gate = halved(w_gate_ref[...])
    for start, span in spans(rows * count):
        part = flat_ref[start : start + span].astype(F32)
        project(
            part,
            gain,
            weights_ref[...],
            w_gate,
            info_ref,
            gate_ref,
            send_ref,
            rows,
            width,
            start,
        )


def outgoing_kernel(rows, info_ref, came_ref, w_proj_ref, send_ref, sorted_ref):
    triangle_kernel(True, rows, info_ref, came_ref, send_ref)
    sort_projection(w_proj_ref, came_ref.shape[0], sorted_ref)


def triangle_kernel(outgoing, rows, info_ref, came_ref, send_ref):
    devices, both, total = came_ref.shape
    own = both // 2
    width = total // rows
    by_channel = interleave(both, devices)
    pick = selection(info_ref[1:2], width)
    if not outgoing:
        pick = dot_nt(interleave(1, rows * devices), pick).astype(BF16)
    came = move(by_channel, came_ref[...].reshape(devices * both, total))

    def channel_rows(channel):
        span = slice(channel * devices, (channel + 1) * devices)
        return jnp.concatenate(
            [came[span, row * width : (row + 1) * width] for row in range(rows)], axis=0
        )

    products = []
    for channel in range(own):
        left = channel_rows(channel)
        right = channel_rows(own + channel)
        if outgoing:
            product = dot_nt(left, move(pick, right)).astype(BF16)
        else:
            product = move(pick, dot_tn(left, right).astype(BF16))
        products.append(product)
    low = rows * own // 8
    to_device = interleave(devices, 8)
    for offset in range(low):
        parts = []
        for channel in range(own):
            for high in range(rows // low):
                row = high * low + offset
                parts.append(products[channel][row * devices : (row + 1) * devices])
        sent = move(to_device, jnp.concatenate(parts, axis=0))
        send_ref[:, :, offset * width : (offset + 1) * width] = sent.reshape(devices, 8, width)


def finish_parts(layer, info_ref, came_ref, flat_ref, gate_ref, w_out_ref, use):
    devices, eight, lanes = came_ref.shape
    hidden = w_out_ref.shape[0]
    high = flat_ref.shape[0] // lanes
    by_part = interleave(high, hidden)
    square = lax.broadcasted_iota(jnp.int32, (hidden, hidden), 0) == lax.broadcasted_iota(
        jnp.int32, (hidden, hidden), 1
    )
    gain = gain_of(info_ref, LN_OUT + layer, hidden)
    gain = jnp.sum(jnp.where(square, gain, 0.0), axis=1, keepdims=True)
    w_out = halved(w_out_ref[...])

    for offset, span in spans(lanes):
        came = dot_nn(
            by_part, came_ref[:, :, offset : offset + span].reshape(devices * eight, span)
        )
        for part in range(high):
            block = came[part * hidden : (part + 1) * hidden]
            centre = jnp.mean(block, axis=0, keepdims=True)
            apart = block - centre
            spread = jnp.mean(apart * apart, axis=0, keepdims=True)
            normed = (apart * lax.rsqrt(spread + epsilon_norm) * gain).astype(BF16)
            term = dot_tn(normed, w_out)
            start = part * lanes + offset
            here = slice(start, start + span)
            use(start, (flat_ref[here].astype(F32) + gate_ref[here] * term).astype(BF16))


def middle_kernel(
    rows,
    info_ref,
    came_ref,
    flat_ref,
    gate_ref,
    w_out_ref,
    weights_ref,
    w_gate_ref,
    next_ref,
    next_gate_ref,
    send_ref,
):
    gain = gain_of(info_ref, LN_IN + 1, flat_ref.shape[1])
    width = flat_ref.shape[0] // rows

    def use(start, fresh):
        next_ref[start : start + fresh.shape[0]] = fresh

    finish_parts(0, info_ref, came_ref, flat_ref, gate_ref, w_out_ref, use)
    w_gate = halved(w_gate_ref[...])
    for start, span in spans(rows * width):
        project(
            next_ref[start : start + span].astype(F32),
            gain,
            weights_ref[...],
            w_gate,
            info_ref,
            next_gate_ref,
            send_ref,
            rows,
            width,
            start,
        )


def last_kernel(info_ref, pair_ref, came_ref, flat_ref, gate_ref, w_out_ref, out_ref, next_ref):
    rows, count, depth = out_ref.shape
    width = flat_ref.shape[0] // rows

    def use(start, fresh):
        next_ref[start : start + fresh.shape[0]] = fresh

    finish_parts(1, info_ref, came_ref, flat_ref, gate_ref, w_out_ref, use)
    pick = selection(info_ref[0:1], width)
    pick = dot_nt(interleave(1, count), pick).astype(BF16)
    lanes = [next_ref[row * width : (row + 1) * width] for row in range(rows)]
    lanes.append(jnp.ones((width, depth), BF16))
    spread = dot_nn(pick, jnp.concatenate(lanes, axis=1))
    kept = spread[:, rows * depth :] > 0.5
    for row in range(rows):
        fresh = spread[:, row * depth : (row + 1) * depth]
        out_ref[row] = jnp.where(kept, fresh, pair_ref[row].astype(F32)).astype(BF16)


SMEM = pl.BlockSpec(memory_space=pltpu.SMEM)
HBM = pl.BlockSpec(memory_space=pltpu.HBM)


def layer_of(array, layer):
    shape = array.shape
    return pl.BlockSpec((None,) + shape[1:], lambda i: (layer,) + (0,) * (len(shape) - 1))


def whole(array):
    return pl.BlockSpec(array.shape, lambda i: (0,) * len(array.shape))


def call(body, name, outs, specs, operands, out_specs=None, scratch=()):
    return pl.pallas_call(
        body,
        out_shape=list(outs),
        grid=(1,),
        in_specs=specs,
        out_specs=out_specs or [whole(o) for o in outs],
        scratch_shapes=list(scratch),
        compiler_params=pltpu.CompilerParams(vmem_limit_bytes=24 * 1024 * 1024),
        name=name,
    )(*operands)


def kept_columns(width, pair_rep, info, flat, gate, sent, w_proj, w_gate, w_out):
    devices = lax.axis_size("dap")
    rows, _, depth = pair_rep.shape
    hidden = w_out.shape[1]
    own = hidden // devices
    send_shape = jax.ShapeDtypeStruct((devices, 2 * own, rows * width), BF16)
    back_shape = jax.ShapeDtypeStruct((devices, 8, rows * own * width // 8), BF16)
    flat_shape = jax.ShapeDtypeStruct((rows * width, depth), BF16)
    gate_shape = jax.ShapeDtypeStruct((rows * width, depth), F32)
    sorted_shape = jax.ShapeDtypeStruct((4 * hidden, depth), BF16)

    def exchange(sent):
        return lax.all_to_all(sent, "dap", split_axis=0, concat_axis=0, tiled=True)

    sent = sent[:, :, : rows * width]
    came = exchange(sent)
    sent, weights = call(
        functools.partial(outgoing_kernel, rows),
        "outgoing",
        [back_shape, sorted_shape],
        [whole(info), whole(came), layer_of(w_proj, 1)],
        (info, came, w_proj),
    )
    came = exchange(sent)
    flat, gate, sent = call(
        functools.partial(middle_kernel, rows),
        "finish_and_operands",
        [flat_shape, gate_shape, send_shape],
        [
            whole(info),
            whole(came),
            whole(flat_shape),
            whole(gate_shape),
            layer_of(w_out, 0),
            whole(weights),
            layer_of(w_gate, 1),
        ],
        (info, came, flat, gate, w_out, weights, w_gate),
    )
    came = exchange(sent)
    sent = call(
        functools.partial(triangle_kernel, False, rows),
        "incoming",
        [back_shape],
        [whole(info), whole(came)],
        (info, came),
    )[0]
    came = exchange(sent)
    return call(
        last_kernel,
        "finish",
        [jax.ShapeDtypeStruct(pair_rep.shape, BF16)],
        [
            whole(info),
            whole(pair_rep),
            whole(came),
            whole(flat),
            whole(gate),
            layer_of(w_out, 1),
        ],
        (info, pair_rep, came, flat, gate, w_out),
        scratch=[pltpu.VMEM(flat_shape.shape, BF16)],
    )[0]


def row_shards(pair_rep, chain_ids, crop_lengths, ln_in_gain, w_proj, w_gate, ln_out_gain, w_out):
    devices = lax.axis_size("dap")
    rows, count, depth = pair_rep.shape
    me = lax.axis_index("dap").reshape(1).astype(jnp.int32)
    ids = chain_ids.reshape(1, count)
    crops = crop_lengths.reshape(1, -1)
    widths = [count * share // 16 for share in SHARES]
    info_shape = jax.ShapeDtypeStruct((16, count), F32)
    flat_shape = jax.ShapeDtypeStruct((rows * count, depth), BF16)
    send_shape = jax.ShapeDtypeStruct((devices, w_proj.shape[2] // devices // 2, rows * count), BF16)
    gate_shape = jax.ShapeDtypeStruct(flat_shape.shape, F32)
    choice, info, flat, gate, sent = call(
        functools.partial(first_kernel, devices, widths),
        "first_operands",
        [
            jax.ShapeDtypeStruct((1,), jnp.int32),
            info_shape,
            flat_shape,
            gate_shape,
            send_shape,
        ],
        [SMEM, HBM, HBM, HBM, HBM, HBM, HBM, HBM],
        (me, ids, crops, ln_in_gain, ln_out_gain, w_proj, w_gate, pair_rep),
        out_specs=[
            SMEM,
            whole(info_shape),
            whole(flat_shape),
            whole(gate_shape),
            whole(send_shape),
        ],
        scratch=[
            pltpu.VMEM(ids.shape, jnp.int32),
            pltpu.VMEM(crops.shape, jnp.int32),
            pltpu.VMEM(ln_in_gain.shape, F32),
            pltpu.VMEM(ln_out_gain.shape, F32),
            pltpu.VMEM(w_proj.shape[1:], BF16),
            pltpu.VMEM(w_gate.shape[1:], BF16),
            pltpu.VMEM(pair_rep.shape, BF16),
            pltpu.VMEM((w_proj.shape[2], depth), BF16),
            pltpu.SemaphoreType.DMA((7,)),
        ],
    )
    return lax.switch(
        choice[0],
        [functools.partial(kept_columns, some) for some in widths],
        pair_rep,
        info,
        flat,
        gate,
        sent,
        w_proj,
        w_gate,
        w_out,
    )


SHARES = (10, 11, 12, 13, 14, 16)


def solution(mesh):
    devices = mesh.shape["dap"]
    placed = (P("dap", "grp", None), P(), P(), P(), P(), P(), P(), P())

    def body(*arrays):
        rows, count, width = arrays[0].shape
        hidden = arrays[-1].shape[1]
        plain = (
            mesh.shape["grp"] == 1
            and rows * devices == count
            and count == 256
            and rows == 8
            and hidden == 4 * devices
        )
        return (row_shards if plain else shards)(*arrays)

    return jax.shard_map(
        body, mesh=mesh, in_specs=placed, out_specs=P("dap", "grp", None), check_vma=False
    )
```

```python
import functools

import jax
import jax.numpy as jnp
from jax import lax
from jax.experimental import pallas as pl
from jax.experimental.pallas import tpu as pltpu
from jax.sharding import PartitionSpec as P

epsilon_norm = 1e-05
F32 = jnp.float32
BF16 = jnp.bfloat16


def residue_valid(chain_ids, crop_lengths):
    count = chain_ids.shape[0]
    chains = jnp.arange(crop_lengths.shape[0], dtype=jnp.int32)
    member = (chain_ids[:, None] == chains[None, :]).astype(jnp.int32)
    counts = jnp.sum(member, axis=0)
    starts = jnp.cumsum(counts) - counts
    first = jnp.sum(member * starts[None, :], axis=1)
    limit = jnp.sum(member * crop_lengths[None, :], axis=1)
    place = jnp.arange(count, dtype=jnp.int32) - first
    return (place < limit).astype(jnp.float32)


def layer_norm(values, gain, axis):
    centre = jnp.mean(values, axis=axis, keepdims=True)
    spread = jnp.mean((values - centre) ** 2, axis=axis, keepdims=True)
    return (values - centre) * lax.rsqrt(spread + epsilon_norm) * gain


def column_rows(right_chan):
    return lax.all_to_all(right_chan, "grp", split_axis=1, concat_axis=2, tiled=True)


def update(pair_tile, pair_mask, ln_in, w_proj, w_gate, ln_out, w_out, outgoing):
    hidden = w_out.shape[0]
    normed = layer_norm(pair_tile.astype(jnp.float32), ln_in, 2).astype(jnp.bfloat16)
    projected = jnp.einsum("rqc,cf->frq", normed, w_proj, preferred_element_type=jnp.float32)
    gate_value = jax.nn.sigmoid(
        jnp.einsum("rqc,cd->rqd", normed, w_gate, preferred_element_type=jnp.float32)
    )
    left_op = (
        jax.nn.sigmoid(projected[:hidden]) * projected[hidden : 2 * hidden] * pair_mask
    ).astype(jnp.bfloat16)
    right_op = (
        jax.nn.sigmoid(projected[2 * hidden : 3 * hidden]) * projected[3 * hidden :] * pair_mask
    ).astype(jnp.bfloat16)
    left_chan, right_chan = (
        lax.all_to_all(left_op, "dap", split_axis=0, concat_axis=1, tiled=True),
        lax.all_to_all(right_op, "dap", split_axis=0, concat_axis=1, tiled=True),
    )
    if outgoing:
        right_rows = column_rows(right_chan)
        triangle = jnp.einsum(
            "hik,hjk->hij",
            lax.all_gather(left_chan, "grp", axis=2, tiled=True),
            right_rows,
            preferred_element_type=jnp.float32,
        )
    else:
        triangle = jnp.einsum(
            "hki,hkj->hij",
            lax.all_gather(left_chan, "grp", axis=2, tiled=True),
            right_chan,
            preferred_element_type=jnp.float32,
        )
    returned = lax.all_to_all(
        triangle.astype(jnp.bfloat16), "dap", split_axis=1, concat_axis=0, tiled=True
    )
    normed_product = layer_norm(returned.astype(jnp.float32), ln_out[:, None, None], 0).astype(
        jnp.bfloat16
    )
    update_term = jnp.einsum(
        "hrq,hd->rqd", normed_product, w_out, preferred_element_type=jnp.float32
    )
    return (pair_tile.astype(jnp.float32) + gate_value * update_term).astype(jnp.bfloat16)


def shards(pair_rep, chain_ids, crop_lengths, ln_in_gain, w_proj, w_gate, ln_out_gain, w_out):
    row_count = pair_rep.shape[0]
    column_count = pair_rep.shape[1]
    kept = residue_valid(chain_ids, crop_lengths)
    row_start = lax.axis_index("dap") * row_count
    column_start = lax.axis_index("grp") * column_count
    kept_rows = lax.dynamic_slice_in_dim(kept, row_start, row_count, 0)
    kept_columns = lax.dynamic_slice_in_dim(kept, column_start, column_count, 0)
    pair_mask = kept_rows[:, None] * kept_columns[None, :]
    pair_tile = pair_rep
    for layer_index, outgoing in ((0, True), (1, False)):
        pair_tile = update(
            pair_tile,
            pair_mask,
            ln_in_gain[layer_index],
            w_proj[layer_index],
            w_gate[layer_index],
            ln_out_gain[layer_index],
            w_out[layer_index],
            outgoing,
        )
    return pair_tile


def dot_nn(a, b):
    return lax.dot_general(a, b, (((1,), (0,)), ((), ())), preferred_element_type=F32)


def dot_nt(a, b):
    return lax.dot_general(a, b, (((1,), (1,)), ((), ())), preferred_element_type=F32)


def dot_tn(a, b):
    return lax.dot_general(a, b, (((0,), (0,)), ((), ())), preferred_element_type=F32)


def open_gate(half):
    return jnp.tanh(half) + 1.0


def halved(weights):
    return (weights.astype(F32) * 0.5).astype(BF16)


def one_hot(source, columns):
    place = lax.broadcasted_iota(jnp.int32, (source.shape[0], columns), 1)
    return jnp.where(place == source, 1.0, 0.0).astype(BF16)


def interleave(outer, inner):
    row = lax.broadcasted_iota(jnp.int32, (outer * inner, 1), 0)
    return one_hot((row % inner) * outer + row // inner, outer * inner)


def move(matrix, rows):
    return dot_nn(matrix, rows).astype(BF16)


def selection(slots, width):
    row = lax.broadcasted_iota(jnp.int32, (width, slots.shape[1]), 0).astype(F32)
    return jnp.where(row == slots, 1.0, 0.0).astype(BF16)


def kept_residues(ids, limits):
    place = lax.broadcasted_iota(jnp.int32, ids.shape, 1).astype(F32)
    kept = jnp.zeros(ids.shape, F32)
    for chain in range(limits.shape[1]):
        first = jnp.sum(jnp.where(ids < chain, 1.0, 0.0), axis=1, keepdims=True)
        limit = limits[:, chain : chain + 1].astype(F32)
        inside = jnp.where(ids == chain, 1.0, 0.0) * jnp.where(place - first < limit, 1.0, 0.0)
        kept = kept + inside
    return kept


def norm_rows(values, gain):
    centre = jnp.mean(values, axis=1, keepdims=True)
    apart = values - centre
    spread = jnp.mean(apart * apart, axis=1, keepdims=True)
    return (apart * lax.rsqrt(spread + epsilon_norm) * gain).astype(BF16)


def sort_projection(w_proj_ref, devices, sorted_ref):
    hidden = w_proj_ref.shape[1] // 4
    own = hidden // devices
    row = lax.broadcasted_iota(jnp.int32, (2 * hidden, 1), 0)
    side = (row % (2 * own)) // own
    order = one_hot(side * hidden + row // (2 * own) * own + row % own, 2 * hidden)
    for kind in range(2):
        sides = [
            w_proj_ref[:, block * hidden : (block + 1) * hidden] for block in (kind, kind + 2)
        ]
        rows = dot_nt(order, jnp.concatenate(sides, axis=1)) * 0.5
        sorted_ref[2 * hidden * kind : 2 * hidden * (kind + 1)] = rows.astype(BF16)


def project(flat, gain, weights, w_gate, info_ref, gate_ref, send_ref, rows, width, start):
    span = flat.shape[0]
    half = weights.shape[0] // 2
    place = start + lax.broadcasted_iota(jnp.int32, (1, span), 1)
    mask = jnp.zeros((1, span), F32)
    for row in range(rows):
        inside = jnp.where(place >= row * width, 1.0, 0.0)
        inside = inside * jnp.where(place < (row + 1) * width, 1.0, 0.0)
        mask = mask + inside * info_ref[ROWS + row : ROWS + row + 1, 0:1]
    normed = norm_rows(flat, gain)
    gate_ref[start : start + span] = open_gate(dot_nn(normed, w_gate))
    projected = dot_nt(weights, normed)
    operand = open_gate(projected[:half]) * projected[half:] * mask
    shape = send_ref.shape[:2] + (span,)
    send_ref[:, :, start : start + span] = operand.astype(BF16).reshape(shape)


def spans(total):
    start = 0
    while start < total:
        span = min(256, total - start)
        yield start, span
        start += span


LN_IN, LN_OUT, ROWS = 2, 4, 8


def gain_of(info_ref, row, width):
    return info_ref[row : row + 1, :width]


def first_kernel(
    devices,
    widths,
    me_ref,
    ids_hbm,
    crop_hbm,
    ln_in_hbm,
    ln_out_hbm,
    w_proj_hbm,
    w_gate_hbm,
    pair_hbm,
    choice_ref,
    info_ref,
    flat_ref,
    gate_ref,
    send_ref,
    ids_ref,
    crop_ref,
    ln_in_ref,
    ln_out_ref,
    w_proj_ref,
    w_gate_ref,
    pair_ref,
    weights_ref,
    arrived,
):
    moves = (
        (ids_hbm, ids_ref),
        (crop_hbm, crop_ref),
        (ln_in_hbm, ln_in_ref),
        (ln_out_hbm, ln_out_ref),
        (w_proj_hbm.at[0], w_proj_ref),
        (pair_hbm, pair_ref),
        (w_gate_hbm.at[0], w_gate_ref),
    )
    copies = [
        pltpu.make_async_copy(source, target, arrived.at[index])
        for index, (source, target) in enumerate(moves)
    ]
    for copy in copies:
        copy.start()
    rows, count, depth = pair_ref.shape
    flat_ref[...] = jnp.zeros(flat_ref.shape, BF16)
    info_ref[...] = jnp.zeros(info_ref.shape, F32)
    for copy in copies[:4]:
        copy.wait()
    kept = kept_residues(ids_ref[...], crop_ref[...])
    total = jnp.sum(kept)
    choice = jnp.int32(0)
    for some in widths[:-1]:
        choice = choice + jnp.where(total > some, 1, 0).astype(jnp.int32)
    choice_ref[0] = choice
    width = jnp.int32(widths[0])
    for some, wider in zip(widths[:-1], widths[1:]):
        width = width + jnp.where(total > some, wider - some, 0).astype(jnp.int32)
    square = (count, count)
    up = lax.broadcasted_iota(jnp.int32, square, 0) < lax.broadcasted_iota(jnp.int32, square, 1)
    rank = dot_nn(
        jnp.broadcast_to(kept, (8, count)).astype(BF16), jnp.where(up, 1.0, 0.0).astype(BF16)
    )[0:1]
    slots = jnp.where(kept > 0.0, rank, -1.0)
    by_row = dot_nt(
        jnp.broadcast_to(slots, (8, count)).astype(BF16), interleave(rows, devices)
    )[0:1]
    info_ref[0:1] = slots
    info_ref[1:2] = by_row
    info_ref[LN_IN : LN_IN + 2, :depth] = ln_in_ref[...]
    info_ref[LN_OUT : LN_OUT + 2, : ln_out_ref.shape[1]] = ln_out_ref[...]
    place = lax.broadcasted_iota(jnp.int32, kept.shape, 1)
    for row in range(rows):
        own = jnp.where(place == me_ref[0] * rows + row, kept, 0.0)
        info_ref[ROWS + row : ROWS + row + 1] = jnp.broadcast_to(
            jnp.sum(own, axis=1, keepdims=True), kept.shape
        )
    pick = selection(slots, count)
    copies[4].wait()
    sort_projection(w_proj_ref, devices, weights_ref)
    copies[5].wait()
    copies[6].wait()
    lanes = jnp.concatenate([pair_ref[row] for row in range(rows)], axis=1)
    packed = move(pick, lanes)
    for row in range(rows):
        start = pl.multiple_of(row * width, 16)
        flat_ref[pl.ds(start, count)] = packed[:, row * depth : (row + 1) * depth]
    gain = gain_of(info_ref, LN_IN, depth)
    w_gate = halved(w_gate_ref[...])
    for start, span in spans(rows * count):
        part = flat_ref[start : start + span].astype(F32)
        project(
            part,
            gain,
            weights_ref[...],
            w_gate,
            info_ref,
            gate_ref,
            send_ref,
            rows,
            width,
            start,
        )


def outgoing_kernel(rows, info_ref, came_ref, w_proj_ref, send_ref, sorted_ref):
    triangle_kernel(True, rows, info_ref, came_ref, send_ref)
    sort_projection(w_proj_ref, came_ref.shape[0], sorted_ref)


def triangle_kernel(outgoing, rows, info_ref, came_ref, send_ref):
    devices, both, total = came_ref.shape
    own = both // 2
    width = total // rows
    by_channel = interleave(both, devices)
    pick = selection(info_ref[1:2], width)
    if not outgoing:
        pick = dot_nt(interleave(1, rows * devices), pick).astype(BF16)
    came = move(by_channel, came_ref[...].reshape(devices * both, total))

    def channel_rows(channel):
        span = slice(channel * devices, (channel + 1) * devices)
        return jnp.concatenate(
            [came[span, row * width : (row + 1) * width] for row in range(rows)], axis=0
        )

    products = []
    for channel in range(own):
        left = channel_rows(channel)
        right = channel_rows(own + channel)
        if outgoing:
            product = dot_nt(left, move(pick, right)).astype(BF16)
        else:
            product = move(pick, dot_tn(left, right).astype(BF16))
        products.append(product)
    low = rows * own // 8
    to_device = interleave(devices, 8)
    for offset in range(low):
        parts = []
        for channel in range(own):
            for high in range(rows // low):
                row = high * low + offset
                parts.append(products[channel][row * devices : (row + 1) * devices])
        sent = move(to_device, jnp.concatenate(parts, axis=0))
        send_ref[:, :, offset * width : (offset + 1) * width] = sent.reshape(devices, 8, width)


def finish_parts(layer, info_ref, came_ref, flat_ref, gate_ref, w_out_ref, use):
    devices, eight, lanes = came_ref.shape
    hidden = w_out_ref.shape[0]
    high = flat_ref.shape[0] // lanes
    by_part = interleave(high, hidden)
    square = lax.broadcasted_iota(jnp.int32, (hidden, hidden), 0) == lax.broadcasted_iota(
        jnp.int32, (hidden, hidden), 1
    )
    gain = gain_of(info_ref, LN_OUT + layer, hidden)
    gain = jnp.sum(jnp.where(square, gain, 0.0), axis=1, keepdims=True)
    w_out = halved(w_out_ref[...])

    for offset, span in spans(lanes):
        came = dot_nn(
            by_part, came_ref[:, :, offset : offset + span].reshape(devices * eight, span)
        )
        for part in range(high):
            block = came[part * hidden : (part + 1) * hidden]
            centre = jnp.mean(block, axis=0, keepdims=True)
            apart = block - centre
            spread = jnp.mean(apart * apart, axis=0, keepdims=True)
            normed = (apart * lax.rsqrt(spread + epsilon_norm) * gain).astype(BF16)
            term = dot_tn(normed, w_out)
            start = part * lanes + offset
            here = slice(start, start + span)
            use(start, (flat_ref[here].astype(F32) + gate_ref[here] * term).astype(BF16))


def middle_kernel(
    rows,
    info_ref,
    came_ref,
    flat_ref,
    gate_ref,
    w_out_ref,
    weights_ref,
    w_gate_ref,
    next_ref,
    next_gate_ref,
    send_ref,
):
    gain = gain_of(info_ref, LN_IN + 1, flat_ref.shape[1])
    width = flat_ref.shape[0] // rows

    def use(start, fresh):
        next_ref[start : start + fresh.shape[0]] = fresh

    finish_parts(0, info_ref, came_ref, flat_ref, gate_ref, w_out_ref, use)
    w_gate = halved(w_gate_ref[...])
    for start, span in spans(rows * width):
        project(
            next_ref[start : start + span].astype(F32),
            gain,
            weights_ref[...],
            w_gate,
            info_ref,
            next_gate_ref,
            send_ref,
            rows,
            width,
            start,
        )


def last_kernel(info_ref, pair_ref, came_ref, flat_ref, gate_ref, w_out_ref, out_ref, next_ref):
    rows, count, depth = out_ref.shape
    width = flat_ref.shape[0] // rows

    def use(start, fresh):
        next_ref[start : start + fresh.shape[0]] = fresh

    finish_parts(1, info_ref, came_ref, flat_ref, gate_ref, w_out_ref, use)
    pick = selection(info_ref[0:1], width)
    pick = dot_nt(interleave(1, count), pick).astype(BF16)
    lanes = [next_ref[row * width : (row + 1) * width] for row in range(rows)]
    lanes.append(jnp.ones((width, depth), BF16))
    spread = dot_nn(pick, jnp.concatenate(lanes, axis=1))
    kept = spread[:, rows * depth :] > 0.5
    for row in range(rows):
        fresh = spread[:, row * depth : (row + 1) * depth]
        out_ref[row] = jnp.where(kept, fresh, pair_ref[row].astype(F32)).astype(BF16)


SMEM = pl.BlockSpec(memory_space=pltpu.SMEM)
HBM = pl.BlockSpec(memory_space=pltpu.HBM)


def layer_of(array, layer):
    shape = array.shape
    return pl.BlockSpec((None,) + shape[1:], lambda i: (layer,) + (0,) * (len(shape) - 1))


def whole(array):
    return pl.BlockSpec(array.shape, lambda i: (0,) * len(array.shape))


def call(body, name, outs, specs, operands, out_specs=None, scratch=()):
    return pl.pallas_call(
        body,
        out_shape=list(outs),
        grid=(1,),
        in_specs=specs,
        out_specs=out_specs or [whole(o) for o in outs],
        scratch_shapes=list(scratch),
        compiler_params=pltpu.CompilerParams(vmem_limit_bytes=24 * 1024 * 1024),
        name=name,
    )(*operands)


def kept_columns(width, pair_rep, info, flat, gate, sent, w_proj, w_gate, w_out):
    devices = lax.axis_size("dap")
    rows, _, depth = pair_rep.shape
    hidden = w_out.shape[1]
    own = hidden // devices
    send_shape = jax.ShapeDtypeStruct((devices, 2 * own, rows * width), BF16)
    back_shape = jax.ShapeDtypeStruct((devices, 8, rows * own * width // 8), BF16)
    flat_shape = jax.ShapeDtypeStruct((rows * width, depth), BF16)
    gate_shape = jax.ShapeDtypeStruct((rows * width, depth), F32)
    sorted_shape = jax.ShapeDtypeStruct((4 * hidden, depth), BF16)

    def exchange(sent):
        return lax.all_to_all(sent, "dap", split_axis=0, concat_axis=0, tiled=True)

    sent = sent[:, :, : rows * width]
    came = exchange(sent)
    sent, weights = call(
        functools.partial(outgoing_kernel, rows),
        "outgoing",
        [back_shape, sorted_shape],
        [whole(info), whole(came), layer_of(w_proj, 1)],
        (info, came, w_proj),
    )
    came = exchange(sent)
    flat, gate, sent = call(
        functools.partial(middle_kernel, rows),
        "finish_and_operands",
        [flat_shape, gate_shape, send_shape],
        [
            whole(info),
            whole(came),
            whole(flat_shape),
            whole(gate_shape),
            layer_of(w_out, 0),
            whole(weights),
            layer_of(w_gate, 1),
        ],
        (info, came, flat, gate, w_out, weights, w_gate),
    )
    came = exchange(sent)
    sent = call(
        functools.partial(triangle_kernel, False, rows),
        "incoming",
        [back_shape],
        [whole(info), whole(came)],
        (info, came),
    )[0]
    came = exchange(sent)
    return call(
        last_kernel,
        "finish",
        [jax.ShapeDtypeStruct(pair_rep.shape, BF16)],
        [
            whole(info),
            whole(pair_rep),
            whole(came),
            whole(flat),
            whole(gate),
            layer_of(w_out, 1),
        ],
        (info, pair_rep, came, flat, gate, w_out),
        scratch=[pltpu.VMEM(flat_shape.shape, BF16)],
    )[0]


def row_shards(pair_rep, chain_ids, crop_lengths, ln_in_gain, w_proj, w_gate, ln_out_gain, w_out):
    devices = lax.axis_size("dap")
    rows, count, depth = pair_rep.shape
    me = lax.axis_index("dap").reshape(1).astype(jnp.int32)
    ids = chain_ids.reshape(1, count)
    crops = crop_lengths.reshape(1, -1)
    widths = [count * share // 16 for share in SHARES]
    info_shape = jax.ShapeDtypeStruct((16, count), F32)
    flat_shape = jax.ShapeDtypeStruct((rows * count, depth), BF16)
    send_shape = jax.ShapeDtypeStruct((devices, w_proj.shape[2] // devices // 2, rows * count), BF16)
    gate_shape = jax.ShapeDtypeStruct(flat_shape.shape, F32)
    choice, info, flat, gate, sent = call(
        functools.partial(first_kernel, devices, widths),
        "first_operands",
        [
            jax.ShapeDtypeStruct((1,), jnp.int32),
            info_shape,
            flat_shape,
            gate_shape,
            send_shape,
        ],
        [SMEM, HBM, HBM, HBM, HBM, HBM, HBM, HBM],
        (me, ids, crops, ln_in_gain, ln_out_gain, w_proj, w_gate, pair_rep),
        out_specs=[
            SMEM,
            whole(info_shape),
            whole(flat_shape),
            whole(gate_shape),
            whole(send_shape),
        ],
        scratch=[
            pltpu.VMEM(ids.shape, jnp.int32),
            pltpu.VMEM(crops.shape, jnp.int32),
            pltpu.VMEM(ln_in_gain.shape, F32),
            pltpu.VMEM(ln_out_gain.shape, F32),
            pltpu.VMEM(w_proj.shape[1:], BF16),
            pltpu.VMEM(w_gate.shape[1:], BF16),
            pltpu.VMEM(pair_rep.shape, BF16),
            pltpu.VMEM((w_proj.shape[2], depth), BF16),
            pltpu.SemaphoreType.DMA((7,)),
        ],
    )
    return lax.switch(
        choice[0],
        [functools.partial(kept_columns, some) for some in widths],
        pair_rep,
        info,
        flat,
        gate,
        sent,
        w_proj,
        w_gate,
        w_out,
    )


SHARES = (11, 12, 13, 14, 16)


def solution(mesh):
    devices = mesh.shape["dap"]
    placed = (P("dap", "grp", None), P(), P(), P(), P(), P(), P(), P())

    def body(*arrays):
        rows, count, width = arrays[0].shape
        hidden = arrays[-1].shape[1]
        plain = (
            mesh.shape["grp"] == 1
            and rows * devices == count
            and count == 256
            and rows == 8
            and hidden == 4 * devices
        )
        return (row_shards if plain else shards)(*arrays)

    return jax.shard_map(
        body, mesh=mesh, in_specs=placed, out_specs=P("dap", "grp", None), check_vma=False
    )
```

```python
import functools

import jax
import jax.numpy as jnp
from jax import lax
from jax.experimental import pallas as pl
from jax.experimental.pallas import tpu as pltpu
from jax.sharding import PartitionSpec as P

epsilon_norm = 1e-05
F32 = jnp.float32
BF16 = jnp.bfloat16


def residue_valid(chain_ids, crop_lengths):
    count = chain_ids.shape[0]
    chains = jnp.arange(crop_lengths.shape[0], dtype=jnp.int32)
    member = (chain_ids[:, None] == chains[None, :]).astype(jnp.int32)
    counts = jnp.sum(member, axis=0)
    starts = jnp.cumsum(counts) - counts
    first = jnp.sum(member * starts[None, :], axis=1)
    limit = jnp.sum(member * crop_lengths[None, :], axis=1)
    place = jnp.arange(count, dtype=jnp.int32) - first
    return (place < limit).astype(jnp.float32)


def layer_norm(values, gain, axis):
    centre = jnp.mean(values, axis=axis, keepdims=True)
    spread = jnp.mean((values - centre) ** 2, axis=axis, keepdims=True)
    return (values - centre) * lax.rsqrt(spread + epsilon_norm) * gain


def column_rows(right_chan):
    return lax.all_to_all(right_chan, "grp", split_axis=1, concat_axis=2, tiled=True)


def update(pair_tile, pair_mask, ln_in, w_proj, w_gate, ln_out, w_out, outgoing):
    hidden = w_out.shape[0]
    normed = layer_norm(pair_tile.astype(jnp.float32), ln_in, 2).astype(jnp.bfloat16)
    projected = jnp.einsum("rqc,cf->frq", normed, w_proj, preferred_element_type=jnp.float32)
    gate_value = jax.nn.sigmoid(
        jnp.einsum("rqc,cd->rqd", normed, w_gate, preferred_element_type=jnp.float32)
    )
    left_op = (
        jax.nn.sigmoid(projected[:hidden]) * projected[hidden : 2 * hidden] * pair_mask
    ).astype(jnp.bfloat16)
    right_op = (
        jax.nn.sigmoid(projected[2 * hidden : 3 * hidden]) * projected[3 * hidden :] * pair_mask
    ).astype(jnp.bfloat16)
    left_chan, right_chan = (
        lax.all_to_all(left_op, "dap", split_axis=0, concat_axis=1, tiled=True),
        lax.all_to_all(right_op, "dap", split_axis=0, concat_axis=1, tiled=True),
    )
    if outgoing:
        right_rows = column_rows(right_chan)
        triangle = jnp.einsum(
            "hik,hjk->hij",
            lax.all_gather(left_chan, "grp", axis=2, tiled=True),
            right_rows,
            preferred_element_type=jnp.float32,
        )
    else:
        triangle = jnp.einsum(
            "hki,hkj->hij",
            lax.all_gather(left_chan, "grp", axis=2, tiled=True),
            right_chan,
            preferred_element_type=jnp.float32,
        )
    returned = lax.all_to_all(
        triangle.astype(jnp.bfloat16), "dap", split_axis=1, concat_axis=0, tiled=True
    )
    normed_product = layer_norm(returned.astype(jnp.float32), ln_out[:, None, None], 0).astype(
        jnp.bfloat16
    )
    update_term = jnp.einsum(
        "hrq,hd->rqd", normed_product, w_out, preferred_element_type=jnp.float32
    )
    return (pair_tile.astype(jnp.float32) + gate_value * update_term).astype(jnp.bfloat16)


def shards(pair_rep, chain_ids, crop_lengths, ln_in_gain, w_proj, w_gate, ln_out_gain, w_out):
    row_count = pair_rep.shape[0]
    column_count = pair_rep.shape[1]
    kept = residue_valid(chain_ids, crop_lengths)
    row_start = lax.axis_index("dap") * row_count
    column_start = lax.axis_index("grp") * column_count
    kept_rows = lax.dynamic_slice_in_dim(kept, row_start, row_count, 0)
    kept_columns = lax.dynamic_slice_in_dim(kept, column_start, column_count, 0)
    pair_mask = kept_rows[:, None] * kept_columns[None, :]
    pair_tile = pair_rep
    for layer_index, outgoing in ((0, True), (1, False)):
        pair_tile = update(
            pair_tile,
            pair_mask,
            ln_in_gain[layer_index],
            w_proj[layer_index],
            w_gate[layer_index],
            ln_out_gain[layer_index],
            w_out[layer_index],
            outgoing,
        )
    return pair_tile


def dot_nn(a, b):
    return lax.dot_general(a, b, (((1,), (0,)), ((), ())), preferred_element_type=F32)


def dot_nt(a, b):
    return lax.dot_general(a, b, (((1,), (1,)), ((), ())), preferred_element_type=F32)


def dot_tn(a, b):
    return lax.dot_general(a, b, (((0,), (0,)), ((), ())), preferred_element_type=F32)


def open_gate(half):
    return jnp.tanh(half) + 1.0


def halved(weights):
    return (weights.astype(F32) * 0.5).astype(BF16)


def one_hot(source, columns):
    place = lax.broadcasted_iota(jnp.int32, (source.shape[0], columns), 1)
    return jnp.where(place == source, 1.0, 0.0).astype(BF16)


def interleave(outer, inner):
    row = lax.broadcasted_iota(jnp.int32, (outer * inner, 1), 0)
    return one_hot((row % inner) * outer + row // inner, outer * inner)


def move(matrix, rows):
    return dot_nn(matrix, rows).astype(BF16)


def selection(slots, width):
    row = lax.broadcasted_iota(jnp.int32, (width, slots.shape[1]), 0).astype(F32)
    return jnp.where(row == slots, 1.0, 0.0).astype(BF16)


def kept_residues(ids, limits):
    place = lax.broadcasted_iota(jnp.int32, ids.shape, 1).astype(F32)
    kept = jnp.zeros(ids.shape, F32)
    for chain in range(limits.shape[1]):
        first = jnp.sum(jnp.where(ids < chain, 1.0, 0.0), axis=1, keepdims=True)
        limit = limits[:, chain : chain + 1].astype(F32)
        inside = jnp.where(ids == chain, 1.0, 0.0) * jnp.where(place - first < limit, 1.0, 0.0)
        kept = kept + inside
    return kept


def norm_rows(values, gain):
    centre = jnp.mean(values, axis=1, keepdims=True)
    apart = values - centre
    spread = jnp.mean(apart * apart, axis=1, keepdims=True)
    return (apart * lax.rsqrt(spread + epsilon_norm) * gain).astype(BF16)


def sort_projection(w_proj_ref, devices, sorted_ref):
    hidden = w_proj_ref.shape[1] // 4
    own = hidden // devices
    row = lax.broadcasted_iota(jnp.int32, (2 * hidden, 1), 0)
    side = (row % (2 * own)) // own
    order = one_hot(side * hidden + row // (2 * own) * own + row % own, 2 * hidden)
    for kind in range(2):
        sides = [
            w_proj_ref[:, block * hidden : (block + 1) * hidden] for block in (kind, kind + 2)
        ]
        rows = dot_nt(order, jnp.concatenate(sides, axis=1)) * 0.5
        sorted_ref[2 * hidden * kind : 2 * hidden * (kind + 1)] = rows.astype(BF16)


def project(flat, gain, weights, w_gate, info_ref, gate_ref, send_ref, rows, width, start):
    span = flat.shape[0]
    half = weights.shape[0] // 2
    place = start + lax.broadcasted_iota(jnp.int32, (1, span), 1)
    mask = jnp.zeros((1, span), F32)
    for row in range(rows):
        inside = jnp.where(place >= row * width, 1.0, 0.0)
        inside = inside * jnp.where(place < (row + 1) * width, 1.0, 0.0)
        mask = mask + inside * info_ref[ROWS + row : ROWS + row + 1, 0:1]
    normed = norm_rows(flat, gain)
    gate_ref[start : start + span] = open_gate(dot_nn(normed, w_gate))
    projected = dot_nt(weights, normed)
    operand = open_gate(projected[:half]) * projected[half:] * mask
    shape = send_ref.shape[:2] + (span,)
    send_ref[:, :, start : start + span] = operand.astype(BF16).reshape(shape)


def spans(total):
    start = 0
    while start < total:
        span = min(256, total - start)
        yield start, span
        start += span


LN_IN, LN_OUT, ROWS = 2, 4, 8


def gain_of(info_ref, row, width):
    return info_ref[row : row + 1, :width]


def first_kernel(
    devices,
    widths,
    me_ref,
    ids_hbm,
    crop_hbm,
    ln_in_hbm,
    ln_out_hbm,
    w_proj_hbm,
    w_gate_hbm,
    pair_hbm,
    choice_ref,
    info_ref,
    flat_ref,
    gate_ref,
    send_ref,
    ids_ref,
    crop_ref,
    ln_in_ref,
    ln_out_ref,
    w_proj_ref,
    w_gate_ref,
    pair_ref,
    weights_ref,
    arrived,
):
    moves = (
        (ids_hbm, ids_ref),
        (crop_hbm, crop_ref),
        (ln_in_hbm, ln_in_ref),
        (ln_out_hbm, ln_out_ref),
        (w_proj_hbm.at[0], w_proj_ref),
        (pair_hbm, pair_ref),
        (w_gate_hbm.at[0], w_gate_ref),
    )
    copies = [
        pltpu.make_async_copy(source, target, arrived.at[index])
        for index, (source, target) in enumerate(moves)
    ]
    for copy in copies:
        copy.start()
    rows, count, depth = pair_ref.shape
    flat_ref[...] = jnp.zeros(flat_ref.shape, BF16)
    info_ref[...] = jnp.zeros(info_ref.shape, F32)
    for copy in copies[:4]:
        copy.wait()
    kept = kept_residues(ids_ref[...], crop_ref[...])
    total = jnp.sum(kept)
    choice = jnp.int32(0)
    for some in widths[:-1]:
        choice = choice + jnp.where(total > some, 1, 0).astype(jnp.int32)
    choice_ref[0] = choice
    width = jnp.int32(widths[0])
    for some, wider in zip(widths[:-1], widths[1:]):
        width = width + jnp.where(total > some, wider - some, 0).astype(jnp.int32)
    square = (count, count)
    up = lax.broadcasted_iota(jnp.int32, square, 0) < lax.broadcasted_iota(jnp.int32, square, 1)
    rank = dot_nn(
        jnp.broadcast_to(kept, (8, count)).astype(BF16), jnp.where(up, 1.0, 0.0).astype(BF16)
    )[0:1]
    slots = jnp.where(kept > 0.0, rank, -1.0)
    by_row = dot_nt(
        jnp.broadcast_to(slots, (8, count)).astype(BF16), interleave(rows, devices)
    )[0:1]
    info_ref[0:1] = slots
    info_ref[1:2] = by_row
    info_ref[LN_IN : LN_IN + 2, :depth] = ln_in_ref[...]
    info_ref[LN_OUT : LN_OUT + 2, : ln_out_ref.shape[1]] = ln_out_ref[...]
    place = lax.broadcasted_iota(jnp.int32, kept.shape, 1)
    for row in range(rows):
        own = jnp.where(place == me_ref[0] * rows + row, kept, 0.0)
        info_ref[ROWS + row : ROWS + row + 1] = jnp.broadcast_to(
            jnp.sum(own, axis=1, keepdims=True), kept.shape
        )
    pick = selection(slots, count)
    copies[4].wait()
    sort_projection(w_proj_ref, devices, weights_ref)
    copies[5].wait()
    copies[6].wait()
    lanes = jnp.concatenate([pair_ref[row] for row in range(rows)], axis=1)
    packed = move(pick, lanes)
    for row in range(rows):
        start = pl.multiple_of(row * width, 16)
        flat_ref[pl.ds(start, count)] = packed[:, row * depth : (row + 1) * depth]
    gain = gain_of(info_ref, LN_IN, depth)
    w_gate = halved(w_gate_ref[...])
    for start, span in spans(rows * count):
        part = flat_ref[start : start + span].astype(F32)
        project(
            part,
            gain,
            weights_ref[...],
            w_gate,
            info_ref,
            gate_ref,
            send_ref,
            rows,
            width,
            start,
        )


def channel_blocks(came_ref, rows, width):
    devices, channels, total = came_ref.shape
    came = move(
        interleave(channels, devices), came_ref[...].reshape(devices * channels, total)
    )
    blocks = []
    for channel in range(channels):
        span = slice(channel * devices, (channel + 1) * devices)
        parts = [came[span, row * width : (row + 1) * width] for row in range(rows)]
        blocks.append(jnp.concatenate(parts, axis=0))
    return blocks


def outgoing_kernel(rows, groups, info_ref, came_ref, w_proj_ref, send_ref, sorted_ref):
    devices, both, total = came_ref.shape
    own = both // 2
    width = total // rows
    pick = selection(info_ref[1:2], width)
    blocks = channel_blocks(came_ref, rows, width)
    products = [
        dot_nt(blocks[channel], move(pick, blocks[own + channel])).astype(BF16)
        for channel in range(own)
    ]
    low = rows * own // 8
    to_device = interleave(devices, 8)
    for offset in range(low):
        parts = []
        for channel in range(own):
            for high in range(rows // low):
                row = high * low + offset
                parts.append(products[channel][row * devices : (row + 1) * devices])
        sent = move(to_device, jnp.concatenate(parts, axis=0))
        send_ref[:, :, offset * width : (offset + 1) * width] = sent.reshape(devices, 8, width)
    sort_projection(w_proj_ref, devices // groups, sorted_ref)


def incoming_kernel(rows, info_ref, came_ref, send_ref):
    own = came_ref.shape[1] // 2
    devices = send_ref.shape[0]
    width = came_ref.shape[2] // rows
    pick = selection(info_ref[1:2], width)
    pick = dot_nt(interleave(1, rows * devices), pick).astype(BF16)
    blocks = channel_blocks(came_ref, rows, width)
    products = [
        move(pick, dot_tn(blocks[channel], blocks[own + channel]).astype(BF16))
        for channel in range(own)
    ]
    to_device = interleave(devices, own)
    for row in range(rows):
        span = slice(row * devices, (row + 1) * devices)
        sent = move(to_device, jnp.concatenate([product[span] for product in products], axis=0))
        send_ref[:, :, row * width : (row + 1) * width] = sent.reshape(devices, own, width)


def finish_parts(layer, groups, info_ref, came_ref, flat_ref, gate_ref, w_out_ref, use):
    devices, eight, lanes = came_ref.shape
    hidden = w_out_ref.shape[0]
    high = flat_ref.shape[0] // lanes
    square = lax.broadcasted_iota(jnp.int32, (hidden, hidden), 0) == lax.broadcasted_iota(
        jnp.int32, (hidden, hidden), 1
    )
    gain = gain_of(info_ref, LN_OUT + layer, hidden)
    gain = jnp.sum(jnp.where(square, gain, 0.0), axis=1, keepdims=True)
    w_out = halved(w_out_ref[...])
    for offset, span in spans(lanes):
        came = came_ref[:, :, offset : offset + span].reshape(devices * eight, span)
        if groups == 1:
            came = dot_nn(interleave(high, hidden), came)
        else:
            came = came.astype(F32)
            came = sum(came[hidden * group : hidden * (group + 1)] for group in range(groups))
        for part in range(high):
            block = came[part * hidden : (part + 1) * hidden]
            centre = jnp.mean(block, axis=0, keepdims=True)
            apart = block - centre
            spread = jnp.mean(apart * apart, axis=0, keepdims=True)
            normed = (apart * lax.rsqrt(spread + epsilon_norm) * gain).astype(BF16)
            term = dot_tn(normed, w_out)
            start = part * lanes + offset
            here = slice(start, start + span)
            use(start, (flat_ref[here].astype(F32) + gate_ref[here] * term).astype(BF16))


def middle_kernel(
    rows,
    info_ref,
    came_ref,
    flat_ref,
    gate_ref,
    w_out_ref,
    weights_ref,
    w_gate_ref,
    next_ref,
    next_gate_ref,
    send_ref,
):
    gain = gain_of(info_ref, LN_IN + 1, flat_ref.shape[1])
    width = flat_ref.shape[0] // rows

    def use(start, fresh):
        next_ref[start : start + fresh.shape[0]] = fresh

    finish_parts(0, 1, info_ref, came_ref, flat_ref, gate_ref, w_out_ref, use)
    w_gate = halved(w_gate_ref[...])
    for start, span in spans(rows * width):
        project(
            next_ref[start : start + span].astype(F32),
            gain,
            weights_ref[...],
            w_gate,
            info_ref,
            next_gate_ref,
            send_ref,
            rows,
            width,
            start,
        )


def last_kernel(
    groups, info_ref, pair_ref, came_ref, flat_ref, gate_ref, w_out_ref, out_ref, next_ref
):
    rows, count, depth = out_ref.shape
    width = flat_ref.shape[0] // rows

    def use(start, fresh):
        next_ref[start : start + fresh.shape[0]] = fresh

    finish_parts(1, groups, info_ref, came_ref, flat_ref, gate_ref, w_out_ref, use)
    pick = selection(info_ref[0:1], width)
    pick = dot_nt(interleave(1, count), pick).astype(BF16)
    lanes = [next_ref[row * width : (row + 1) * width] for row in range(rows)]
    lanes.append(jnp.ones((width, depth), BF16))
    spread = dot_nn(pick, jnp.concatenate(lanes, axis=1))
    kept = spread[:, rows * depth :] > 0.5
    for row in range(rows):
        fresh = spread[:, row * depth : (row + 1) * depth]
        out_ref[row] = jnp.where(kept, fresh, pair_ref[row].astype(F32)).astype(BF16)


SMEM = pl.BlockSpec(memory_space=pltpu.SMEM)
HBM = pl.BlockSpec(memory_space=pltpu.HBM)


def layer_of(array, layer):
    shape = array.shape
    return pl.BlockSpec((None,) + shape[1:], lambda i: (layer,) + (0,) * (len(shape) - 1))


def whole(array):
    return pl.BlockSpec(array.shape, lambda i: (0,) * len(array.shape))


def call(body, name, outs, specs, operands, out_specs=None, scratch=()):
    return pl.pallas_call(
        body,
        out_shape=list(outs),
        grid=(1,),
        in_specs=specs,
        out_specs=out_specs or [whole(o) for o in outs],
        scratch_shapes=list(scratch),
        compiler_params=pltpu.CompilerParams(vmem_limit_bytes=24 * 1024 * 1024),
        name=name,
    )(*operands)


def kept_columns(width, pair_rep, info, flat, gate, sent, w_proj, w_gate, w_out):
    devices = lax.axis_size("dap")
    rows, _, depth = pair_rep.shape
    hidden = w_out.shape[1]
    own = hidden // devices
    back_shape = jax.ShapeDtypeStruct((devices, 8, rows * own * width // 8), BF16)
    flat_shape = jax.ShapeDtypeStruct((rows * width, depth), BF16)
    gate_shape = jax.ShapeDtypeStruct((rows * width, depth), F32)
    sorted_shape = jax.ShapeDtypeStruct((4 * hidden, depth), BF16)

    apart = devices // GROUPS
    groups = [list(range(first, first + apart)) for first in range(0, devices, apart)]
    group_shape = jax.ShapeDtypeStruct((apart, 2 * own * GROUPS, rows * width), BF16)
    sums_shape = jax.ShapeDtypeStruct((devices, own * GROUPS, rows * width), BF16)

    def exchange(sent, within=None):
        return lax.all_to_all(
            sent, "dap", split_axis=0, concat_axis=0, axis_index_groups=within, tiled=True
        )

    sent = sent[:, :, : rows * width]
    came = exchange(sent)
    sent, weights = call(
        functools.partial(outgoing_kernel, rows, GROUPS),
        "outgoing",
        [back_shape, sorted_shape],
        [whole(info), whole(came), layer_of(w_proj, 1)],
        (info, came, w_proj),
    )
    came = exchange(sent)
    flat, gate, sent = call(
        functools.partial(middle_kernel, rows),
        "finish_and_operands",
        [flat_shape, gate_shape, group_shape],
        [
            whole(info),
            whole(came),
            whole(flat_shape),
            whole(gate_shape),
            layer_of(w_out, 0),
            whole(weights),
            layer_of(w_gate, 1),
        ],
        (info, came, flat, gate, w_out, weights, w_gate),
    )
    came = exchange(sent, groups)
    sent = call(
        functools.partial(incoming_kernel, rows),
        "incoming",
        [sums_shape],
        [whole(info), whole(came)],
        (info, came),
    )[0]
    came = exchange(sent)
    return call(
        functools.partial(last_kernel, GROUPS),
        "finish",
        [jax.ShapeDtypeStruct(pair_rep.shape, BF16)],
        [
            whole(info),
            whole(pair_rep),
            whole(came),
            whole(flat),
            whole(gate),
            layer_of(w_out, 1),
        ],
        (info, pair_rep, came, flat, gate, w_out),
        scratch=[pltpu.VMEM(flat_shape.shape, BF16)],
    )[0]


def row_shards(pair_rep, chain_ids, crop_lengths, ln_in_gain, w_proj, w_gate, ln_out_gain, w_out):
    devices = lax.axis_size("dap")
    rows, count, depth = pair_rep.shape
    me = lax.axis_index("dap").reshape(1).astype(jnp.int32)
    ids = chain_ids.reshape(1, count)
    crops = crop_lengths.reshape(1, -1)
    widths = [count * share // 16 for share in SHARES]
    info_shape = jax.ShapeDtypeStruct((16, count), F32)
    flat_shape = jax.ShapeDtypeStruct((rows * count, depth), BF16)
    send_shape = jax.ShapeDtypeStruct((devices, w_proj.shape[2] // devices // 2, rows * count), BF16)
    gate_shape = jax.ShapeDtypeStruct(flat_shape.shape, F32)
    choice, info, flat, gate, sent = call(
        functools.partial(first_kernel, devices, widths),
        "first_operands",
        [
            jax.ShapeDtypeStruct((1,), jnp.int32),
            info_shape,
            flat_shape,
            gate_shape,
            send_shape,
        ],
        [SMEM, HBM, HBM, HBM, HBM, HBM, HBM, HBM],
        (me, ids, crops, ln_in_gain, ln_out_gain, w_proj, w_gate, pair_rep),
        out_specs=[
            SMEM,
            whole(info_shape),
            whole(flat_shape),
            whole(gate_shape),
            whole(send_shape),
        ],
        scratch=[
            pltpu.VMEM(ids.shape, jnp.int32),
            pltpu.VMEM(crops.shape, jnp.int32),
            pltpu.VMEM(ln_in_gain.shape, F32),
            pltpu.VMEM(ln_out_gain.shape, F32),
            pltpu.VMEM(w_proj.shape[1:], BF16),
            pltpu.VMEM(w_gate.shape[1:], BF16),
            pltpu.VMEM(pair_rep.shape, BF16),
            pltpu.VMEM((w_proj.shape[2], depth), BF16),
            pltpu.SemaphoreType.DMA((7,)),
        ],
    )
    return lax.switch(
        choice[0],
        [functools.partial(kept_columns, some) for some in widths],
        pair_rep,
        info,
        flat,
        gate,
        sent,
        w_proj,
        w_gate,
        w_out,
    )


GROUPS = 2
SHARES = (11, 12, 13, 14, 16)


def solution(mesh):
    devices = mesh.shape["dap"]
    placed = (P("dap", "grp", None), P(), P(), P(), P(), P(), P(), P())

    def body(*arrays):
        rows, count, width = arrays[0].shape
        hidden = arrays[-1].shape[1]
        plain = (
            mesh.shape["grp"] == 1
            and rows * devices == count
            and count == 256
            and rows == 8
            and hidden == 4 * devices
        )
        return (row_shards if plain else shards)(*arrays)

    return jax.shard_map(
        body, mesh=mesh, in_specs=placed, out_specs=P("dap", "grp", None), check_vma=False
    )
```

```python
import functools

import jax
import jax.numpy as jnp
from jax import lax
from jax.experimental import pallas as pl
from jax.experimental.pallas import tpu as pltpu
from jax.sharding import PartitionSpec as P

epsilon_norm = 1e-05
F32 = jnp.float32
BF16 = jnp.bfloat16


def residue_valid(chain_ids, crop_lengths):
    count = chain_ids.shape[0]
    chains = jnp.arange(crop_lengths.shape[0], dtype=jnp.int32)
    member = (chain_ids[:, None] == chains[None, :]).astype(jnp.int32)
    counts = jnp.sum(member, axis=0)
    starts = jnp.cumsum(counts) - counts
    first = jnp.sum(member * starts[None, :], axis=1)
    limit = jnp.sum(member * crop_lengths[None, :], axis=1)
    place = jnp.arange(count, dtype=jnp.int32) - first
    return (place < limit).astype(jnp.float32)


def layer_norm(values, gain, axis):
    centre = jnp.mean(values, axis=axis, keepdims=True)
    spread = jnp.mean((values - centre) ** 2, axis=axis, keepdims=True)
    return (values - centre) * lax.rsqrt(spread + epsilon_norm) * gain


def column_rows(right_chan):
    return lax.all_to_all(right_chan, "grp", split_axis=1, concat_axis=2, tiled=True)


def update(pair_tile, pair_mask, ln_in, w_proj, w_gate, ln_out, w_out, outgoing):
    hidden = w_out.shape[0]
    normed = layer_norm(pair_tile.astype(jnp.float32), ln_in, 2).astype(jnp.bfloat16)
    projected = jnp.einsum("rqc,cf->frq", normed, w_proj, preferred_element_type=jnp.float32)
    gate_value = jax.nn.sigmoid(
        jnp.einsum("rqc,cd->rqd", normed, w_gate, preferred_element_type=jnp.float32)
    )
    left_op = (
        jax.nn.sigmoid(projected[:hidden]) * projected[hidden : 2 * hidden] * pair_mask
    ).astype(jnp.bfloat16)
    right_op = (
        jax.nn.sigmoid(projected[2 * hidden : 3 * hidden]) * projected[3 * hidden :] * pair_mask
    ).astype(jnp.bfloat16)
    left_chan, right_chan = (
        lax.all_to_all(left_op, "dap", split_axis=0, concat_axis=1, tiled=True),
        lax.all_to_all(right_op, "dap", split_axis=0, concat_axis=1, tiled=True),
    )
    if outgoing:
        right_rows = column_rows(right_chan)
        triangle = jnp.einsum(
            "hik,hjk->hij",
            lax.all_gather(left_chan, "grp", axis=2, tiled=True),
            right_rows,
            preferred_element_type=jnp.float32,
        )
    else:
        triangle = jnp.einsum(
            "hki,hkj->hij",
            lax.all_gather(left_chan, "grp", axis=2, tiled=True),
            right_chan,
            preferred_element_type=jnp.float32,
        )
    returned = lax.all_to_all(
        triangle.astype(jnp.bfloat16), "dap", split_axis=1, concat_axis=0, tiled=True
    )
    normed_product = layer_norm(returned.astype(jnp.float32), ln_out[:, None, None], 0).astype(
        jnp.bfloat16
    )
    update_term = jnp.einsum(
        "hrq,hd->rqd", normed_product, w_out, preferred_element_type=jnp.float32
    )
    return (pair_tile.astype(jnp.float32) + gate_value * update_term).astype(jnp.bfloat16)


def shards(pair_rep, chain_ids, crop_lengths, ln_in_gain, w_proj, w_gate, ln_out_gain, w_out):
    row_count = pair_rep.shape[0]
    column_count = pair_rep.shape[1]
    kept = residue_valid(chain_ids, crop_lengths)
    row_start = lax.axis_index("dap") * row_count
    column_start = lax.axis_index("grp") * column_count
    kept_rows = lax.dynamic_slice_in_dim(kept, row_start, row_count, 0)
    kept_columns = lax.dynamic_slice_in_dim(kept, column_start, column_count, 0)
    pair_mask = kept_rows[:, None] * kept_columns[None, :]
    pair_tile = pair_rep
    for layer_index, outgoing in ((0, True), (1, False)):
        pair_tile = update(
            pair_tile,
            pair_mask,
            ln_in_gain[layer_index],
            w_proj[layer_index],
            w_gate[layer_index],
            ln_out_gain[layer_index],
            w_out[layer_index],
            outgoing,
        )
    return pair_tile


def dot_nn(a, b):
    return lax.dot_general(a, b, (((1,), (0,)), ((), ())), preferred_element_type=F32)


def dot_nt(a, b):
    return lax.dot_general(a, b, (((1,), (1,)), ((), ())), preferred_element_type=F32)


def dot_tn(a, b):
    return lax.dot_general(a, b, (((0,), (0,)), ((), ())), preferred_element_type=F32)


def open_gate(half):
    return jnp.tanh(half) + 1.0


def halved(weights):
    return (weights.astype(F32) * 0.5).astype(BF16)


def one_hot(source, columns):
    place = lax.broadcasted_iota(jnp.int32, (source.shape[0], columns), 1)
    return jnp.where(place == source, 1.0, 0.0).astype(BF16)


def interleave(outer, inner):
    row = lax.broadcasted_iota(jnp.int32, (outer * inner, 1), 0)
    return one_hot((row % inner) * outer + row // inner, outer * inner)


def move(matrix, rows):
    return dot_nn(matrix, rows).astype(BF16)


def selection(slots, width):
    row = lax.broadcasted_iota(jnp.int32, (width, slots.shape[1]), 0).astype(F32)
    return jnp.where(row == slots, 1.0, 0.0).astype(BF16)


def kept_residues(ids, limits):
    place = lax.broadcasted_iota(jnp.int32, ids.shape, 1).astype(F32)
    kept = jnp.zeros(ids.shape, F32)
    for chain in range(limits.shape[1]):
        first = jnp.sum(jnp.where(ids < chain, 1.0, 0.0), axis=1, keepdims=True)
        limit = limits[:, chain : chain + 1].astype(F32)
        inside = jnp.where(ids == chain, 1.0, 0.0) * jnp.where(place - first < limit, 1.0, 0.0)
        kept = kept + inside
    return kept


def norm_rows(values, gain):
    centre = jnp.mean(values, axis=1, keepdims=True)
    apart = values - centre
    spread = jnp.mean(apart * apart, axis=1, keepdims=True)
    return (apart * lax.rsqrt(spread + epsilon_norm) * gain).astype(BF16)


def sort_projection(w_proj_ref, devices, sorted_ref):
    hidden = w_proj_ref.shape[1] // 4
    own = hidden // devices
    row = lax.broadcasted_iota(jnp.int32, (2 * hidden, 1), 0)
    side = (row % (2 * own)) // own
    order = one_hot(side * hidden + row // (2 * own) * own + row % own, 2 * hidden)
    for kind in range(2):
        sides = [
            w_proj_ref[:, block * hidden : (block + 1) * hidden] for block in (kind, kind + 2)
        ]
        rows = dot_nt(order, jnp.concatenate(sides, axis=1)) * 0.5
        sorted_ref[2 * hidden * kind : 2 * hidden * (kind + 1)] = rows.astype(BF16)


def project(flat, gain, weights, w_gate, info_ref, gate_ref, send_ref, rows, width, start):
    span = flat.shape[0]
    half = weights.shape[0] // 2
    place = start + lax.broadcasted_iota(jnp.int32, (1, span), 1)
    mask = jnp.zeros((1, span), F32)
    for row in range(rows):
        inside = jnp.where(place >= row * width, 1.0, 0.0)
        inside = inside * jnp.where(place < (row + 1) * width, 1.0, 0.0)
        mask = mask + inside * info_ref[ROWS + row : ROWS + row + 1, 0:1]
    normed = norm_rows(flat, gain)
    gate_ref[start : start + span] = open_gate(dot_nn(normed, w_gate))
    projected = dot_nt(weights, normed)
    operand = open_gate(projected[:half]) * projected[half:] * mask
    shape = send_ref.shape[:2] + (span,)
    send_ref[:, :, start : start + span] = operand.astype(BF16).reshape(shape)


def spans(total):
    start = 0
    while start < total:
        span = min(256, total - start)
        yield start, span
        start += span


ROWS = 8


def first_kernel(
    devices,
    widths,
    me_ref,
    ids_hbm,
    crop_hbm,
    ln_in_hbm,
    w_proj_hbm,
    w_gate_hbm,
    pair_hbm,
    choice_ref,
    info_ref,
    flat_ref,
    gate_ref,
    send_ref,
    ids_ref,
    crop_ref,
    ln_in_ref,
    w_proj_ref,
    w_gate_ref,
    pair_ref,
    weights_ref,
    arrived,
):
    moves = (
        (ids_hbm, ids_ref),
        (crop_hbm, crop_ref),
        (ln_in_hbm, ln_in_ref),
        (w_proj_hbm.at[0], w_proj_ref),
        (pair_hbm, pair_ref),
        (w_gate_hbm.at[0], w_gate_ref),
    )
    copies = [
        pltpu.make_async_copy(source, target, arrived.at[index])
        for index, (source, target) in enumerate(moves)
    ]
    for copy in copies:
        copy.start()
    rows, count, depth = pair_ref.shape
    flat_ref[...] = jnp.zeros(flat_ref.shape, BF16)
    info_ref[...] = jnp.zeros(info_ref.shape, F32)
    for copy in copies[:3]:
        copy.wait()
    kept = kept_residues(ids_ref[...], crop_ref[...])
    total = jnp.sum(kept)
    choice = jnp.int32(0)
    for some in widths[:-1]:
        choice = choice + jnp.where(total > some, 1, 0).astype(jnp.int32)
    choice_ref[0] = choice
    width = jnp.int32(widths[0])
    for some, wider in zip(widths[:-1], widths[1:]):
        width = width + jnp.where(total > some, wider - some, 0).astype(jnp.int32)
    square = (count, count)
    up = lax.broadcasted_iota(jnp.int32, square, 0) < lax.broadcasted_iota(jnp.int32, square, 1)
    rank = dot_nn(
        jnp.broadcast_to(kept, (8, count)).astype(BF16), jnp.where(up, 1.0, 0.0).astype(BF16)
    )[0:1]
    slots = jnp.where(kept > 0.0, rank, -1.0)
    by_row = dot_nt(
        jnp.broadcast_to(slots, (8, count)).astype(BF16), interleave(rows, devices)
    )[0:1]
    info_ref[0:1] = slots
    info_ref[1:2] = by_row
    place = lax.broadcasted_iota(jnp.int32, kept.shape, 1)
    for row in range(rows):
        own = jnp.where(place == me_ref[0] * rows + row, kept, 0.0)
        info_ref[ROWS + row : ROWS + row + 1] = jnp.broadcast_to(
            jnp.sum(own, axis=1, keepdims=True), kept.shape
        )
    pick = selection(slots, count)
    copies[3].wait()
    sort_projection(w_proj_ref, devices, weights_ref)
    copies[4].wait()
    copies[5].wait()
    lanes = jnp.concatenate([pair_ref[row] for row in range(rows)], axis=1)
    packed = move(pick, lanes)
    for row in range(rows):
        start = pl.multiple_of(row * width, 16)
        flat_ref[pl.ds(start, count)] = packed[:, row * depth : (row + 1) * depth]
    gain = ln_in_ref[0:1]
    w_gate = halved(w_gate_ref[...])

    def operands(start, span):
        part = flat_ref[start : start + span].astype(F32)
        project(
            part,
            gain,
            weights_ref[...],
            w_gate,
            info_ref,
            gate_ref,
            send_ref,
            rows,
            width,
            start,
        )

    for start, span in spans(rows * count):
        if start < rows * widths[0]:
            operands(start, span)
        else:
            pl.when(start < rows * width)(functools.partial(operands, start, span))


def channel_blocks(came_ref, rows, width):
    devices, channels, total = came_ref.shape
    came = move(
        interleave(channels, devices), came_ref[...].reshape(devices * channels, total)
    )
    blocks = []
    for channel in range(channels):
        span = slice(channel * devices, (channel + 1) * devices)
        parts = [came[span, row * width : (row + 1) * width] for row in range(rows)]
        blocks.append(jnp.concatenate(parts, axis=0))
    return blocks


def outgoing_kernel(rows, groups, info_ref, came_ref, w_proj_ref, send_ref, sorted_ref):
    devices, both, total = came_ref.shape
    own = both // 2
    width = total // rows
    pick = selection(info_ref[1:2], width)
    blocks = channel_blocks(came_ref, rows, width)
    products = [
        dot_nt(blocks[channel], move(pick, blocks[own + channel])).astype(BF16)
        for channel in range(own)
    ]
    low = rows * own // 8
    to_device = interleave(devices, 8)
    for offset in range(low):
        parts = []
        for channel in range(own):
            for high in range(rows // low):
                row = high * low + offset
                parts.append(products[channel][row * devices : (row + 1) * devices])
        sent = move(to_device, jnp.concatenate(parts, axis=0))
        send_ref[:, :, offset * width : (offset + 1) * width] = sent.reshape(devices, 8, width)
    sort_projection(w_proj_ref.at[1], devices // groups, sorted_ref)


def incoming_kernel(rows, info_ref, came_ref, send_ref):
    own = came_ref.shape[1] // 2
    devices = send_ref.shape[0]
    width = came_ref.shape[2] // rows
    pick = selection(info_ref[1:2], width)
    pick = dot_nt(interleave(1, rows * devices), pick).astype(BF16)
    blocks = channel_blocks(came_ref, rows, width)
    products = [
        move(pick, dot_tn(blocks[channel], blocks[own + channel]).astype(BF16))
        for channel in range(own)
    ]
    to_device = interleave(devices, own)
    for row in range(rows):
        span = slice(row * devices, (row + 1) * devices)
        sent = move(to_device, jnp.concatenate([product[span] for product in products], axis=0))
        send_ref[:, :, row * width : (row + 1) * width] = sent.reshape(devices, own, width)


def finish_parts(layer, groups, came_ref, flat_ref, gate_ref, ln_out_ref, w_out_ref, use):
    devices, eight, lanes = came_ref.shape
    hidden = w_out_ref.shape[1]
    high = devices * eight // hidden // groups
    square = lax.broadcasted_iota(jnp.int32, (hidden, hidden), 0) == lax.broadcasted_iota(
        jnp.int32, (hidden, hidden), 1
    )
    gain = ln_out_ref[layer : layer + 1]
    gain = jnp.sum(jnp.where(square, gain, 0.0), axis=1, keepdims=True)
    w_out = halved(w_out_ref[layer])
    for offset, span in spans(lanes):
        came = came_ref[:, :, offset : offset + span].reshape(devices * eight, span)
        if groups == 1:
            came = dot_nn(interleave(high, hidden), came)
        else:
            came = came.astype(F32)
            came = sum(came[hidden * group : hidden * (group + 1)] for group in range(groups))
        for part in range(high):
            block = came[part * hidden : (part + 1) * hidden]
            centre = jnp.mean(block, axis=0, keepdims=True)
            apart = block - centre
            spread = jnp.mean(apart * apart, axis=0, keepdims=True)
            normed = (apart * lax.rsqrt(spread + epsilon_norm) * gain).astype(BF16)
            term = dot_tn(normed, w_out)
            start = part * lanes + offset
            here = slice(start, start + span)
            use(start, (flat_ref[here].astype(F32) + gate_ref[here] * term).astype(BF16))


def middle_kernel(
    rows,
    info_ref,
    came_ref,
    flat_ref,
    gate_ref,
    ln_out_ref,
    w_out_ref,
    ln_in_ref,
    weights_ref,
    w_gate_ref,
    next_ref,
    next_gate_ref,
    send_ref,
):
    gain = ln_in_ref[1:2]
    width = next_ref.shape[0] // rows

    def use(start, fresh):
        next_ref[start : start + fresh.shape[0]] = fresh

    finish_parts(0, 1, came_ref, flat_ref, gate_ref, ln_out_ref, w_out_ref, use)
    w_gate = halved(w_gate_ref[1])
    for start, span in spans(rows * width):
        project(
            next_ref[start : start + span].astype(F32),
            gain,
            weights_ref[...],
            w_gate,
            info_ref,
            next_gate_ref,
            send_ref,
            rows,
            width,
            start,
        )


def last_kernel(
    groups,
    info_ref,
    ids_hbm,
    crop_hbm,
    pair_ref,
    came_ref,
    flat_ref,
    gate_ref,
    ln_out_ref,
    w_out_ref,
    out_ref,
    next_ref,
):
    rows, count, depth = out_ref.shape
    width = flat_ref.shape[0] // rows

    def use(start, fresh):
        next_ref[start : start + fresh.shape[0]] = fresh

    finish_parts(1, groups, came_ref, flat_ref, gate_ref, ln_out_ref, w_out_ref, use)
    pick = selection(info_ref[0:1], width)
    pick = dot_nt(interleave(1, count), pick).astype(BF16)
    lanes = [next_ref[row * width : (row + 1) * width] for row in range(rows)]
    lanes.append(jnp.ones((width, depth), BF16))
    spread = dot_nn(pick, jnp.concatenate(lanes, axis=1))
    kept = spread[:, rows * depth :] > 0.5
    for row in range(rows):
        fresh = spread[:, row * depth : (row + 1) * depth]
        out_ref[row] = jnp.where(kept, fresh, pair_ref[row].astype(F32)).astype(BF16)


SMEM = pl.BlockSpec(memory_space=pltpu.SMEM)
HBM = pl.BlockSpec(memory_space=pltpu.HBM)


VMEM = pl.BlockSpec(memory_space=pltpu.VMEM)


def call(body, name, outs, operands, specs=None, out_specs=None, scratch=()):
    return pl.pallas_call(
        body,
        out_shape=list(outs),
        in_specs=specs or [VMEM] * len(operands),
        out_specs=out_specs or [VMEM] * len(outs),
        scratch_shapes=list(scratch),
        compiler_params=pltpu.CompilerParams(vmem_limit_bytes=24 * 1024 * 1024),
        name=name,
    )(*operands)


def kept_columns(
    width, pair_rep, ids, crops, info, flat, gate, sent, ln_in, w_proj, w_gate, ln_out, w_out
):
    devices = lax.axis_size("dap")
    rows, _, depth = pair_rep.shape
    hidden = w_out.shape[1]
    own = hidden // devices
    back_shape = jax.ShapeDtypeStruct((devices, 8, rows * own * width // 8), BF16)
    flat_shape = jax.ShapeDtypeStruct((rows * width, depth), BF16)
    gate_shape = jax.ShapeDtypeStruct((rows * width, depth), F32)
    sorted_shape = jax.ShapeDtypeStruct((4 * hidden, depth), BF16)

    apart = devices // GROUPS
    groups = [list(range(first, first + apart)) for first in range(0, devices, apart)]
    group_shape = jax.ShapeDtypeStruct((apart, 2 * own * GROUPS, rows * width), BF16)
    sums_shape = jax.ShapeDtypeStruct((devices, own * GROUPS, rows * width), BF16)

    def exchange(sent, within=None):
        return lax.all_to_all(
            sent, "dap", split_axis=0, concat_axis=0, axis_index_groups=within, tiled=True
        )

    sent = sent[:, :, : rows * width]
    came = exchange(sent)
    sent, weights = call(
        functools.partial(outgoing_kernel, rows, GROUPS),
        "outgoing",
        [back_shape, sorted_shape],
        (info, came, w_proj),
    )
    came = exchange(sent)
    flat, gate, sent = call(
        functools.partial(middle_kernel, rows),
        "finish_and_operands",
        [flat_shape, gate_shape, group_shape],
        (info, came, flat, gate, ln_out, w_out, ln_in, weights, w_gate),
    )
    came = exchange(sent, groups)
    sent = call(
        functools.partial(incoming_kernel, rows),
        "incoming",
        [sums_shape],
        (info, came),
    )[0]
    came = exchange(sent)
    return call(
        functools.partial(last_kernel, GROUPS),
        "finish",
        [jax.ShapeDtypeStruct(pair_rep.shape, BF16)],
        (info, ids, crops, pair_rep, came, flat, gate, ln_out, w_out),
        specs=[VMEM, HBM, HBM] + [VMEM] * 6,
        scratch=[pltpu.VMEM(flat_shape.shape, BF16)],
    )[0]


def row_shards(pair_rep, chain_ids, crop_lengths, ln_in_gain, w_proj, w_gate, ln_out_gain, w_out):
    devices = lax.axis_size("dap")
    rows, count, depth = pair_rep.shape
    me = lax.axis_index("dap").reshape(1).astype(jnp.int32)
    ids = chain_ids.reshape(1, count)
    crops = crop_lengths.reshape(1, -1)
    widths = [count * share // 16 for share in SHARES]
    info_shape = jax.ShapeDtypeStruct((16, count), F32)
    flat_shape = jax.ShapeDtypeStruct((rows * count, depth), BF16)
    send_shape = jax.ShapeDtypeStruct((devices, w_proj.shape[2] // devices // 2, rows * count), BF16)
    gate_shape = jax.ShapeDtypeStruct(flat_shape.shape, F32)
    choice, info, flat, gate, sent = call(
        functools.partial(first_kernel, devices, widths),
        "first_operands",
        [
            jax.ShapeDtypeStruct((1,), jnp.int32),
            info_shape,
            flat_shape,
            gate_shape,
            send_shape,
        ],
        (me, ids, crops, ln_in_gain, w_proj, w_gate, pair_rep),
        specs=[SMEM] + [HBM] * 6,
        out_specs=[SMEM] + [VMEM] * 4,
        scratch=[
            pltpu.VMEM(ids.shape, jnp.int32),
            pltpu.VMEM(crops.shape, jnp.int32),
            pltpu.VMEM(ln_in_gain.shape, F32),
            pltpu.VMEM(w_proj.shape[1:], BF16),
            pltpu.VMEM(w_gate.shape[1:], BF16),
            pltpu.VMEM(pair_rep.shape, BF16),
            pltpu.VMEM((w_proj.shape[2], depth), BF16),
            pltpu.SemaphoreType.DMA((6,)),
        ],
    )
    return lax.switch(
        choice[0],
        [functools.partial(kept_columns, some) for some in widths],
        pair_rep,
        ids,
        crops,
        info,
        flat,
        gate,
        sent,
        ln_in_gain,
        w_proj,
        w_gate,
        ln_out_gain,
        w_out,
    )


GROUPS = 2
SHARES = (11, 12, 13, 14, 16)


def solution(mesh):
    devices = mesh.shape["dap"]
    placed = (P("dap", "grp", None), P(), P(), P(), P(), P(), P(), P())

    def body(*arrays):
        rows, count, width = arrays[0].shape
        hidden = arrays[-1].shape[1]
        plain = (
            mesh.shape["grp"] == 1
            and rows * devices == count
            and count == 256
            and rows == 8
            and hidden == 4 * devices
        )
        return (row_shards if plain else shards)(*arrays)

    return jax.shard_map(
        body, mesh=mesh, in_specs=placed, out_specs=P("dap", "grp", None), check_vma=False
    )
```

```python
import functools

import jax
import jax.numpy as jnp
from jax import lax
from jax.experimental import pallas as pl
from jax.experimental.pallas import tpu as pltpu
from jax.sharding import PartitionSpec as P

epsilon_norm = 1e-05
F32 = jnp.float32
BF16 = jnp.bfloat16


def residue_valid(chain_ids, crop_lengths):
    count = chain_ids.shape[0]
    chains = jnp.arange(crop_lengths.shape[0], dtype=jnp.int32)
    member = (chain_ids[:, None] == chains[None, :]).astype(jnp.int32)
    counts = jnp.sum(member, axis=0)
    starts = jnp.cumsum(counts) - counts
    first = jnp.sum(member * starts[None, :], axis=1)
    limit = jnp.sum(member * crop_lengths[None, :], axis=1)
    place = jnp.arange(count, dtype=jnp.int32) - first
    return (place < limit).astype(jnp.float32)


def layer_norm(values, gain, axis):
    centre = jnp.mean(values, axis=axis, keepdims=True)
    spread = jnp.mean((values - centre) ** 2, axis=axis, keepdims=True)
    return (values - centre) * lax.rsqrt(spread + epsilon_norm) * gain


def column_rows(right_chan):
    return lax.all_to_all(right_chan, "grp", split_axis=1, concat_axis=2, tiled=True)


def update(pair_tile, pair_mask, ln_in, w_proj, w_gate, ln_out, w_out, outgoing):
    hidden = w_out.shape[0]
    normed = layer_norm(pair_tile.astype(jnp.float32), ln_in, 2).astype(jnp.bfloat16)
    projected = jnp.einsum("rqc,cf->frq", normed, w_proj, preferred_element_type=jnp.float32)
    gate_value = jax.nn.sigmoid(
        jnp.einsum("rqc,cd->rqd", normed, w_gate, preferred_element_type=jnp.float32)
    )
    left_op = (
        jax.nn.sigmoid(projected[:hidden]) * projected[hidden : 2 * hidden] * pair_mask
    ).astype(jnp.bfloat16)
    right_op = (
        jax.nn.sigmoid(projected[2 * hidden : 3 * hidden]) * projected[3 * hidden :] * pair_mask
    ).astype(jnp.bfloat16)
    left_chan, right_chan = (
        lax.all_to_all(left_op, "dap", split_axis=0, concat_axis=1, tiled=True),
        lax.all_to_all(right_op, "dap", split_axis=0, concat_axis=1, tiled=True),
    )
    if outgoing:
        right_rows = column_rows(right_chan)
        triangle = jnp.einsum(
            "hik,hjk->hij",
            lax.all_gather(left_chan, "grp", axis=2, tiled=True),
            right_rows,
            preferred_element_type=jnp.float32,
        )
    else:
        triangle = jnp.einsum(
            "hki,hkj->hij",
            lax.all_gather(left_chan, "grp", axis=2, tiled=True),
            right_chan,
            preferred_element_type=jnp.float32,
        )
    returned = lax.all_to_all(
        triangle.astype(jnp.bfloat16), "dap", split_axis=1, concat_axis=0, tiled=True
    )
    normed_product = layer_norm(returned.astype(jnp.float32), ln_out[:, None, None], 0).astype(
        jnp.bfloat16
    )
    update_term = jnp.einsum(
        "hrq,hd->rqd", normed_product, w_out, preferred_element_type=jnp.float32
    )
    return (pair_tile.astype(jnp.float32) + gate_value * update_term).astype(jnp.bfloat16)


def shards(pair_rep, chain_ids, crop_lengths, ln_in_gain, w_proj, w_gate, ln_out_gain, w_out):
    row_count = pair_rep.shape[0]
    column_count = pair_rep.shape[1]
    kept = residue_valid(chain_ids, crop_lengths)
    row_start = lax.axis_index("dap") * row_count
    column_start = lax.axis_index("grp") * column_count
    kept_rows = lax.dynamic_slice_in_dim(kept, row_start, row_count, 0)
    kept_columns = lax.dynamic_slice_in_dim(kept, column_start, column_count, 0)
    pair_mask = kept_rows[:, None] * kept_columns[None, :]
    pair_tile = pair_rep
    for layer_index, outgoing in ((0, True), (1, False)):
        pair_tile = update(
            pair_tile,
            pair_mask,
            ln_in_gain[layer_index],
            w_proj[layer_index],
            w_gate[layer_index],
            ln_out_gain[layer_index],
            w_out[layer_index],
            outgoing,
        )
    return pair_tile


def dot_nn(a, b):
    return lax.dot_general(a, b, (((1,), (0,)), ((), ())), preferred_element_type=F32)


def dot_nt(a, b):
    return lax.dot_general(a, b, (((1,), (1,)), ((), ())), preferred_element_type=F32)


def dot_tn(a, b):
    return lax.dot_general(a, b, (((0,), (0,)), ((), ())), preferred_element_type=F32)


def open_gate(half):
    return jnp.tanh(half) + 1.0


def halved(weights):
    return (weights.astype(F32) * 0.5).astype(BF16)


def one_hot(source, columns):
    place = lax.broadcasted_iota(jnp.int32, (source.shape[0], columns), 1)
    return jnp.where(place == source, 1.0, 0.0).astype(BF16)


def interleave(outer, inner):
    row = lax.broadcasted_iota(jnp.int32, (outer * inner, 1), 0)
    return one_hot((row % inner) * outer + row // inner, outer * inner)


def move(matrix, rows):
    return dot_nn(matrix, rows).astype(BF16)


def selection(slots, width):
    row = lax.broadcasted_iota(jnp.int32, (width, slots.shape[1]), 0).astype(F32)
    return jnp.where(row == slots, 1.0, 0.0).astype(BF16)


def kept_residues(ids, limits):
    place = lax.broadcasted_iota(jnp.int32, ids.shape, 1).astype(F32)
    kept = jnp.zeros(ids.shape, F32)
    for chain in range(limits.shape[1]):
        first = jnp.sum(jnp.where(ids < chain, 1.0, 0.0), axis=1, keepdims=True)
        limit = limits[:, chain : chain + 1].astype(F32)
        inside = jnp.where(ids == chain, 1.0, 0.0) * jnp.where(place - first < limit, 1.0, 0.0)
        kept = kept + inside
    return kept


def norm_rows(values, gain):
    centre = jnp.mean(values, axis=1, keepdims=True)
    apart = values - centre
    spread = jnp.mean(apart * apart, axis=1, keepdims=True)
    return (apart * lax.rsqrt(spread + epsilon_norm) * gain).astype(BF16)


def sort_projection(w_proj_ref, devices, sorted_ref):
    hidden = w_proj_ref.shape[1] // 4
    own = hidden // devices
    row = lax.broadcasted_iota(jnp.int32, (2 * hidden, 1), 0)
    side = (row % (2 * own)) // own
    order = one_hot(side * hidden + row // (2 * own) * own + row % own, 2 * hidden)
    for kind in range(2):
        sides = [
            w_proj_ref[:, block * hidden : (block + 1) * hidden] for block in (kind, kind + 2)
        ]
        rows = dot_nt(order, jnp.concatenate(sides, axis=1)) * 0.5
        sorted_ref[2 * hidden * kind : 2 * hidden * (kind + 1)] = rows.astype(BF16)


def project(normed, weights, w_gate, info_ref, gate_ref, send_ref, rows, width, start):
    span = normed.shape[0]
    half = weights.shape[0] // 2
    place = start + lax.broadcasted_iota(jnp.int32, (1, span), 1)
    mask = jnp.zeros((1, span), F32)
    for row in range(rows):
        inside = jnp.where(place >= row * width, 1.0, 0.0)
        inside = inside * jnp.where(place < (row + 1) * width, 1.0, 0.0)
        mask = mask + inside * info_ref[ROWS + row : ROWS + row + 1, 0:1]
    gate_ref[start : start + span] = open_gate(dot_nn(normed, w_gate))
    projected = dot_nt(weights, normed)
    operand = open_gate(projected[:half]) * projected[half:] * mask
    shape = send_ref.shape[:2] + (span,)
    send_ref[:, :, start : start + span] = operand.astype(BF16).reshape(shape)


def spans(total):
    start = 0
    while start < total:
        span = min(256, total - start)
        yield start, span
        start += span


LN_IN, LN_OUT, ROWS = 2, 4, 8


def gain_of(info_ref, row, width):
    return info_ref[row : row + 1, :width]


def first_kernel(
    devices,
    widths,
    me_ref,
    ids_hbm,
    crop_hbm,
    ln_in_hbm,
    ln_out_hbm,
    w_proj_hbm,
    w_gate_hbm,
    pair_hbm,
    choice_ref,
    info_ref,
    flat_ref,
    gate_ref,
    send_ref,
    ids_ref,
    crop_ref,
    ln_in_ref,
    ln_out_ref,
    w_proj_ref,
    w_gate_ref,
    pair_ref,
    normed_ref,
    weights_ref,
    arrived,
):
    moves = (
        (pair_hbm, pair_ref),
        (w_proj_hbm.at[0], w_proj_ref),
        (ids_hbm, ids_ref),
        (crop_hbm, crop_ref),
        (ln_in_hbm, ln_in_ref),
        (ln_out_hbm, ln_out_ref),
        (w_gate_hbm.at[0], w_gate_ref),
    )
    copies = [
        pltpu.make_async_copy(source, target, arrived.at[index])
        for index, (source, target) in enumerate(moves)
    ]
    for copy in copies:
        copy.start()
    rows, count, depth = pair_ref.shape
    flat_ref[...] = jnp.zeros(flat_ref.shape, BF16)
    normed_ref[...] = jnp.zeros(normed_ref.shape, BF16)
    info_ref[...] = jnp.zeros(info_ref.shape, F32)
    square = (count, count)
    up = lax.broadcasted_iota(jnp.int32, square, 0) < lax.broadcasted_iota(jnp.int32, square, 1)
    up = jnp.where(up, 1.0, 0.0).astype(BF16)
    for copy in copies:
        copy.wait()
    kept = kept_residues(ids_ref[...], crop_ref[...])
    total = jnp.sum(kept)
    choice = jnp.int32(0)
    width = jnp.int32(widths[0])
    for some, wider in zip(widths[:-1], widths[1:]):
        choice = choice + jnp.where(total > some, 1, 0).astype(jnp.int32)
        width = width + jnp.where(total > some, wider - some, 0).astype(jnp.int32)
    choice_ref[0] = choice
    rank = dot_nn(jnp.broadcast_to(kept, (8, count)).astype(BF16), up)[0:1]
    slots = jnp.where(kept > 0.0, rank, -1.0)
    pick = selection(slots, count)
    gain = ln_in_ref[0:1]
    lanes = [pair_ref[row] for row in range(rows)]
    lanes = lanes + [norm_rows(part.astype(F32), gain) for part in lanes]
    sort_projection(w_proj_ref, devices, weights_ref)
    packed = move(pick, jnp.concatenate(lanes, axis=1))
    for row in range(rows):
        here = pl.ds(pl.multiple_of(row * width, 16), count)
        flat_ref[here] = packed[:, row * depth : (row + 1) * depth]
        normed_ref[here] = packed[:, (rows + row) * depth : (rows + row + 1) * depth]
    place = lax.broadcasted_iota(jnp.int32, kept.shape, 1)
    for row in range(rows):
        own = jnp.where(place == me_ref[0] * rows + row, kept, 0.0)
        info_ref[ROWS + row : ROWS + row + 1] = jnp.broadcast_to(
            jnp.sum(own, axis=1, keepdims=True), kept.shape
        )
    info_ref[0:1] = slots
    info_ref[1:2] = dot_nt(
        jnp.broadcast_to(slots, (8, count)).astype(BF16), interleave(rows, devices)
    )[0:1]
    info_ref[LN_IN : LN_IN + 2, :depth] = ln_in_ref[...]
    info_ref[LN_OUT : LN_OUT + 2, : ln_out_ref.shape[1]] = ln_out_ref[...]
    w_gate = halved(w_gate_ref[...])
    for start, span in spans(rows * count):
        project(
            normed_ref[start : start + span],
            weights_ref[...],
            w_gate,
            info_ref,
            gate_ref,
            send_ref,
            rows,
            width,
            start,
        )


def channel_blocks(came_ref, rows, width):
    devices, channels, total = came_ref.shape
    came = move(
        interleave(channels, devices), came_ref[...].reshape(devices * channels, total)
    )
    blocks = []
    for channel in range(channels):
        span = slice(channel * devices, (channel + 1) * devices)
        parts = [came[span, row * width : (row + 1) * width] for row in range(rows)]
        blocks.append(jnp.concatenate(parts, axis=0))
    return blocks


def outgoing_kernel(rows, groups, info_ref, came_ref, w_proj_ref, send_ref, sorted_ref):
    devices, both, total = came_ref.shape
    own = both // 2
    width = total // rows
    pick = selection(info_ref[1:2], width)
    blocks = channel_blocks(came_ref, rows, width)
    products = [
        dot_nt(blocks[channel], move(pick, blocks[own + channel])).astype(BF16)
        for channel in range(own)
    ]
    low = rows * own // 8
    to_device = interleave(devices, 8)
    for offset in range(low):
        parts = []
        for channel in range(own):
            for high in range(rows // low):
                row = high * low + offset
                parts.append(products[channel][row * devices : (row + 1) * devices])
        sent = move(to_device, jnp.concatenate(parts, axis=0))
        send_ref[:, :, offset * width : (offset + 1) * width] = sent.reshape(devices, 8, width)
    sort_projection(w_proj_ref.at[1], devices // groups, sorted_ref)


def incoming_kernel(rows, info_ref, came_ref, send_ref):
    own = came_ref.shape[1] // 2
    devices = send_ref.shape[0]
    width = came_ref.shape[2] // rows
    pick = selection(info_ref[1:2], width)
    pick = dot_nt(interleave(1, rows * devices), pick).astype(BF16)
    blocks = channel_blocks(came_ref, rows, width)
    products = [
        move(pick, dot_tn(blocks[channel], blocks[own + channel]).astype(BF16))
        for channel in range(own)
    ]
    to_device = interleave(devices, own)
    for row in range(rows):
        span = slice(row * devices, (row + 1) * devices)
        sent = move(to_device, jnp.concatenate([product[span] for product in products], axis=0))
        send_ref[:, :, row * width : (row + 1) * width] = sent.reshape(devices, own, width)


def finish_parts(layer, groups, info_ref, came_ref, flat_ref, gate_ref, w_out_ref, use):
    devices, eight, lanes = came_ref.shape
    hidden = w_out_ref.shape[1]
    high = devices * eight // hidden // groups
    square = lax.broadcasted_iota(jnp.int32, (hidden, hidden), 0) == lax.broadcasted_iota(
        jnp.int32, (hidden, hidden), 1
    )
    gain = gain_of(info_ref, LN_OUT + layer, hidden)
    gain = jnp.sum(jnp.where(square, gain, 0.0), axis=1, keepdims=True)
    w_out = halved(w_out_ref[layer])
    for offset, span in spans(lanes):
        came = came_ref[:, :, offset : offset + span].reshape(devices * eight, span)
        if groups == 1:
            came = dot_nn(interleave(high, hidden), came)
        else:
            came = came.astype(F32)
            came = sum(came[hidden * group : hidden * (group + 1)] for group in range(groups))
        for part in range(high):
            block = came[part * hidden : (part + 1) * hidden]
            centre = jnp.mean(block, axis=0, keepdims=True)
            apart = block - centre
            spread = jnp.mean(apart * apart, axis=0, keepdims=True)
            normed = (apart * lax.rsqrt(spread + epsilon_norm) * gain).astype(BF16)
            term = dot_tn(normed, w_out)
            start = part * lanes + offset
            here = slice(start, start + span)
            use(start, (flat_ref[here].astype(F32) + gate_ref[here] * term).astype(BF16))


def middle_kernel(
    rows,
    info_ref,
    came_ref,
    flat_ref,
    gate_ref,
    w_out_ref,
    weights_ref,
    w_gate_ref,
    next_ref,
    next_gate_ref,
    send_ref,
):
    gain = gain_of(info_ref, LN_IN + 1, flat_ref.shape[1])
    width = next_ref.shape[0] // rows

    def use(start, fresh):
        next_ref[start : start + fresh.shape[0]] = fresh

    finish_parts(0, 1, info_ref, came_ref, flat_ref, gate_ref, w_out_ref, use)
    w_gate = halved(w_gate_ref[1])
    for start, span in spans(rows * width):
        project(
            norm_rows(next_ref[start : start + span].astype(F32), gain),
            weights_ref[...],
            w_gate,
            info_ref,
            next_gate_ref,
            send_ref,
            rows,
            width,
            start,
        )


def last_kernel(
    groups,
    info_ref,
    pair_ref,
    came_ref,
    flat_ref,
    gate_ref,
    w_out_ref,
    out_ref,
    next_ref,
):
    rows, count, depth = out_ref.shape
    width = flat_ref.shape[0] // rows

    def use(start, fresh):
        next_ref[start : start + fresh.shape[0]] = fresh

    finish_parts(1, groups, info_ref, came_ref, flat_ref, gate_ref, w_out_ref, use)
    pick = selection(info_ref[0:1], width)
    pick = dot_nt(interleave(1, count), pick).astype(BF16)
    lanes = [next_ref[row * width : (row + 1) * width] for row in range(rows)]
    lanes.append(jnp.ones((width, depth), BF16))
    spread = dot_nn(pick, jnp.concatenate(lanes, axis=1))
    kept = spread[:, rows * depth :] > 0.5
    for row in range(rows):
        fresh = spread[:, row * depth : (row + 1) * depth]
        out_ref[row] = jnp.where(kept, fresh, pair_ref[row].astype(F32)).astype(BF16)


SMEM = pl.BlockSpec(memory_space=pltpu.SMEM)
HBM = pl.BlockSpec(memory_space=pltpu.HBM)


VMEM = pl.BlockSpec(memory_space=pltpu.VMEM)


def call(body, name, outs, operands, specs=None, out_specs=None, scratch=()):
    return pl.pallas_call(
        body,
        out_shape=list(outs),
        in_specs=specs or [VMEM] * len(operands),
        out_specs=out_specs or [VMEM] * len(outs),
        scratch_shapes=list(scratch),
        compiler_params=pltpu.CompilerParams(vmem_limit_bytes=24 * 1024 * 1024),
        name=name,
    )(*operands)


def kept_columns(width, pair_rep, info, flat, gate, sent, w_proj, w_gate, w_out):
    devices = lax.axis_size("dap")
    rows, _, depth = pair_rep.shape
    hidden = w_out.shape[1]
    own = hidden // devices
    back_shape = jax.ShapeDtypeStruct((devices, 8, rows * own * width // 8), BF16)
    flat_shape = jax.ShapeDtypeStruct((rows * width, depth), BF16)
    gate_shape = jax.ShapeDtypeStruct((rows * width, depth), F32)
    sorted_shape = jax.ShapeDtypeStruct((4 * hidden, depth), BF16)

    apart = devices // GROUPS
    groups = [list(range(first, first + apart)) for first in range(0, devices, apart)]
    group_shape = jax.ShapeDtypeStruct((apart, 2 * own * GROUPS, rows * width), BF16)
    sums_shape = jax.ShapeDtypeStruct((devices, own * GROUPS, rows * width), BF16)

    def exchange(sent, within=None):
        return lax.all_to_all(
            sent, "dap", split_axis=0, concat_axis=0, axis_index_groups=within, tiled=True
        )

    sent = sent[:, :, : rows * width]
    came = exchange(sent)
    sent, weights = call(
        functools.partial(outgoing_kernel, rows, GROUPS),
        "outgoing",
        [back_shape, sorted_shape],
        (info, came, w_proj),
    )
    came = exchange(sent)
    flat, gate, sent = call(
        functools.partial(middle_kernel, rows),
        "finish_and_operands",
        [flat_shape, gate_shape, group_shape],
        (info, came, flat, gate, w_out, weights, w_gate),
    )
    came = exchange(sent, groups)
    sent = call(
        functools.partial(incoming_kernel, rows),
        "incoming",
        [sums_shape],
        (info, came),
    )[0]
    came = exchange(sent)
    return call(
        functools.partial(last_kernel, GROUPS),
        "finish",
        [jax.ShapeDtypeStruct(pair_rep.shape, BF16)],
        (info, pair_rep, came, flat, gate, w_out),
        scratch=[pltpu.VMEM(flat_shape.shape, BF16)],
    )[0]


def row_shards(pair_rep, chain_ids, crop_lengths, ln_in_gain, w_proj, w_gate, ln_out_gain, w_out):
    devices = lax.axis_size("dap")
    rows, count, depth = pair_rep.shape
    me = lax.axis_index("dap").reshape(1).astype(jnp.int32)
    ids = chain_ids.reshape(1, count)
    crops = crop_lengths.reshape(1, -1)
    widths = [count * share // 16 for share in SHARES]
    info_shape = jax.ShapeDtypeStruct((16, count), F32)
    flat_shape = jax.ShapeDtypeStruct((rows * count, depth), BF16)
    send_shape = jax.ShapeDtypeStruct((devices, w_proj.shape[2] // devices // 2, rows * count), BF16)
    gate_shape = jax.ShapeDtypeStruct(flat_shape.shape, F32)
    choice, info, flat, gate, sent = call(
        functools.partial(first_kernel, devices, widths),
        "first_operands",
        [
            jax.ShapeDtypeStruct((1,), jnp.int32),
            info_shape,
            flat_shape,
            gate_shape,
            send_shape,
        ],
        (me, ids, crops, ln_in_gain, ln_out_gain, w_proj, w_gate, pair_rep),
        specs=[SMEM] + [HBM] * 7,
        out_specs=[SMEM] + [VMEM] * 4,
        scratch=[
            pltpu.VMEM(ids.shape, jnp.int32),
            pltpu.VMEM(crops.shape, jnp.int32),
            pltpu.VMEM(ln_in_gain.shape, F32),
            pltpu.VMEM(ln_out_gain.shape, F32),
            pltpu.VMEM(w_proj.shape[1:], BF16),
            pltpu.VMEM(w_gate.shape[1:], BF16),
            pltpu.VMEM(pair_rep.shape, BF16),
            pltpu.VMEM(flat_shape.shape, BF16),
            pltpu.VMEM((w_proj.shape[2], depth), BF16),
            pltpu.SemaphoreType.DMA((7,)),
        ],
    )
    return lax.switch(
        choice[0],
        [functools.partial(kept_columns, some) for some in widths],
        pair_rep,
        info,
        flat,
        gate,
        sent,
        w_proj,
        w_gate,
        w_out,
    )


GROUPS = 2
SHARES = (11, 12, 13, 14, 16)


def solution(mesh):
    devices = mesh.shape["dap"]
    placed = (P("dap", "grp", None), P(), P(), P(), P(), P(), P(), P())

    def body(*arrays):
        rows, count, width = arrays[0].shape
        hidden = arrays[-1].shape[1]
        plain = (
            mesh.shape["grp"] == 1
            and rows * devices == count
            and count == 256
            and rows == 8
            and hidden == 4 * devices
        )
        return (row_shards if plain else shards)(*arrays)

    return jax.shard_map(
        body, mesh=mesh, in_specs=placed, out_specs=P("dap", "grp", None), check_vma=False
    )
```

```python
import functools

import jax
import jax.numpy as jnp
from jax import lax
from jax.experimental import pallas as pl
from jax.experimental.pallas import tpu as pltpu
from jax.sharding import PartitionSpec as P

epsilon_norm = 1e-05
F32 = jnp.float32
BF16 = jnp.bfloat16


def residue_valid(chain_ids, crop_lengths):
    count = chain_ids.shape[0]
    chains = jnp.arange(crop_lengths.shape[0], dtype=jnp.int32)
    member = (chain_ids[:, None] == chains[None, :]).astype(jnp.int32)
    counts = jnp.sum(member, axis=0)
    starts = jnp.cumsum(counts) - counts
    first = jnp.sum(member * starts[None, :], axis=1)
    limit = jnp.sum(member * crop_lengths[None, :], axis=1)
    place = jnp.arange(count, dtype=jnp.int32) - first
    return (place < limit).astype(jnp.float32)


def layer_norm(values, gain, axis):
    centre = jnp.mean(values, axis=axis, keepdims=True)
    spread = jnp.mean((values - centre) ** 2, axis=axis, keepdims=True)
    return (values - centre) * lax.rsqrt(spread + epsilon_norm) * gain


def column_rows(right_chan):
    return lax.all_to_all(right_chan, "grp", split_axis=1, concat_axis=2, tiled=True)


def update(pair_tile, pair_mask, ln_in, w_proj, w_gate, ln_out, w_out, outgoing):
    hidden = w_out.shape[0]
    normed = layer_norm(pair_tile.astype(jnp.float32), ln_in, 2).astype(jnp.bfloat16)
    projected = jnp.einsum("rqc,cf->frq", normed, w_proj, preferred_element_type=jnp.float32)
    gate_value = jax.nn.sigmoid(
        jnp.einsum("rqc,cd->rqd", normed, w_gate, preferred_element_type=jnp.float32)
    )
    left_op = (
        jax.nn.sigmoid(projected[:hidden]) * projected[hidden : 2 * hidden] * pair_mask
    ).astype(jnp.bfloat16)
    right_op = (
        jax.nn.sigmoid(projected[2 * hidden : 3 * hidden]) * projected[3 * hidden :] * pair_mask
    ).astype(jnp.bfloat16)
    left_chan, right_chan = (
        lax.all_to_all(left_op, "dap", split_axis=0, concat_axis=1, tiled=True),
        lax.all_to_all(right_op, "dap", split_axis=0, concat_axis=1, tiled=True),
    )
    if outgoing:
        right_rows = column_rows(right_chan)
        triangle = jnp.einsum(
            "hik,hjk->hij",
            lax.all_gather(left_chan, "grp", axis=2, tiled=True),
            right_rows,
            preferred_element_type=jnp.float32,
        )
    else:
        triangle = jnp.einsum(
            "hki,hkj->hij",
            lax.all_gather(left_chan, "grp", axis=2, tiled=True),
            right_chan,
            preferred_element_type=jnp.float32,
        )
    returned = lax.all_to_all(
        triangle.astype(jnp.bfloat16), "dap", split_axis=1, concat_axis=0, tiled=True
    )
    normed_product = layer_norm(returned.astype(jnp.float32), ln_out[:, None, None], 0).astype(
        jnp.bfloat16
    )
    update_term = jnp.einsum(
        "hrq,hd->rqd", normed_product, w_out, preferred_element_type=jnp.float32
    )
    return (pair_tile.astype(jnp.float32) + gate_value * update_term).astype(jnp.bfloat16)


def shards(pair_rep, chain_ids, crop_lengths, ln_in_gain, w_proj, w_gate, ln_out_gain, w_out):
    row_count = pair_rep.shape[0]
    column_count = pair_rep.shape[1]
    kept = residue_valid(chain_ids, crop_lengths)
    row_start = lax.axis_index("dap") * row_count
    column_start = lax.axis_index("grp") * column_count
    kept_rows = lax.dynamic_slice_in_dim(kept, row_start, row_count, 0)
    kept_columns = lax.dynamic_slice_in_dim(kept, column_start, column_count, 0)
    pair_mask = kept_rows[:, None] * kept_columns[None, :]
    pair_tile = pair_rep
    for layer_index, outgoing in ((0, True), (1, False)):
        pair_tile = update(
            pair_tile,
            pair_mask,
            ln_in_gain[layer_index],
            w_proj[layer_index],
            w_gate[layer_index],
            ln_out_gain[layer_index],
            w_out[layer_index],
            outgoing,
        )
    return pair_tile


def dot_nn(a, b):
    return lax.dot_general(a, b, (((1,), (0,)), ((), ())), preferred_element_type=F32)


def dot_nt(a, b):
    return lax.dot_general(a, b, (((1,), (1,)), ((), ())), preferred_element_type=F32)


def dot_tn(a, b):
    return lax.dot_general(a, b, (((0,), (0,)), ((), ())), preferred_element_type=F32)


def open_gate(half):
    return jnp.tanh(half) + 1.0


def halved(weights):
    return (weights.astype(F32) * 0.5).astype(BF16)


def one_hot(source, columns):
    place = lax.broadcasted_iota(jnp.int32, (source.shape[0], columns), 1)
    return jnp.where(place == source, 1.0, 0.0).astype(BF16)


def interleave(outer, inner):
    row = lax.broadcasted_iota(jnp.int32, (outer * inner, 1), 0)
    return one_hot((row % inner) * outer + row // inner, outer * inner)


def move(matrix, rows):
    return dot_nn(matrix, rows).astype(BF16)


def selection(slots, width):
    row = lax.broadcasted_iota(jnp.int32, (width, slots.shape[1]), 0).astype(F32)
    return jnp.where(row == slots, 1.0, 0.0).astype(BF16)


def kept_residues(ids, limits):
    place = lax.broadcasted_iota(jnp.int32, ids.shape, 1).astype(F32)
    kept = jnp.zeros(ids.shape, F32)
    for chain in range(limits.shape[1]):
        first = jnp.sum(jnp.where(ids < chain, 1.0, 0.0), axis=1, keepdims=True)
        limit = limits[:, chain : chain + 1].astype(F32)
        inside = jnp.where(ids == chain, 1.0, 0.0) * jnp.where(place - first < limit, 1.0, 0.0)
        kept = kept + inside
    return kept


def norm_rows(values, gain):
    centre = jnp.mean(values, axis=1, keepdims=True)
    apart = values - centre
    spread = jnp.mean(apart * apart, axis=1, keepdims=True)
    return (apart * lax.rsqrt(spread + epsilon_norm) * gain).astype(BF16)


def sort_projection(w_proj_ref, devices, sorted_ref):
    hidden = w_proj_ref.shape[1] // 4
    own = hidden // devices
    row = lax.broadcasted_iota(jnp.int32, (2 * hidden, 1), 0)
    side = (row % (2 * own)) // own
    order = one_hot(side * hidden + row // (2 * own) * own + row % own, 2 * hidden)
    for kind in range(2):
        sides = [
            w_proj_ref[:, block * hidden : (block + 1) * hidden] for block in (kind, kind + 2)
        ]
        rows = dot_nt(order, jnp.concatenate(sides, axis=1)) * 0.5
        sorted_ref[2 * hidden * kind : 2 * hidden * (kind + 1)] = rows.astype(BF16)


def project(normed, weights, w_gate, info_ref, gate_ref, send_ref, rows, width, start):
    span = normed.shape[0]
    half = weights.shape[0] // 2
    place = start + lax.broadcasted_iota(jnp.int32, (1, span), 1)
    mask = jnp.zeros((1, span), F32)
    for row in range(rows):
        inside = jnp.where(place >= row * width, 1.0, 0.0)
        inside = inside * jnp.where(place < (row + 1) * width, 1.0, 0.0)
        mask = mask + inside * info_ref[ROWS + row : ROWS + row + 1, 0:1]
    gate_ref[start : start + span] = open_gate(dot_nn(normed, w_gate))
    projected = dot_nt(weights, normed)
    operand = open_gate(projected[:half]) * projected[half:] * mask
    shape = send_ref.shape[:2] + (span,)
    send_ref[:, :, start : start + span] = operand.astype(BF16).reshape(shape)


def spans(total):
    start = 0
    while start < total:
        span = min(256, total - start)
        yield start, span
        start += span


LN_IN, LN_OUT, ROWS = 2, 4, 8


def gain_of(info_ref, row, width):
    return info_ref[row : row + 1, :width]


def first_kernel(
    devices,
    widths,
    me_ref,
    ids_hbm,
    crop_hbm,
    ln_in_hbm,
    ln_out_hbm,
    w_proj_hbm,
    w_gate_hbm,
    pair_hbm,
    choice_ref,
    info_ref,
    flat_ref,
    gate_ref,
    send_ref,
    ids_ref,
    crop_ref,
    ln_in_ref,
    ln_out_ref,
    w_proj_ref,
    w_gate_ref,
    pair_ref,
    normed_ref,
    weights_ref,
    arrived,
):
    moves = (
        (pair_hbm, pair_ref),
        (w_proj_hbm.at[0], w_proj_ref),
        (ids_hbm, ids_ref),
        (crop_hbm, crop_ref),
        (ln_in_hbm, ln_in_ref),
        (ln_out_hbm, ln_out_ref),
        (w_gate_hbm.at[0], w_gate_ref),
    )
    copies = [
        pltpu.make_async_copy(source, target, arrived.at[index])
        for index, (source, target) in enumerate(moves)
    ]
    for copy in copies:
        copy.start()
    rows, count, depth = pair_ref.shape
    flat_ref[...] = jnp.zeros(flat_ref.shape, BF16)
    normed_ref[...] = jnp.zeros(normed_ref.shape, BF16)
    info_ref[...] = jnp.zeros(info_ref.shape, F32)
    square = (count, count)
    up = lax.broadcasted_iota(jnp.int32, square, 0) < lax.broadcasted_iota(jnp.int32, square, 1)
    up = jnp.where(up, 1.0, 0.0).astype(BF16)
    for copy in copies:
        copy.wait()
    kept = kept_residues(ids_ref[...], crop_ref[...])
    total = jnp.sum(kept)
    choice = jnp.int32(0)
    width = jnp.int32(widths[0])
    for some, wider in zip(widths[:-1], widths[1:]):
        choice = choice + jnp.where(total > some, 1, 0).astype(jnp.int32)
        width = width + jnp.where(total > some, wider - some, 0).astype(jnp.int32)
    choice_ref[0] = choice
    rank = dot_nn(jnp.broadcast_to(kept, (8, count)).astype(BF16), up)[0:1]
    slots = jnp.where(kept > 0.0, rank, -1.0)
    pick = selection(slots, count)
    gain = ln_in_ref[0:1]
    lanes = [pair_ref[row] for row in range(rows)]
    lanes = lanes + [norm_rows(part.astype(F32), gain) for part in lanes]
    sort_projection(w_proj_ref, devices, weights_ref)
    packed = move(pick, jnp.concatenate(lanes, axis=1))
    for row in range(rows):
        here = pl.ds(pl.multiple_of(row * width, 16), count)
        flat_ref[here] = packed[:, row * depth : (row + 1) * depth]
        normed_ref[here] = packed[:, (rows + row) * depth : (rows + row + 1) * depth]
    place = lax.broadcasted_iota(jnp.int32, kept.shape, 1)
    for row in range(rows):
        own = jnp.where(place == me_ref[0] * rows + row, kept, 0.0)
        info_ref[ROWS + row : ROWS + row + 1] = jnp.broadcast_to(
            jnp.sum(own, axis=1, keepdims=True), kept.shape
        )
    info_ref[0:1] = slots
    info_ref[1:2] = dot_nt(
        jnp.broadcast_to(slots, (8, count)).astype(BF16), interleave(rows, devices)
    )[0:1]
    info_ref[LN_IN : LN_IN + 2, :depth] = ln_in_ref[...]
    info_ref[LN_OUT : LN_OUT + 2, : ln_out_ref.shape[1]] = ln_out_ref[...]
    w_gate = halved(w_gate_ref[...])
    for start, span in spans(rows * count):
        project(
            normed_ref[start : start + span],
            weights_ref[...],
            w_gate,
            info_ref,
            gate_ref,
            send_ref,
            rows,
            width,
            start,
        )


def channel_blocks(came_ref, rows, width):
    devices, channels, total = came_ref.shape
    came = move(
        interleave(channels, devices), came_ref[...].reshape(devices * channels, total)
    )
    blocks = []
    for channel in range(channels):
        span = slice(channel * devices, (channel + 1) * devices)
        parts = [came[span, row * width : (row + 1) * width] for row in range(rows)]
        blocks.append(jnp.concatenate(parts, axis=0))
    return blocks


def outgoing_kernel(rows, groups, info_ref, came_ref, w_proj_ref, send_ref, sorted_ref):
    devices, both, total = came_ref.shape
    own = both // 2
    width = total // rows
    pick = selection(info_ref[1:2], width)
    blocks = channel_blocks(came_ref, rows, width)
    products = [
        dot_nt(blocks[channel], move(pick, blocks[own + channel])).astype(BF16)
        for channel in range(own)
    ]
    low = rows * own // 8
    to_device = interleave(devices, 8)
    for offset in range(low):
        parts = []
        for channel in range(own):
            for high in range(rows // low):
                row = high * low + offset
                parts.append(products[channel][row * devices : (row + 1) * devices])
        sent = move(to_device, jnp.concatenate(parts, axis=0))
        send_ref[:, :, offset * width : (offset + 1) * width] = sent.reshape(devices, 8, width)
    sort_projection(w_proj_ref.at[1], devices // groups, sorted_ref)


def incoming_kernel(rows, info_ref, came_ref, send_ref):
    own = came_ref.shape[1] // 2
    devices = send_ref.shape[0]
    width = came_ref.shape[2] // rows
    pick = selection(info_ref[1:2], width)
    pick = dot_nt(interleave(1, rows * devices), pick).astype(BF16)
    blocks = channel_blocks(came_ref, rows, width)
    products = [
        move(pick, dot_tn(blocks[channel], blocks[own + channel]).astype(BF16))
        for channel in range(own)
    ]
    to_device = interleave(devices, own)
    for row in range(rows):
        span = slice(row * devices, (row + 1) * devices)
        sent = move(to_device, jnp.concatenate([product[span] for product in products], axis=0))
        send_ref[:, :, row * width : (row + 1) * width] = sent.reshape(devices, own, width)


def finish_parts(layer, groups, info_ref, came_ref, flat_ref, gate_ref, w_out_ref, use):
    devices, eight, lanes = came_ref.shape
    hidden = w_out_ref.shape[1]
    high = devices * eight // hidden // groups
    square = lax.broadcasted_iota(jnp.int32, (hidden, hidden), 0) == lax.broadcasted_iota(
        jnp.int32, (hidden, hidden), 1
    )
    gain = gain_of(info_ref, LN_OUT + layer, hidden)
    gain = jnp.sum(jnp.where(square, gain, 0.0), axis=1, keepdims=True)
    w_out = halved(w_out_ref[layer])
    for offset, span in spans(lanes):
        came = came_ref[:, :, offset : offset + span].reshape(devices * eight, span)
        if groups == 1:
            came = dot_nn(interleave(high, hidden), came)
        else:
            came = came.astype(F32)
            came = sum(came[hidden * group : hidden * (group + 1)] for group in range(groups))
        for part in range(high):
            block = came[part * hidden : (part + 1) * hidden]
            centre = jnp.mean(block, axis=0, keepdims=True)
            apart = block - centre
            spread = jnp.mean(apart * apart, axis=0, keepdims=True)
            normed = (apart * lax.rsqrt(spread + epsilon_norm) * gain).astype(BF16)
            term = dot_tn(normed, w_out)
            start = part * lanes + offset
            here = slice(start, start + span)
            use(start, (flat_ref[here].astype(F32) + gate_ref[here] * term).astype(BF16))


def middle_kernel(
    rows,
    info_ref,
    came_ref,
    flat_ref,
    gate_ref,
    w_out_ref,
    weights_ref,
    w_gate_ref,
    next_ref,
    next_gate_ref,
    send_ref,
):
    gain = gain_of(info_ref, LN_IN + 1, flat_ref.shape[1])
    width = next_ref.shape[0] // rows

    def use(start, fresh):
        next_ref[start : start + fresh.shape[0]] = fresh

    finish_parts(0, 1, info_ref, came_ref, flat_ref, gate_ref, w_out_ref, use)
    w_gate = halved(w_gate_ref[1])
    for start, span in spans(rows * width):
        project(
            norm_rows(next_ref[start : start + span].astype(F32), gain),
            weights_ref[...],
            w_gate,
            info_ref,
            next_gate_ref,
            send_ref,
            rows,
            width,
            start,
        )


def last_kernel(
    groups,
    info_ref,
    pair_ref,
    came_ref,
    flat_ref,
    gate_ref,
    w_out_ref,
    out_hbm,
    next_ref,
    row_ref,
    left,
):
    rows, count, depth = pair_ref.shape
    width = flat_ref.shape[0] // rows

    def use(start, fresh):
        next_ref[start : start + fresh.shape[0]] = fresh

    finish_parts(1, groups, info_ref, came_ref, flat_ref, gate_ref, w_out_ref, use)
    pick = selection(info_ref[0:1], width)
    pick = dot_nt(interleave(1, count), pick).astype(BF16)
    lanes = [next_ref[row * width : (row + 1) * width] for row in range(rows)]
    lanes.append(jnp.ones((width, depth), BF16))
    spread = dot_nn(pick, jnp.concatenate(lanes, axis=1))
    kept = spread[:, rows * depth :] > 0.5
    copies = []
    for row in range(rows):
        fresh = spread[:, row * depth : (row + 1) * depth]
        row_ref[row] = jnp.where(kept, fresh, pair_ref[row].astype(F32)).astype(BF16)
        copies.append(pltpu.make_async_copy(row_ref.at[row], out_hbm.at[row], left.at[row]))
        copies[row].start()
    for copy in copies:
        copy.wait()


SMEM = pl.BlockSpec(memory_space=pltpu.SMEM)
HBM = pl.BlockSpec(memory_space=pltpu.HBM)


VMEM = pl.BlockSpec(memory_space=pltpu.VMEM)


def call(body, name, outs, operands, specs=None, out_specs=None, scratch=()):
    return pl.pallas_call(
        body,
        out_shape=list(outs),
        in_specs=specs or [VMEM] * len(operands),
        out_specs=out_specs or [VMEM] * len(outs),
        scratch_shapes=list(scratch),
        compiler_params=pltpu.CompilerParams(vmem_limit_bytes=24 * 1024 * 1024),
        name=name,
    )(*operands)


def kept_columns(width, pair_rep, info, flat, gate, sent, w_proj, w_gate, w_out):
    devices = lax.axis_size("dap")
    rows, _, depth = pair_rep.shape
    hidden = w_out.shape[1]
    own = hidden // devices
    back_shape = jax.ShapeDtypeStruct((devices, 8, rows * own * width // 8), BF16)
    flat_shape = jax.ShapeDtypeStruct((rows * width, depth), BF16)
    gate_shape = jax.ShapeDtypeStruct((rows * width, depth), F32)
    sorted_shape = jax.ShapeDtypeStruct((4 * hidden, depth), BF16)

    apart = devices // GROUPS
    groups = [list(range(first, first + apart)) for first in range(0, devices, apart)]
    group_shape = jax.ShapeDtypeStruct((apart, 2 * own * GROUPS, rows * width), BF16)
    sums_shape = jax.ShapeDtypeStruct((devices, own * GROUPS, rows * width), BF16)

    def exchange(sent, within=None):
        return lax.all_to_all(
            sent, "dap", split_axis=0, concat_axis=0, axis_index_groups=within, tiled=True
        )

    sent = sent[:, :, : rows * width]
    came = exchange(sent)
    sent, weights = call(
        functools.partial(outgoing_kernel, rows, GROUPS),
        "outgoing",
        [back_shape, sorted_shape],
        (info, came, w_proj),
    )
    came = exchange(sent)
    flat, gate, sent = call(
        functools.partial(middle_kernel, rows),
        "finish_and_operands",
        [flat_shape, gate_shape, group_shape],
        (info, came, flat, gate, w_out, weights, w_gate),
    )
    came = exchange(sent, groups)
    sent = call(
        functools.partial(incoming_kernel, rows),
        "incoming",
        [sums_shape],
        (info, came),
    )[0]
    came = exchange(sent)
    return call(
        functools.partial(last_kernel, GROUPS),
        "finish",
        [pltpu.HBM(pair_rep.shape, BF16)],
        (info, pair_rep, came, flat, gate, w_out),
        out_specs=[HBM],
        scratch=[
            pltpu.VMEM(flat_shape.shape, BF16),
            pltpu.VMEM(pair_rep.shape, BF16),
            pltpu.SemaphoreType.DMA((rows,)),
        ],
    )[0]


def row_shards(pair_rep, chain_ids, crop_lengths, ln_in_gain, w_proj, w_gate, ln_out_gain, w_out):
    devices = lax.axis_size("dap")
    rows, count, depth = pair_rep.shape
    me = lax.axis_index("dap").reshape(1).astype(jnp.int32)
    ids = chain_ids.reshape(1, count)
    crops = crop_lengths.reshape(1, -1)
    widths = [count * share // 16 for share in SHARES]
    info_shape = jax.ShapeDtypeStruct((16, count), F32)
    flat_shape = jax.ShapeDtypeStruct((rows * count, depth), BF16)
    send_shape = jax.ShapeDtypeStruct((devices, w_proj.shape[2] // devices // 2, rows * count), BF16)
    gate_shape = jax.ShapeDtypeStruct(flat_shape.shape, F32)
    choice, info, flat, gate, sent = call(
        functools.partial(first_kernel, devices, widths),
        "first_operands",
        [
            pltpu.SMEM((1,), jnp.int32),
            info_shape,
            flat_shape,
            gate_shape,
            send_shape,
        ],
        [me]
        + [
            pltpu.with_memory_space_constraint(array, pltpu.HBM)
            for array in (ids, crops, ln_in_gain, ln_out_gain, w_proj, w_gate, pair_rep)
        ],
        specs=[SMEM] + [HBM] * 7,
        out_specs=[SMEM] + [VMEM] * 4,
        scratch=[
            pltpu.VMEM(ids.shape, jnp.int32),
            pltpu.VMEM(crops.shape, jnp.int32),
            pltpu.VMEM(ln_in_gain.shape, F32),
            pltpu.VMEM(ln_out_gain.shape, F32),
            pltpu.VMEM(w_proj.shape[1:], BF16),
            pltpu.VMEM(w_gate.shape[1:], BF16),
            pltpu.VMEM(pair_rep.shape, BF16),
            pltpu.VMEM(flat_shape.shape, BF16),
            pltpu.VMEM((w_proj.shape[2], depth), BF16),
            pltpu.SemaphoreType.DMA((7,)),
        ],
    )
    return lax.switch(
        choice[0],
        [functools.partial(kept_columns, some) for some in widths],
        pair_rep,
        info,
        flat,
        gate,
        sent,
        w_proj,
        w_gate,
        w_out,
    )


GROUPS = 2
SHARES = (11, 12, 13, 14, 16)


def solution(mesh):
    devices = mesh.shape["dap"]
    placed = (P("dap", "grp", None), P(), P(), P(), P(), P(), P(), P())

    def body(*arrays):
        rows, count, width = arrays[0].shape
        hidden = arrays[-1].shape[1]
        plain = (
            mesh.shape["grp"] == 1
            and rows * devices == count
            and count == 256
            and rows == 8
            and hidden == 4 * devices
        )
        return (row_shards if plain else shards)(*arrays)

    return jax.shard_map(
        body, mesh=mesh, in_specs=placed, out_specs=P("dap", "grp", None), check_vma=False
    )
```

```python
import functools

import jax
import jax.numpy as jnp
from jax import lax
from jax.experimental import pallas as pl
from jax.experimental.pallas import tpu as pltpu
from jax.sharding import PartitionSpec as P

epsilon_norm = 1e-05
F32 = jnp.float32
BF16 = jnp.bfloat16


def residue_valid(chain_ids, crop_lengths):
    count = chain_ids.shape[0]
    chains = jnp.arange(crop_lengths.shape[0], dtype=jnp.int32)
    member = (chain_ids[:, None] == chains[None, :]).astype(jnp.int32)
    counts = jnp.sum(member, axis=0)
    starts = jnp.cumsum(counts) - counts
    first = jnp.sum(member * starts[None, :], axis=1)
    limit = jnp.sum(member * crop_lengths[None, :], axis=1)
    place = jnp.arange(count, dtype=jnp.int32) - first
    return (place < limit).astype(jnp.float32)


def layer_norm(values, gain, axis):
    centre = jnp.mean(values, axis=axis, keepdims=True)
    spread = jnp.mean((values - centre) ** 2, axis=axis, keepdims=True)
    return (values - centre) * lax.rsqrt(spread + epsilon_norm) * gain


def column_rows(right_chan):
    return lax.all_to_all(right_chan, "grp", split_axis=1, concat_axis=2, tiled=True)


def update(pair_tile, pair_mask, ln_in, w_proj, w_gate, ln_out, w_out, outgoing):
    hidden = w_out.shape[0]
    normed = layer_norm(pair_tile.astype(jnp.float32), ln_in, 2).astype(jnp.bfloat16)
    projected = jnp.einsum("rqc,cf->frq", normed, w_proj, preferred_element_type=jnp.float32)
    gate_value = jax.nn.sigmoid(
        jnp.einsum("rqc,cd->rqd", normed, w_gate, preferred_element_type=jnp.float32)
    )
    left_op = (
        jax.nn.sigmoid(projected[:hidden]) * projected[hidden : 2 * hidden] * pair_mask
    ).astype(jnp.bfloat16)
    right_op = (
        jax.nn.sigmoid(projected[2 * hidden : 3 * hidden]) * projected[3 * hidden :] * pair_mask
    ).astype(jnp.bfloat16)
    left_chan, right_chan = (
        lax.all_to_all(left_op, "dap", split_axis=0, concat_axis=1, tiled=True),
        lax.all_to_all(right_op, "dap", split_axis=0, concat_axis=1, tiled=True),
    )
    if outgoing:
        right_rows = column_rows(right_chan)
        triangle = jnp.einsum(
            "hik,hjk->hij",
            lax.all_gather(left_chan, "grp", axis=2, tiled=True),
            right_rows,
            preferred_element_type=jnp.float32,
        )
    else:
        triangle = jnp.einsum(
            "hki,hkj->hij",
            lax.all_gather(left_chan, "grp", axis=2, tiled=True),
            right_chan,
            preferred_element_type=jnp.float32,
        )
    returned = lax.all_to_all(
        triangle.astype(jnp.bfloat16), "dap", split_axis=1, concat_axis=0, tiled=True
    )
    normed_product = layer_norm(returned.astype(jnp.float32), ln_out[:, None, None], 0).astype(
        jnp.bfloat16
    )
    update_term = jnp.einsum(
        "hrq,hd->rqd", normed_product, w_out, preferred_element_type=jnp.float32
    )
    return (pair_tile.astype(jnp.float32) + gate_value * update_term).astype(jnp.bfloat16)


def shards(pair_rep, chain_ids, crop_lengths, ln_in_gain, w_proj, w_gate, ln_out_gain, w_out):
    row_count = pair_rep.shape[0]
    column_count = pair_rep.shape[1]
    kept = residue_valid(chain_ids, crop_lengths)
    row_start = lax.axis_index("dap") * row_count
    column_start = lax.axis_index("grp") * column_count
    kept_rows = lax.dynamic_slice_in_dim(kept, row_start, row_count, 0)
    kept_columns = lax.dynamic_slice_in_dim(kept, column_start, column_count, 0)
    pair_mask = kept_rows[:, None] * kept_columns[None, :]
    pair_tile = pair_rep
    for layer_index, outgoing in ((0, True), (1, False)):
        pair_tile = update(
            pair_tile,
            pair_mask,
            ln_in_gain[layer_index],
            w_proj[layer_index],
            w_gate[layer_index],
            ln_out_gain[layer_index],
            w_out[layer_index],
            outgoing,
        )
    return pair_tile


def dot_nn(a, b):
    return lax.dot_general(a, b, (((1,), (0,)), ((), ())), preferred_element_type=F32)


def dot_nt(a, b):
    return lax.dot_general(a, b, (((1,), (1,)), ((), ())), preferred_element_type=F32)


def dot_tn(a, b):
    return lax.dot_general(a, b, (((0,), (0,)), ((), ())), preferred_element_type=F32)


def open_gate(half):
    return jnp.tanh(half) + 1.0


def halved(weights):
    return (weights.astype(F32) * 0.5).astype(BF16)


def one_hot(source, columns):
    place = lax.broadcasted_iota(jnp.int32, (source.shape[0], columns), 1)
    return jnp.where(place == source, 1.0, 0.0).astype(BF16)


def interleave(outer, inner):
    row = lax.broadcasted_iota(jnp.int32, (outer * inner, 1), 0)
    return one_hot((row % inner) * outer + row // inner, outer * inner)


def move(matrix, rows):
    return dot_nn(matrix, rows).astype(BF16)


def selection(slots, width):
    row = lax.broadcasted_iota(jnp.int32, (width, slots.shape[1]), 0).astype(F32)
    return jnp.where(row == slots, 1.0, 0.0).astype(BF16)


def kept_residues(ids, limits):
    place = lax.broadcasted_iota(jnp.int32, ids.shape, 1).astype(F32)
    kept = jnp.zeros(ids.shape, F32)
    for chain in range(limits.shape[1]):
        first = jnp.sum(jnp.where(ids < chain, 1.0, 0.0), axis=1, keepdims=True)
        limit = limits[:, chain : chain + 1].astype(F32)
        inside = jnp.where(ids == chain, 1.0, 0.0) * jnp.where(place - first < limit, 1.0, 0.0)
        kept = kept + inside
    return kept


def norm_rows(values, gain):
    centre = jnp.mean(values, axis=1, keepdims=True)
    apart = values - centre
    spread = jnp.mean(apart * apart, axis=1, keepdims=True)
    return (apart * lax.rsqrt(spread + epsilon_norm) * gain).astype(BF16)


def sort_projection(w_proj_ref, devices, sorted_ref):
    hidden = w_proj_ref.shape[1] // 4
    own = hidden // devices
    row = lax.broadcasted_iota(jnp.int32, (2 * hidden, 1), 0)
    side = (row % (2 * own)) // own
    order = one_hot(side * hidden + row // (2 * own) * own + row % own, 2 * hidden)
    for kind in range(2):
        sides = [
            w_proj_ref[:, block * hidden : (block + 1) * hidden] for block in (kind, kind + 2)
        ]
        rows = dot_nt(order, jnp.concatenate(sides, axis=1)) * 0.5
        sorted_ref[2 * hidden * kind : 2 * hidden * (kind + 1)] = rows.astype(BF16)


def project(normed, weights, w_gate, info_ref, gate_ref, send_ref, rows, width, start):
    span = normed.shape[0]
    half = weights.shape[0] // 2
    place = start + lax.broadcasted_iota(jnp.int32, (1, span), 1)
    mask = jnp.zeros((1, span), F32)
    for row in range(rows):
        inside = jnp.where(place >= row * width, 1.0, 0.0)
        inside = inside * jnp.where(place < (row + 1) * width, 1.0, 0.0)
        mask = mask + inside * info_ref[ROWS + row : ROWS + row + 1, 0:1]
    gate_ref[start : start + span] = open_gate(dot_nn(normed, w_gate))
    projected = dot_nt(weights, normed)
    operand = open_gate(projected[:half]) * projected[half:] * mask
    shape = send_ref.shape[:2] + (span,)
    send_ref[:, :, start : start + span] = operand.astype(BF16).reshape(shape)


def spans(total):
    start = 0
    while start < total:
        span = min(256, total - start)
        yield start, span
        start += span


LN_IN, LN_OUT, ROWS = 2, 4, 8
BY_CHANNEL, BY_GROUP_CHANNEL, TO_DEVICE, BY_PART, PICK, SPREAD, SPREAD_COLUMNS = range(7)


def gain_of(info_ref, row, width):
    return info_ref[row : row + 1, :width]


def first_kernel(
    devices,
    widths,
    me_ref,
    ids_hbm,
    crop_hbm,
    ln_in_hbm,
    ln_out_hbm,
    w_proj_hbm,
    w_gate_hbm,
    pair_hbm,
    choice_ref,
    info_ref,
    tables_ref,
    flat_ref,
    gate_ref,
    send_ref,
    ids_ref,
    crop_ref,
    ln_in_ref,
    ln_out_ref,
    w_proj_ref,
    w_gate_ref,
    pair_ref,
    normed_ref,
    weights_ref,
    arrived,
):
    moves = (
        (pair_hbm, pair_ref),
        (w_proj_hbm.at[0], w_proj_ref),
        (ids_hbm, ids_ref),
        (crop_hbm, crop_ref),
        (ln_in_hbm, ln_in_ref),
        (ln_out_hbm, ln_out_ref),
        (w_gate_hbm.at[0], w_gate_ref),
    )
    copies = [
        pltpu.make_async_copy(source, target, arrived.at[index])
        for index, (source, target) in enumerate(moves)
    ]
    for copy in copies:
        copy.start()
    rows, count, depth = pair_ref.shape
    flat_ref[...] = jnp.zeros(flat_ref.shape, BF16)
    normed_ref[...] = jnp.zeros(normed_ref.shape, BF16)
    info_ref[...] = jnp.zeros(info_ref.shape, F32)
    square = (count, count)
    up = lax.broadcasted_iota(jnp.int32, square, 0) < lax.broadcasted_iota(jnp.int32, square, 1)
    up = jnp.where(up, 1.0, 0.0).astype(BF16)
    by_row = interleave(rows, devices)
    alike = interleave(1, count)
    tables_ref[BY_CHANNEL] = interleave(count // devices, devices)
    tables_ref[BY_GROUP_CHANNEL] = interleave(count * GROUPS // devices, devices // GROUPS)
    tables_ref[TO_DEVICE] = interleave(devices, rows)
    tables_ref[BY_PART] = interleave(2, count // 2)
    for copy in copies:
        copy.wait()
    kept = kept_residues(ids_ref[...], crop_ref[...])
    total = jnp.sum(kept)
    choice = jnp.int32(0)
    width = jnp.int32(widths[0])
    for some, wider in zip(widths[:-1], widths[1:]):
        choice = choice + jnp.where(total > some, 1, 0).astype(jnp.int32)
        width = width + jnp.where(total > some, wider - some, 0).astype(jnp.int32)
    choice_ref[0] = choice
    rank = dot_nn(jnp.broadcast_to(kept, (8, count)).astype(BF16), up)[0:1]
    slots = jnp.where(kept > 0.0, rank, -1.0)
    pick = selection(slots, count)
    gain = ln_in_ref[0:1]
    lanes = [pair_ref[row] for row in range(rows)]
    lanes = lanes + [norm_rows(part.astype(F32), gain) for part in lanes]
    sort_projection(w_proj_ref, devices, weights_ref)
    packed = move(pick, jnp.concatenate(lanes, axis=1))
    for row in range(rows):
        here = pl.ds(pl.multiple_of(row * width, 16), count)
        flat_ref[here] = packed[:, row * depth : (row + 1) * depth]
        normed_ref[here] = packed[:, (rows + row) * depth : (rows + row + 1) * depth]
    place = lax.broadcasted_iota(jnp.int32, kept.shape, 1)
    for row in range(rows):
        own = jnp.where(place == me_ref[0] * rows + row, kept, 0.0)
        info_ref[ROWS + row : ROWS + row + 1] = jnp.broadcast_to(
            jnp.sum(own, axis=1, keepdims=True), kept.shape
        )
    tables_ref[SPREAD_COLUMNS] = dot_nt(alike, pick).astype(BF16)
    pick = dot_nt(pick, by_row).astype(BF16)
    tables_ref[PICK] = pick
    tables_ref[SPREAD] = dot_nt(alike, pick).astype(BF16)
    info_ref[LN_IN : LN_IN + 2, :depth] = ln_in_ref[...]
    info_ref[LN_OUT : LN_OUT + 2, : ln_out_ref.shape[1]] = ln_out_ref[...]
    w_gate = halved(w_gate_ref[...])
    for start, span in spans(rows * count):
        project(
            normed_ref[start : start + span],
            weights_ref[...],
            w_gate,
            info_ref,
            gate_ref,
            send_ref,
            rows,
            width,
            start,
        )


def channel_blocks(order, came_ref, rows, width):
    devices, channels, total = came_ref.shape
    came = move(order, came_ref[...].reshape(devices * channels, total))
    blocks = []
    for channel in range(channels):
        span = slice(channel * devices, (channel + 1) * devices)
        parts = [came[span, row * width : (row + 1) * width] for row in range(rows)]
        blocks.append(jnp.concatenate(parts, axis=0))
    return blocks


def outgoing_kernel(rows, groups, tables_ref, came_ref, w_proj_ref, send_ref, sorted_ref):
    devices, both, total = came_ref.shape
    own = both // 2
    width = total // rows
    pick = tables_ref[PICK, :width]
    blocks = channel_blocks(tables_ref[BY_CHANNEL], came_ref, rows, width)
    products = [
        dot_nt(blocks[channel], move(pick, blocks[own + channel])).astype(BF16)
        for channel in range(own)
    ]
    low = rows * own // 8
    to_device = tables_ref[TO_DEVICE]
    for offset in range(low):
        parts = []
        for channel in range(own):
            for high in range(rows // low):
                row = high * low + offset
                parts.append(products[channel][row * devices : (row + 1) * devices])
        sent = move(to_device, jnp.concatenate(parts, axis=0))
        send_ref[:, :, offset * width : (offset + 1) * width] = sent.reshape(devices, 8, width)
    sort_projection(w_proj_ref.at[1], devices // groups, sorted_ref)


def incoming_kernel(rows, tables_ref, came_ref, send_ref):
    own = came_ref.shape[1] // 2
    devices = send_ref.shape[0]
    width = came_ref.shape[2] // rows
    spread = tables_ref[SPREAD, :, :width]
    blocks = channel_blocks(tables_ref[BY_GROUP_CHANNEL], came_ref, rows, width)
    products = [
        move(spread, dot_tn(blocks[channel], blocks[own + channel]).astype(BF16))
        for channel in range(own)
    ]
    to_device = tables_ref[TO_DEVICE]
    for row in range(rows):
        span = slice(row * devices, (row + 1) * devices)
        sent = move(to_device, jnp.concatenate([product[span] for product in products], axis=0))
        send_ref[:, :, row * width : (row + 1) * width] = sent.reshape(devices, own, width)


def finish_parts(
    layer, groups, info_ref, tables_ref, came_ref, flat_ref, gate_ref, w_out_ref, use
):
    devices, eight, lanes = came_ref.shape
    hidden = w_out_ref.shape[1]
    high = devices * eight // hidden // groups
    square = lax.broadcasted_iota(jnp.int32, (hidden, hidden), 0) == lax.broadcasted_iota(
        jnp.int32, (hidden, hidden), 1
    )
    gain = gain_of(info_ref, LN_OUT + layer, hidden)
    gain = jnp.sum(jnp.where(square, gain, 0.0), axis=1, keepdims=True)
    w_out = halved(w_out_ref[layer])
    for offset, span in spans(lanes):
        came = came_ref[:, :, offset : offset + span].reshape(devices * eight, span)
        if groups == 1:
            came = dot_nn(tables_ref[BY_PART], came)
        else:
            came = came.astype(F32)
            came = sum(came[hidden * group : hidden * (group + 1)] for group in range(groups))
        for part in range(high):
            block = came[part * hidden : (part + 1) * hidden]
            centre = jnp.mean(block, axis=0, keepdims=True)
            apart = block - centre
            spread = jnp.mean(apart * apart, axis=0, keepdims=True)
            normed = (apart * lax.rsqrt(spread + epsilon_norm) * gain).astype(BF16)
            term = dot_tn(normed, w_out)
            start = part * lanes + offset
            here = slice(start, start + span)
            use(start, (flat_ref[here].astype(F32) + gate_ref[here] * term).astype(BF16))


def middle_kernel(
    rows,
    info_ref,
    tables_ref,
    came_ref,
    flat_ref,
    gate_ref,
    w_out_ref,
    weights_ref,
    w_gate_ref,
    next_ref,
    next_gate_ref,
    send_ref,
):
    gain = gain_of(info_ref, LN_IN + 1, flat_ref.shape[1])
    width = next_ref.shape[0] // rows

    def use(start, fresh):
        next_ref[start : start + fresh.shape[0]] = fresh

    finish_parts(0, 1, info_ref, tables_ref, came_ref, flat_ref, gate_ref, w_out_ref, use)
    w_gate = halved(w_gate_ref[1])
    for start, span in spans(rows * width):
        project(
            norm_rows(next_ref[start : start + span].astype(F32), gain),
            weights_ref[...],
            w_gate,
            info_ref,
            next_gate_ref,
            send_ref,
            rows,
            width,
            start,
        )


def last_kernel(
    groups,
    info_ref,
    tables_ref,
    pair_ref,
    came_ref,
    flat_ref,
    gate_ref,
    w_out_ref,
    out_ref,
    next_ref,
):
    rows, count, depth = out_ref.shape
    width = flat_ref.shape[0] // rows

    def use(start, fresh):
        next_ref[start : start + fresh.shape[0]] = fresh

    finish_parts(1, groups, info_ref, tables_ref, came_ref, flat_ref, gate_ref, w_out_ref, use)
    lanes = [next_ref[row * width : (row + 1) * width] for row in range(rows)]
    lanes.append(jnp.ones((width, depth), BF16))
    spread = dot_nn(tables_ref[SPREAD_COLUMNS, :, :width], jnp.concatenate(lanes, axis=1))
    kept = spread[:, rows * depth :] > 0.5
    for row in range(rows):
        fresh = spread[:, row * depth : (row + 1) * depth]
        out_ref[row] = jnp.where(kept, fresh, pair_ref[row].astype(F32)).astype(BF16)


SMEM = pl.BlockSpec(memory_space=pltpu.SMEM)
HBM = pl.BlockSpec(memory_space=pltpu.HBM)


VMEM = pl.BlockSpec(memory_space=pltpu.VMEM)


def call(body, name, outs, operands, specs=None, out_specs=None, scratch=()):
    return pl.pallas_call(
        body,
        out_shape=list(outs),
        in_specs=specs or [VMEM] * len(operands),
        out_specs=out_specs or [VMEM] * len(outs),
        scratch_shapes=list(scratch),
        compiler_params=pltpu.CompilerParams(vmem_limit_bytes=24 * 1024 * 1024),
        name=name,
    )(*operands)


def kept_columns(width, pair_rep, info, tables, flat, gate, sent, w_proj, w_gate, w_out):
    devices = lax.axis_size("dap")
    rows, _, depth = pair_rep.shape
    hidden = w_out.shape[1]
    own = hidden // devices
    back_shape = jax.ShapeDtypeStruct((devices, 8, rows * own * width // 8), BF16)
    flat_shape = jax.ShapeDtypeStruct((rows * width, depth), BF16)
    gate_shape = jax.ShapeDtypeStruct((rows * width, depth), F32)
    sorted_shape = jax.ShapeDtypeStruct((4 * hidden, depth), BF16)

    apart = devices // GROUPS
    groups = [list(range(first, first + apart)) for first in range(0, devices, apart)]
    group_shape = jax.ShapeDtypeStruct((apart, 2 * own * GROUPS, rows * width), BF16)
    sums_shape = jax.ShapeDtypeStruct((devices, own * GROUPS, rows * width), BF16)

    def exchange(sent, within=None):
        return lax.all_to_all(
            sent, "dap", split_axis=0, concat_axis=0, axis_index_groups=within, tiled=True
        )

    sent = sent[:, :, : rows * width]
    came = exchange(sent)
    sent, weights = call(
        functools.partial(outgoing_kernel, rows, GROUPS),
        "outgoing",
        [back_shape, sorted_shape],
        (tables, came, w_proj),
    )
    came = exchange(sent)
    flat, gate, sent = call(
        functools.partial(middle_kernel, rows),
        "finish_and_operands",
        [flat_shape, gate_shape, group_shape],
        (info, tables, came, flat, gate, w_out, weights, w_gate),
    )
    came = exchange(sent, groups)
    sent = call(
        functools.partial(incoming_kernel, rows),
        "incoming",
        [sums_shape],
        (tables, came),
    )[0]
    came = exchange(sent)
    return call(
        functools.partial(last_kernel, GROUPS),
        "finish",
        [jax.ShapeDtypeStruct(pair_rep.shape, BF16)],
        (info, tables, pair_rep, came, flat, gate, w_out),
        scratch=[pltpu.VMEM(flat_shape.shape, BF16)],
    )[0]


def row_shards(pair_rep, chain_ids, crop_lengths, ln_in_gain, w_proj, w_gate, ln_out_gain, w_out):
    devices = lax.axis_size("dap")
    rows, count, depth = pair_rep.shape
    me = lax.axis_index("dap").reshape(1).astype(jnp.int32)
    ids = chain_ids.reshape(1, count)
    crops = crop_lengths.reshape(1, -1)
    widths = [count * share // 16 for share in SHARES]
    info_shape = jax.ShapeDtypeStruct((16, count), F32)
    flat_shape = jax.ShapeDtypeStruct((rows * count, depth), BF16)
    send_shape = jax.ShapeDtypeStruct((devices, w_proj.shape[2] // devices // 2, rows * count), BF16)
    gate_shape = jax.ShapeDtypeStruct(flat_shape.shape, F32)
    tables_shape = jax.ShapeDtypeStruct((7, count, count), BF16)
    choice, info, tables, flat, gate, sent = call(
        functools.partial(first_kernel, devices, widths),
        "first_operands",
        [
            pltpu.SMEM((1,), jnp.int32),
            info_shape,
            tables_shape,
            flat_shape,
            gate_shape,
            send_shape,
        ],
        [me]
        + [
            pltpu.with_memory_space_constraint(array, pltpu.HBM)
            for array in (ids, crops, ln_in_gain, ln_out_gain, w_proj, w_gate, pair_rep)
        ],
        specs=[SMEM] + [HBM] * 7,
        out_specs=[SMEM] + [VMEM] * 5,
        scratch=[
            pltpu.VMEM(ids.shape, jnp.int32),
            pltpu.VMEM(crops.shape, jnp.int32),
            pltpu.VMEM(ln_in_gain.shape, F32),
            pltpu.VMEM(ln_out_gain.shape, F32),
            pltpu.VMEM(w_proj.shape[1:], BF16),
            pltpu.VMEM(w_gate.shape[1:], BF16),
            pltpu.VMEM(pair_rep.shape, BF16),
            pltpu.VMEM(flat_shape.shape, BF16),
            pltpu.VMEM((w_proj.shape[2], depth), BF16),
            pltpu.SemaphoreType.DMA((7,)),
        ],
    )
    return lax.switch(
        choice[0],
        [functools.partial(kept_columns, some) for some in widths],
        pair_rep,
        info,
        tables,
        flat,
        gate,
        sent,
        w_proj,
        w_gate,
        w_out,
    )


GROUPS = 2
SHARES = (11, 12, 13, 14, 16)


def solution(mesh):
    devices = mesh.shape["dap"]
    placed = (P("dap", "grp", None), P(), P(), P(), P(), P(), P(), P())

    def body(*arrays):
        rows, count, width = arrays[0].shape
        hidden = arrays[-1].shape[1]
        plain = (
            mesh.shape["grp"] == 1
            and rows * devices == count
            and count == 256
            and rows == 8
            and hidden == 4 * devices
        )
        return (row_shards if plain else shards)(*arrays)

    return jax.shard_map(
        body, mesh=mesh, in_specs=placed, out_specs=P("dap", "grp", None), check_vma=False
    )
```

```python
import functools

import jax
import jax.numpy as jnp
from jax import lax
from jax.experimental import pallas as pl
from jax.experimental.pallas import tpu as pltpu
from jax.sharding import PartitionSpec as P

epsilon_norm = 1e-05
F32 = jnp.float32
BF16 = jnp.bfloat16


def residue_valid(chain_ids, crop_lengths):
    count = chain_ids.shape[0]
    chains = jnp.arange(crop_lengths.shape[0], dtype=jnp.int32)
    member = (chain_ids[:, None] == chains[None, :]).astype(jnp.int32)
    counts = jnp.sum(member, axis=0)
    starts = jnp.cumsum(counts) - counts
    first = jnp.sum(member * starts[None, :], axis=1)
    limit = jnp.sum(member * crop_lengths[None, :], axis=1)
    place = jnp.arange(count, dtype=jnp.int32) - first
    return (place < limit).astype(jnp.float32)


def layer_norm(values, gain, axis):
    centre = jnp.mean(values, axis=axis, keepdims=True)
    spread = jnp.mean((values - centre) ** 2, axis=axis, keepdims=True)
    return (values - centre) * lax.rsqrt(spread + epsilon_norm) * gain


def column_rows(right_chan):
    return lax.all_to_all(right_chan, "grp", split_axis=1, concat_axis=2, tiled=True)


def update(pair_tile, pair_mask, ln_in, w_proj, w_gate, ln_out, w_out, outgoing):
    hidden = w_out.shape[0]
    normed = layer_norm(pair_tile.astype(jnp.float32), ln_in, 2).astype(jnp.bfloat16)
    projected = jnp.einsum("rqc,cf->frq", normed, w_proj, preferred_element_type=jnp.float32)
    gate_value = jax.nn.sigmoid(
        jnp.einsum("rqc,cd->rqd", normed, w_gate, preferred_element_type=jnp.float32)
    )
    left_op = (
        jax.nn.sigmoid(projected[:hidden]) * projected[hidden : 2 * hidden] * pair_mask
    ).astype(jnp.bfloat16)
    right_op = (
        jax.nn.sigmoid(projected[2 * hidden : 3 * hidden]) * projected[3 * hidden :] * pair_mask
    ).astype(jnp.bfloat16)
    left_chan, right_chan = (
        lax.all_to_all(left_op, "dap", split_axis=0, concat_axis=1, tiled=True),
        lax.all_to_all(right_op, "dap", split_axis=0, concat_axis=1, tiled=True),
    )
    if outgoing:
        right_rows = column_rows(right_chan)
        triangle = jnp.einsum(
            "hik,hjk->hij",
            lax.all_gather(left_chan, "grp", axis=2, tiled=True),
            right_rows,
            preferred_element_type=jnp.float32,
        )
    else:
        triangle = jnp.einsum(
            "hki,hkj->hij",
            lax.all_gather(left_chan, "grp", axis=2, tiled=True),
            right_chan,
            preferred_element_type=jnp.float32,
        )
    returned = lax.all_to_all(
        triangle.astype(jnp.bfloat16), "dap", split_axis=1, concat_axis=0, tiled=True
    )
    normed_product = layer_norm(returned.astype(jnp.float32), ln_out[:, None, None], 0).astype(
        jnp.bfloat16
    )
    update_term = jnp.einsum(
        "hrq,hd->rqd", normed_product, w_out, preferred_element_type=jnp.float32
    )
    return (pair_tile.astype(jnp.float32) + gate_value * update_term).astype(jnp.bfloat16)


def shards(pair_rep, chain_ids, crop_lengths, ln_in_gain, w_proj, w_gate, ln_out_gain, w_out):
    row_count = pair_rep.shape[0]
    column_count = pair_rep.shape[1]
    kept = residue_valid(chain_ids, crop_lengths)
    row_start = lax.axis_index("dap") * row_count
    column_start = lax.axis_index("grp") * column_count
    kept_rows = lax.dynamic_slice_in_dim(kept, row_start, row_count, 0)
    kept_columns = lax.dynamic_slice_in_dim(kept, column_start, column_count, 0)
    pair_mask = kept_rows[:, None] * kept_columns[None, :]
    pair_tile = pair_rep
    for layer_index, outgoing in ((0, True), (1, False)):
        pair_tile = update(
            pair_tile,
            pair_mask,
            ln_in_gain[layer_index],
            w_proj[layer_index],
            w_gate[layer_index],
            ln_out_gain[layer_index],
            w_out[layer_index],
            outgoing,
        )
    return pair_tile


def dot_nn(a, b):
    return lax.dot_general(a, b, (((1,), (0,)), ((), ())), preferred_element_type=F32)


def dot_nt(a, b):
    return lax.dot_general(a, b, (((1,), (1,)), ((), ())), preferred_element_type=F32)


def dot_tn(a, b):
    return lax.dot_general(a, b, (((0,), (0,)), ((), ())), preferred_element_type=F32)


def open_gate(half):
    return jnp.tanh(half) + 1.0


def halved(weights):
    return (weights.astype(F32) * 0.5).astype(BF16)


def one_hot(source, columns):
    place = lax.broadcasted_iota(jnp.int32, (source.shape[0], columns), 1)
    return jnp.where(place == source, 1.0, 0.0).astype(BF16)


def interleave(outer, inner):
    row = lax.broadcasted_iota(jnp.int32, (outer * inner, 1), 0)
    return one_hot((row % inner) * outer + row // inner, outer * inner)


def move(matrix, rows):
    return dot_nn(matrix, rows).astype(BF16)


def selection(slots, width):
    row = lax.broadcasted_iota(jnp.int32, (width, slots.shape[1]), 0).astype(F32)
    return jnp.where(row == slots, 1.0, 0.0).astype(BF16)


def kept_residues(ids, limits):
    place = lax.broadcasted_iota(jnp.int32, ids.shape, 1).astype(F32)
    kept = jnp.zeros(ids.shape, F32)
    for chain in range(limits.shape[1]):
        first = jnp.sum(jnp.where(ids < chain, 1.0, 0.0), axis=1, keepdims=True)
        limit = limits[:, chain : chain + 1].astype(F32)
        inside = jnp.where(ids == chain, 1.0, 0.0) * jnp.where(place - first < limit, 1.0, 0.0)
        kept = kept + inside
    return kept


def norm_rows(values, gain):
    centre = jnp.mean(values, axis=1, keepdims=True)
    apart = values - centre
    spread = jnp.mean(apart * apart, axis=1, keepdims=True)
    return (apart * lax.rsqrt(spread + epsilon_norm) * gain).astype(BF16)


def sort_projection(w_proj_ref, devices, sorted_ref):
    hidden = w_proj_ref.shape[1] // 4
    own = hidden // devices
    row = lax.broadcasted_iota(jnp.int32, (2 * hidden, 1), 0)
    side = (row % (2 * own)) // own
    order = one_hot(side * hidden + row // (2 * own) * own + row % own, 2 * hidden)
    for kind in range(2):
        sides = [
            w_proj_ref[:, block * hidden : (block + 1) * hidden] for block in (kind, kind + 2)
        ]
        rows = dot_nt(order, jnp.concatenate(sides, axis=1)) * 0.5
        sorted_ref[2 * hidden * kind : 2 * hidden * (kind + 1)] = rows.astype(BF16)


def project(normed, weights, w_gate, info_ref, gate_ref, send_ref, rows, width, start):
    span = normed.shape[0]
    half = weights.shape[0] // 2
    place = start + lax.broadcasted_iota(jnp.int32, (1, span), 1)
    mask = jnp.zeros((1, span), F32)
    for row in range(rows):
        if isinstance(width, int) and not start - width < row * width < start + span:
            continue
        inside = jnp.where(place >= row * width, 1.0, 0.0)
        inside = inside * jnp.where(place < (row + 1) * width, 1.0, 0.0)
        mask = mask + inside * info_ref[ROWS + row : ROWS + row + 1, 0:1]
    gate_ref[start : start + span] = open_gate(dot_nn(normed, w_gate))
    projected = dot_nt(weights, normed)
    operand = open_gate(projected[:half]) * projected[half:] * mask
    shape = send_ref.shape[:2] + (span,)
    send_ref[:, :, start : start + span] = operand.astype(BF16).reshape(shape)


def spans(total):
    start = 0
    while start < total:
        span = min(256, total - start)
        yield start, span
        start += span


LN_IN, LN_OUT, ROWS = 2, 4, 8


def gain_of(info_ref, row, width):
    return info_ref[row : row + 1, :width]


def first_kernel(
    devices,
    widths,
    me_ref,
    ids_hbm,
    crop_hbm,
    ln_in_hbm,
    ln_out_hbm,
    w_proj_hbm,
    w_gate_hbm,
    pair_hbm,
    choice_ref,
    info_ref,
    flat_ref,
    gate_ref,
    send_ref,
    ids_ref,
    crop_ref,
    ln_in_ref,
    ln_out_ref,
    w_proj_ref,
    w_gate_ref,
    pair_ref,
    normed_ref,
    weights_ref,
    arrived,
):
    moves = (
        (pair_hbm, pair_ref),
        (w_proj_hbm.at[0], w_proj_ref),
        (ids_hbm, ids_ref),
        (crop_hbm, crop_ref),
        (ln_in_hbm, ln_in_ref),
        (ln_out_hbm, ln_out_ref),
        (w_gate_hbm.at[0], w_gate_ref),
    )
    copies = [
        pltpu.make_async_copy(source, target, arrived.at[index])
        for index, (source, target) in enumerate(moves)
    ]
    for copy in copies:
        copy.start()
    rows, count, depth = pair_ref.shape
    flat_ref[...] = jnp.zeros(flat_ref.shape, BF16)
    normed_ref[...] = jnp.zeros(normed_ref.shape, BF16)
    info_ref[...] = jnp.zeros(info_ref.shape, F32)
    square = (count, count)
    up = lax.broadcasted_iota(jnp.int32, square, 0) < lax.broadcasted_iota(jnp.int32, square, 1)
    up = jnp.where(up, 1.0, 0.0).astype(BF16)
    for copy in copies:
        copy.wait()
    kept = kept_residues(ids_ref[...], crop_ref[...])
    total = jnp.sum(kept)
    choice = jnp.int32(0)
    width = jnp.int32(widths[0])
    for some, wider in zip(widths[:-1], widths[1:]):
        choice = choice + jnp.where(total > some, 1, 0).astype(jnp.int32)
        width = width + jnp.where(total > some, wider - some, 0).astype(jnp.int32)
    choice_ref[0] = choice
    rank = dot_nn(jnp.broadcast_to(kept, (8, count)).astype(BF16), up)[0:1]
    slots = jnp.where(kept > 0.0, rank, -1.0)
    pick = selection(slots, count)
    gain = ln_in_ref[0:1]
    lanes = [pair_ref[row] for row in range(rows)]
    lanes = lanes + [norm_rows(part.astype(F32), gain) for part in lanes]
    sort_projection(w_proj_ref, devices, weights_ref)
    packed = move(pick, jnp.concatenate(lanes, axis=1))
    for row in range(rows):
        here = pl.ds(pl.multiple_of(row * width, 16), count)
        flat_ref[here] = packed[:, row * depth : (row + 1) * depth]
        normed_ref[here] = packed[:, (rows + row) * depth : (rows + row + 1) * depth]
    place = lax.broadcasted_iota(jnp.int32, kept.shape, 1)
    for row in range(rows):
        own = jnp.where(place == me_ref[0] * rows + row, kept, 0.0)
        info_ref[ROWS + row : ROWS + row + 1] = jnp.broadcast_to(
            jnp.sum(own, axis=1, keepdims=True), kept.shape
        )
    info_ref[0:1] = slots
    info_ref[1:2] = dot_nt(
        jnp.broadcast_to(slots, (8, count)).astype(BF16), interleave(rows, devices)
    )[0:1]
    info_ref[LN_IN : LN_IN + 2, :depth] = ln_in_ref[...]
    info_ref[LN_OUT : LN_OUT + 2, : ln_out_ref.shape[1]] = ln_out_ref[...]
    w_gate = halved(w_gate_ref[...])
    for start, span in spans(rows * count):
        project(
            normed_ref[start : start + span],
            weights_ref[...],
            w_gate,
            info_ref,
            gate_ref,
            send_ref,
            rows,
            width,
            start,
        )


def channel_blocks(came_ref, rows, width):
    devices, channels, total = came_ref.shape
    came = move(
        interleave(channels, devices), came_ref[...].reshape(devices * channels, total)
    )
    blocks = []
    for channel in range(channels):
        span = slice(channel * devices, (channel + 1) * devices)
        parts = [came[span, row * width : (row + 1) * width] for row in range(rows)]
        blocks.append(jnp.concatenate(parts, axis=0))
    return blocks


def outgoing_kernel(rows, groups, info_ref, came_ref, w_proj_ref, send_ref, sorted_ref):
    devices, both, total = came_ref.shape
    own = both // 2
    width = total // rows
    pick = selection(info_ref[1:2], width)
    blocks = channel_blocks(came_ref, rows, width)
    products = [
        dot_nt(blocks[channel], move(pick, blocks[own + channel])).astype(BF16)
        for channel in range(own)
    ]
    low = rows * own // 8
    to_device = interleave(devices, 8)
    for offset in range(low):
        parts = []
        for channel in range(own):
            for high in range(rows // low):
                row = high * low + offset
                parts.append(products[channel][row * devices : (row + 1) * devices])
        sent = move(to_device, jnp.concatenate(parts, axis=0))
        send_ref[:, :, offset * width : (offset + 1) * width] = sent.reshape(devices, 8, width)
    sort_projection(w_proj_ref.at[1], devices // groups, sorted_ref)


def incoming_kernel(rows, info_ref, came_ref, send_ref):
    own = came_ref.shape[1] // 2
    devices = send_ref.shape[0]
    width = came_ref.shape[2] // rows
    pick = selection(info_ref[1:2], width)
    pick = dot_nt(interleave(1, rows * devices), pick).astype(BF16)
    blocks = channel_blocks(came_ref, rows, width)
    products = [
        move(pick, dot_tn(blocks[channel], blocks[own + channel]).astype(BF16))
        for channel in range(own)
    ]
    to_device = interleave(devices, own)
    for row in range(rows):
        span = slice(row * devices, (row + 1) * devices)
        sent = move(to_device, jnp.concatenate([product[span] for product in products], axis=0))
        send_ref[:, :, row * width : (row + 1) * width] = sent.reshape(devices, own, width)


def finish_parts(layer, groups, info_ref, came_ref, flat_ref, gate_ref, w_out_ref, use):
    devices, eight, lanes = came_ref.shape
    hidden = w_out_ref.shape[1]
    high = devices * eight // hidden // groups
    square = lax.broadcasted_iota(jnp.int32, (hidden, hidden), 0) == lax.broadcasted_iota(
        jnp.int32, (hidden, hidden), 1
    )
    gain = gain_of(info_ref, LN_OUT + layer, hidden)
    gain = jnp.sum(jnp.where(square, gain, 0.0), axis=1, keepdims=True)
    w_out = halved(w_out_ref[layer])
    for offset, span in spans(lanes):
        came = came_ref[:, :, offset : offset + span].reshape(devices * eight, span)
        if groups == 1:
            came = dot_nn(interleave(high, hidden), came)
        else:
            came = came.astype(F32)
            came = sum(came[hidden * group : hidden * (group + 1)] for group in range(groups))
        for part in range(high):
            block = came[part * hidden : (part + 1) * hidden]
            centre = jnp.mean(block, axis=0, keepdims=True)
            apart = block - centre
            spread = jnp.mean(apart * apart, axis=0, keepdims=True)
            normed = (apart * lax.rsqrt(spread + epsilon_norm) * gain).astype(BF16)
            term = dot_tn(normed, w_out)
            start = part * lanes + offset
            here = slice(start, start + span)
            use(start, (flat_ref[here].astype(F32) + gate_ref[here] * term).astype(BF16))


def middle_kernel(
    rows,
    info_ref,
    came_ref,
    flat_ref,
    gate_ref,
    w_out_ref,
    weights_ref,
    w_gate_ref,
    next_ref,
    next_gate_ref,
    send_ref,
):
    gain = gain_of(info_ref, LN_IN + 1, flat_ref.shape[1])
    width = next_ref.shape[0] // rows

    def use(start, fresh):
        next_ref[start : start + fresh.shape[0]] = fresh

    finish_parts(0, 1, info_ref, came_ref, flat_ref, gate_ref, w_out_ref, use)
    w_gate = halved(w_gate_ref[1])
    for start, span in spans(rows * width):
        project(
            norm_rows(next_ref[start : start + span].astype(F32), gain),
            weights_ref[...],
            w_gate,
            info_ref,
            next_gate_ref,
            send_ref,
            rows,
            width,
            start,
        )


def last_kernel(
    groups,
    info_ref,
    pair_ref,
    came_ref,
    flat_ref,
    gate_ref,
    w_out_ref,
    out_ref,
    next_ref,
):
    rows, count, depth = out_ref.shape
    width = flat_ref.shape[0] // rows

    def use(start, fresh):
        next_ref[start : start + fresh.shape[0]] = fresh

    finish_parts(1, groups, info_ref, came_ref, flat_ref, gate_ref, w_out_ref, use)
    pick = selection(info_ref[0:1], width)
    pick = dot_nt(interleave(1, count), pick).astype(BF16)
    lanes = [next_ref[row * width : (row + 1) * width] for row in range(rows)]
    lanes.append(jnp.ones((width, depth), BF16))
    spread = dot_nn(pick, jnp.concatenate(lanes, axis=1))
    kept = spread[:, rows * depth :] > 0.5
    for row in range(rows):
        fresh = spread[:, row * depth : (row + 1) * depth]
        out_ref[row] = jnp.where(kept, fresh, pair_ref[row].astype(F32)).astype(BF16)


SMEM = pl.BlockSpec(memory_space=pltpu.SMEM)
HBM = pl.BlockSpec(memory_space=pltpu.HBM)


VMEM = pl.BlockSpec(memory_space=pltpu.VMEM)


def call(body, name, outs, operands, specs=None, out_specs=None, scratch=()):
    return pl.pallas_call(
        body,
        out_shape=list(outs),
        in_specs=specs or [VMEM] * len(operands),
        out_specs=out_specs or [VMEM] * len(outs),
        scratch_shapes=list(scratch),
        compiler_params=pltpu.CompilerParams(vmem_limit_bytes=24 * 1024 * 1024),
        name=name,
    )(*operands)


def kept_columns(width, pair_rep, info, flat, gate, sent, w_proj, w_gate, w_out):
    devices = lax.axis_size("dap")
    rows, _, depth = pair_rep.shape
    hidden = w_out.shape[1]
    own = hidden // devices
    back_shape = jax.ShapeDtypeStruct((devices, 8, rows * own * width // 8), BF16)
    flat_shape = jax.ShapeDtypeStruct((rows * width, depth), BF16)
    gate_shape = jax.ShapeDtypeStruct((rows * width, depth), F32)
    sorted_shape = jax.ShapeDtypeStruct((4 * hidden, depth), BF16)

    apart = devices // GROUPS
    groups = [list(range(first, first + apart)) for first in range(0, devices, apart)]
    group_shape = jax.ShapeDtypeStruct((apart, 2 * own * GROUPS, rows * width), BF16)
    sums_shape = jax.ShapeDtypeStruct((devices, own * GROUPS, rows * width), BF16)

    def exchange(sent, within=None):
        return lax.all_to_all(
            sent, "dap", split_axis=0, concat_axis=0, axis_index_groups=within, tiled=True
        )

    sent = sent[:, :, : rows * width]
    came = exchange(sent)
    sent, weights = call(
        functools.partial(outgoing_kernel, rows, GROUPS),
        "outgoing",
        [back_shape, sorted_shape],
        (info, came, w_proj),
    )
    came = exchange(sent)
    flat, gate, sent = call(
        functools.partial(middle_kernel, rows),
        "finish_and_operands",
        [flat_shape, gate_shape, group_shape],
        (info, came, flat, gate, w_out, weights, w_gate),
    )
    came = exchange(sent, groups)
    sent = call(
        functools.partial(incoming_kernel, rows),
        "incoming",
        [sums_shape],
        (info, came),
    )[0]
    came = exchange(sent)
    return call(
        functools.partial(last_kernel, GROUPS),
        "finish",
        [jax.ShapeDtypeStruct(pair_rep.shape, BF16)],
        (info, pair_rep, came, flat, gate, w_out),
        scratch=[pltpu.VMEM(flat_shape.shape, BF16)],
    )[0]


def row_shards(pair_rep, chain_ids, crop_lengths, ln_in_gain, w_proj, w_gate, ln_out_gain, w_out):
    devices = lax.axis_size("dap")
    rows, count, depth = pair_rep.shape
    me = lax.axis_index("dap").reshape(1).astype(jnp.int32)
    ids = chain_ids.reshape(1, count)
    crops = crop_lengths.reshape(1, -1)
    widths = [count * share // 16 for share in SHARES]
    info_shape = jax.ShapeDtypeStruct((16, count), F32)
    flat_shape = jax.ShapeDtypeStruct((rows * count, depth), BF16)
    send_shape = jax.ShapeDtypeStruct((devices, w_proj.shape[2] // devices // 2, rows * count), BF16)
    gate_shape = jax.ShapeDtypeStruct(flat_shape.shape, F32)
    choice, info, flat, gate, sent = call(
        functools.partial(first_kernel, devices, widths),
        "first_operands",
        [
            pltpu.SMEM((1,), jnp.int32),
            info_shape,
            flat_shape,
            gate_shape,
            send_shape,
        ],
        [me]
        + [
            pltpu.with_memory_space_constraint(array, pltpu.HBM)
            for array in (ids, crops, ln_in_gain, ln_out_gain, w_proj, w_gate, pair_rep)
        ],
        specs=[SMEM] + [HBM] * 7,
        out_specs=[SMEM] + [VMEM] * 4,
        scratch=[
            pltpu.VMEM(ids.shape, jnp.int32),
            pltpu.VMEM(crops.shape, jnp.int32),
            pltpu.VMEM(ln_in_gain.shape, F32),
            pltpu.VMEM(ln_out_gain.shape, F32),
            pltpu.VMEM(w_proj.shape[1:], BF16),
            pltpu.VMEM(w_gate.shape[1:], BF16),
            pltpu.VMEM(pair_rep.shape, BF16),
            pltpu.VMEM(flat_shape.shape, BF16),
            pltpu.VMEM((w_proj.shape[2], depth), BF16),
            pltpu.SemaphoreType.DMA((7,)),
        ],
    )
    return lax.switch(
        choice[0],
        [functools.partial(kept_columns, some) for some in widths],
        pair_rep,
        info,
        flat,
        gate,
        sent,
        w_proj,
        w_gate,
        w_out,
    )


GROUPS = 2
SHARES = (11, 12, 13, 14, 16)


def solution(mesh):
    devices = mesh.shape["dap"]
    placed = (P("dap", "grp", None), P(), P(), P(), P(), P(), P(), P())

    def body(*arrays):
        rows, count, width = arrays[0].shape
        hidden = arrays[-1].shape[1]
        plain = (
            mesh.shape["grp"] == 1
            and rows * devices == count
            and count == 256
            and rows == 8
            and hidden == 4 * devices
        )
        return (row_shards if plain else shards)(*arrays)

    return jax.shard_map(
        body, mesh=mesh, in_specs=placed, out_specs=P("dap", "grp", None), check_vma=False
    )
```

```python
import functools

import jax
import jax.numpy as jnp
from jax import lax
from jax.experimental import pallas as pl
from jax.experimental.pallas import tpu as pltpu
from jax.sharding import PartitionSpec as P

epsilon_norm = 1e-05
F32 = jnp.float32
BF16 = jnp.bfloat16


def residue_valid(chain_ids, crop_lengths):
    count = chain_ids.shape[0]
    chains = jnp.arange(crop_lengths.shape[0], dtype=jnp.int32)
    member = (chain_ids[:, None] == chains[None, :]).astype(jnp.int32)
    counts = jnp.sum(member, axis=0)
    starts = jnp.cumsum(counts) - counts
    first = jnp.sum(member * starts[None, :], axis=1)
    limit = jnp.sum(member * crop_lengths[None, :], axis=1)
    place = jnp.arange(count, dtype=jnp.int32) - first
    return (place < limit).astype(jnp.float32)


def layer_norm(values, gain, axis):
    centre = jnp.mean(values, axis=axis, keepdims=True)
    spread = jnp.mean((values - centre) ** 2, axis=axis, keepdims=True)
    return (values - centre) * lax.rsqrt(spread + epsilon_norm) * gain


def column_rows(right_chan):
    return lax.all_to_all(right_chan, "grp", split_axis=1, concat_axis=2, tiled=True)


def update(pair_tile, pair_mask, ln_in, w_proj, w_gate, ln_out, w_out, outgoing):
    hidden = w_out.shape[0]
    normed = layer_norm(pair_tile.astype(jnp.float32), ln_in, 2).astype(jnp.bfloat16)
    projected = jnp.einsum("rqc,cf->frq", normed, w_proj, preferred_element_type=jnp.float32)
    gate_value = jax.nn.sigmoid(
        jnp.einsum("rqc,cd->rqd", normed, w_gate, preferred_element_type=jnp.float32)
    )
    left_op = (
        jax.nn.sigmoid(projected[:hidden]) * projected[hidden : 2 * hidden] * pair_mask
    ).astype(jnp.bfloat16)
    right_op = (
        jax.nn.sigmoid(projected[2 * hidden : 3 * hidden]) * projected[3 * hidden :] * pair_mask
    ).astype(jnp.bfloat16)
    left_chan, right_chan = (
        lax.all_to_all(left_op, "dap", split_axis=0, concat_axis=1, tiled=True),
        lax.all_to_all(right_op, "dap", split_axis=0, concat_axis=1, tiled=True),
    )
    if outgoing:
        right_rows = column_rows(right_chan)
        triangle = jnp.einsum(
            "hik,hjk->hij",
            lax.all_gather(left_chan, "grp", axis=2, tiled=True),
            right_rows,
            preferred_element_type=jnp.float32,
        )
    else:
        triangle = jnp.einsum(
            "hki,hkj->hij",
            lax.all_gather(left_chan, "grp", axis=2, tiled=True),
            right_chan,
            preferred_element_type=jnp.float32,
        )
    returned = lax.all_to_all(
        triangle.astype(jnp.bfloat16), "dap", split_axis=1, concat_axis=0, tiled=True
    )
    normed_product = layer_norm(returned.astype(jnp.float32), ln_out[:, None, None], 0).astype(
        jnp.bfloat16
    )
    update_term = jnp.einsum(
        "hrq,hd->rqd", normed_product, w_out, preferred_element_type=jnp.float32
    )
    return (pair_tile.astype(jnp.float32) + gate_value * update_term).astype(jnp.bfloat16)


def shards(pair_rep, chain_ids, crop_lengths, ln_in_gain, w_proj, w_gate, ln_out_gain, w_out):
    row_count = pair_rep.shape[0]
    column_count = pair_rep.shape[1]
    kept = residue_valid(chain_ids, crop_lengths)
    row_start = lax.axis_index("dap") * row_count
    column_start = lax.axis_index("grp") * column_count
    kept_rows = lax.dynamic_slice_in_dim(kept, row_start, row_count, 0)
    kept_columns = lax.dynamic_slice_in_dim(kept, column_start, column_count, 0)
    pair_mask = kept_rows[:, None] * kept_columns[None, :]
    pair_tile = pair_rep
    for layer_index, outgoing in ((0, True), (1, False)):
        pair_tile = update(
            pair_tile,
            pair_mask,
            ln_in_gain[layer_index],
            w_proj[layer_index],
            w_gate[layer_index],
            ln_out_gain[layer_index],
            w_out[layer_index],
            outgoing,
        )
    return pair_tile


def dot_nn(a, b):
    return lax.dot_general(a, b, (((1,), (0,)), ((), ())), preferred_element_type=F32)


def dot_nt(a, b):
    return lax.dot_general(a, b, (((1,), (1,)), ((), ())), preferred_element_type=F32)


def dot_tn(a, b):
    return lax.dot_general(a, b, (((0,), (0,)), ((), ())), preferred_element_type=F32)


def open_gate(half):
    return jnp.tanh(half) + 1.0


def halved(weights):
    return (weights.astype(F32) * 0.5).astype(BF16)


def one_hot(source, columns):
    place = lax.broadcasted_iota(jnp.int32, (source.shape[0], columns), 1)
    return jnp.where(place == source, 1.0, 0.0).astype(BF16)


def interleave(outer, inner):
    row = lax.broadcasted_iota(jnp.int32, (outer * inner, 1), 0)
    return one_hot((row % inner) * outer + row // inner, outer * inner)


def move(matrix, rows):
    return dot_nn(matrix, rows).astype(BF16)


def selection(slots, width):
    row = lax.broadcasted_iota(jnp.int32, (width, slots.shape[1]), 0).astype(F32)
    return jnp.where(row == slots, 1.0, 0.0).astype(BF16)


def kept_residues(ids, limits):
    place = lax.broadcasted_iota(jnp.int32, ids.shape, 1).astype(F32)
    kept = jnp.zeros(ids.shape, F32)
    for chain in range(limits.shape[1]):
        first = jnp.sum(jnp.where(ids < chain, 1.0, 0.0), axis=1, keepdims=True)
        limit = limits[:, chain : chain + 1].astype(F32)
        inside = jnp.where(ids == chain, 1.0, 0.0) * jnp.where(place - first < limit, 1.0, 0.0)
        kept = kept + inside
    return kept


def norm_rows(values, gain):
    centre = jnp.mean(values, axis=1, keepdims=True)
    apart = values - centre
    spread = jnp.mean(apart * apart, axis=1, keepdims=True)
    return (apart * lax.rsqrt(spread + epsilon_norm) * gain).astype(BF16)


def sort_projection(w_proj_ref, devices, sorted_ref):
    hidden = w_proj_ref.shape[1] // 4
    own = hidden // devices
    row = lax.broadcasted_iota(jnp.int32, (2 * hidden, 1), 0)
    side = (row % (2 * own)) // own
    order = one_hot(side * hidden + row // (2 * own) * own + row % own, 2 * hidden)
    for kind in range(2):
        sides = [
            w_proj_ref[:, block * hidden : (block + 1) * hidden] for block in (kind, kind + 2)
        ]
        rows = dot_nt(order, jnp.concatenate(sides, axis=1)) * 0.5
        sorted_ref[2 * hidden * kind : 2 * hidden * (kind + 1)] = rows.astype(BF16)


def project(normed, weights, w_gate, info_ref, gate_ref, send_ref, rows, width, start):
    span = normed.shape[0]
    half = weights.shape[0] // 2
    place = start + lax.broadcasted_iota(jnp.int32, (1, span), 1)
    mask = jnp.zeros((1, span), F32)
    for row in range(rows):
        if isinstance(width, int) and not start - width < row * width < start + span:
            continue
        inside = jnp.where(place >= row * width, 1.0, 0.0)
        inside = inside * jnp.where(place < (row + 1) * width, 1.0, 0.0)
        mask = mask + inside * info_ref[ROWS + row : ROWS + row + 1, 0:1]
    gate_ref[start : start + span] = open_gate(dot_nn(normed, w_gate))
    projected = dot_nt(weights, normed)
    operand = open_gate(projected[:half]) * projected[half:] * mask
    shape = send_ref.shape[:2] + (span,)
    send_ref[:, :, start : start + span] = operand.astype(BF16).reshape(shape)


def spans(total):
    start = 0
    while start < total:
        span = min(256, total - start)
        yield start, span
        start += span


LN_IN, LN_OUT, ROWS = 2, 4, 8


def gain_of(info_ref, row, width):
    return info_ref[row : row + 1, :width]


def first_kernel(
    devices,
    widths,
    me_ref,
    ids_hbm,
    crop_hbm,
    ln_in_hbm,
    ln_out_hbm,
    w_proj_hbm,
    w_gate_hbm,
    pair_hbm,
    choice_ref,
    info_ref,
    flat_ref,
    gate_ref,
    send_ref,
    ids_ref,
    crop_ref,
    ln_in_ref,
    ln_out_ref,
    w_proj_ref,
    w_gate_ref,
    pair_ref,
    normed_ref,
    weights_ref,
    arrived,
):
    moves = (
        (ids_hbm, ids_ref),
        (crop_hbm, crop_ref),
        (ln_in_hbm, ln_in_ref),
        (ln_out_hbm, ln_out_ref),
        (pair_hbm, pair_ref),
        (w_proj_hbm.at[0], w_proj_ref),
        (w_gate_hbm.at[0], w_gate_ref),
    )
    copies = [
        pltpu.make_async_copy(source, target, arrived.at[index])
        for index, (source, target) in enumerate(moves)
    ]
    for copy in copies:
        copy.start()
    rows, count, depth = pair_ref.shape
    flat_ref[...] = jnp.zeros(flat_ref.shape, BF16)
    normed_ref[...] = jnp.zeros(normed_ref.shape, BF16)
    info_ref[...] = jnp.zeros(info_ref.shape, F32)
    square = (count, count)
    up = lax.broadcasted_iota(jnp.int32, square, 0) < lax.broadcasted_iota(jnp.int32, square, 1)
    up = jnp.where(up, 1.0, 0.0).astype(BF16)
    by_row = interleave(rows, devices)
    for copy in copies[:4]:
        copy.wait()
    kept = kept_residues(ids_ref[...], crop_ref[...])
    total = jnp.sum(kept)
    choice = jnp.int32(0)
    width = jnp.int32(widths[0])
    for some, wider in zip(widths[:-1], widths[1:]):
        choice = choice + jnp.where(total > some, 1, 0).astype(jnp.int32)
        width = width + jnp.where(total > some, wider - some, 0).astype(jnp.int32)
    choice_ref[0] = choice
    place = lax.broadcasted_iota(jnp.int32, kept.shape, 1)
    for row in range(rows):
        own = jnp.where(place == me_ref[0] * rows + row, kept, 0.0)
        info_ref[ROWS + row : ROWS + row + 1] = jnp.broadcast_to(
            jnp.sum(own, axis=1, keepdims=True), kept.shape
        )
    rank = dot_nn(jnp.broadcast_to(kept, (8, count)).astype(BF16), up)[0:1]
    slots = jnp.where(kept > 0.0, rank, -1.0)
    info_ref[0:1] = slots
    info_ref[1:2] = dot_nt(jnp.broadcast_to(slots, (8, count)).astype(BF16), by_row)[0:1]
    info_ref[LN_IN : LN_IN + 2, :depth] = ln_in_ref[...]
    info_ref[LN_OUT : LN_OUT + 2, : ln_out_ref.shape[1]] = ln_out_ref[...]
    pick = selection(slots, count)
    for copy in copies[4:]:
        copy.wait()
    gain = ln_in_ref[0:1]
    lanes = [pair_ref[row] for row in range(rows)]
    lanes = lanes + [norm_rows(part.astype(F32), gain) for part in lanes]
    sort_projection(w_proj_ref, devices, weights_ref)
    packed = move(pick, jnp.concatenate(lanes, axis=1))
    for row in range(rows):
        here = pl.ds(pl.multiple_of(row * width, 16), count)
        flat_ref[here] = packed[:, row * depth : (row + 1) * depth]
        normed_ref[here] = packed[:, (rows + row) * depth : (rows + row + 1) * depth]
    w_gate = halved(w_gate_ref[...])
    for start, span in spans(rows * count):
        project(
            normed_ref[start : start + span],
            weights_ref[...],
            w_gate,
            info_ref,
            gate_ref,
            send_ref,
            rows,
            width,
            start,
        )


def channel_blocks(came_ref, rows, width):
    devices, channels, total = came_ref.shape
    came = move(
        interleave(channels, devices), came_ref[...].reshape(devices * channels, total)
    )
    blocks = []
    for channel in range(channels):
        span = slice(channel * devices, (channel + 1) * devices)
        parts = [came[span, row * width : (row + 1) * width] for row in range(rows)]
        blocks.append(jnp.concatenate(parts, axis=0))
    return blocks


def outgoing_kernel(rows, groups, info_ref, came_ref, w_proj_ref, send_ref, sorted_ref):
    devices, both, total = came_ref.shape
    own = both // 2
    width = total // rows
    pick = selection(info_ref[1:2], width)
    blocks = channel_blocks(came_ref, rows, width)
    products = [
        dot_nt(blocks[channel], move(pick, blocks[own + channel])).astype(BF16)
        for channel in range(own)
    ]
    low = rows * own // 8
    to_device = interleave(devices, 8)
    for offset in range(low):
        parts = []
        for channel in range(own):
            for high in range(rows // low):
                row = high * low + offset
                parts.append(products[channel][row * devices : (row + 1) * devices])
        sent = move(to_device, jnp.concatenate(parts, axis=0))
        send_ref[:, :, offset * width : (offset + 1) * width] = sent.reshape(devices, 8, width)
    sort_projection(w_proj_ref.at[1], devices // groups, sorted_ref)


def incoming_kernel(rows, info_ref, came_ref, send_ref):
    own = came_ref.shape[1] // 2
    devices = send_ref.shape[0]
    width = came_ref.shape[2] // rows
    pick = selection(info_ref[1:2], width)
    pick = dot_nt(interleave(1, rows * devices), pick).astype(BF16)
    blocks = channel_blocks(came_ref, rows, width)
    products = [
        move(pick, dot_tn(blocks[channel], blocks[own + channel]).astype(BF16))
        for channel in range(own)
    ]
    to_device = interleave(devices, own)
    for row in range(rows):
        span = slice(row * devices, (row + 1) * devices)
        sent = move(to_device, jnp.concatenate([product[span] for product in products], axis=0))
        send_ref[:, :, row * width : (row + 1) * width] = sent.reshape(devices, own, width)


def finish_parts(layer, groups, info_ref, came_ref, flat_ref, gate_ref, w_out_ref, use):
    devices, eight, lanes = came_ref.shape
    hidden = w_out_ref.shape[1]
    high = devices * eight // hidden // groups
    square = lax.broadcasted_iota(jnp.int32, (hidden, hidden), 0) == lax.broadcasted_iota(
        jnp.int32, (hidden, hidden), 1
    )
    gain = gain_of(info_ref, LN_OUT + layer, hidden)
    gain = jnp.sum(jnp.where(square, gain, 0.0), axis=1, keepdims=True)
    w_out = halved(w_out_ref[layer])
    for offset, span in spans(lanes):
        came = came_ref[:, :, offset : offset + span].reshape(devices * eight, span)
        if groups == 1:
            came = dot_nn(interleave(high, hidden), came)
        else:
            came = came.astype(F32)
            came = sum(came[hidden * group : hidden * (group + 1)] for group in range(groups))
        for part in range(high):
            block = came[part * hidden : (part + 1) * hidden]
            centre = jnp.mean(block, axis=0, keepdims=True)
            apart = block - centre
            spread = jnp.mean(apart * apart, axis=0, keepdims=True)
            normed = (apart * lax.rsqrt(spread + epsilon_norm) * gain).astype(BF16)
            term = dot_tn(normed, w_out)
            start = part * lanes + offset
            here = slice(start, start + span)
            use(start, (flat_ref[here].astype(F32) + gate_ref[here] * term).astype(BF16))


def middle_kernel(
    rows,
    info_ref,
    came_ref,
    flat_ref,
    gate_ref,
    w_out_ref,
    weights_ref,
    w_gate_ref,
    next_ref,
    next_gate_ref,
    send_ref,
):
    gain = gain_of(info_ref, LN_IN + 1, flat_ref.shape[1])
    width = next_ref.shape[0] // rows

    def use(start, fresh):
        next_ref[start : start + fresh.shape[0]] = fresh

    finish_parts(0, 1, info_ref, came_ref, flat_ref, gate_ref, w_out_ref, use)
    w_gate = halved(w_gate_ref[1])
    for start, span in spans(rows * width):
        project(
            norm_rows(next_ref[start : start + span].astype(F32), gain),
            weights_ref[...],
            w_gate,
            info_ref,
            next_gate_ref,
            send_ref,
            rows,
            width,
            start,
        )


def last_kernel(
    groups,
    info_ref,
    pair_ref,
    came_ref,
    flat_ref,
    gate_ref,
    w_out_ref,
    out_ref,
    next_ref,
):
    rows, count, depth = out_ref.shape
    width = flat_ref.shape[0] // rows

    def use(start, fresh):
        next_ref[start : start + fresh.shape[0]] = fresh

    finish_parts(1, groups, info_ref, came_ref, flat_ref, gate_ref, w_out_ref, use)
    pick = selection(info_ref[0:1], width)
    pick = dot_nt(interleave(1, count), pick).astype(BF16)
    lanes = [next_ref[row * width : (row + 1) * width] for row in range(rows)]
    lanes.append(jnp.ones((width, depth), BF16))
    spread = dot_nn(pick, jnp.concatenate(lanes, axis=1))
    kept = spread[:, rows * depth :] > 0.5
    for row in range(rows):
        fresh = spread[:, row * depth : (row + 1) * depth]
        out_ref[row] = jnp.where(kept, fresh, pair_ref[row].astype(F32)).astype(BF16)


SMEM = pl.BlockSpec(memory_space=pltpu.SMEM)
HBM = pl.BlockSpec(memory_space=pltpu.HBM)


VMEM = pl.BlockSpec(memory_space=pltpu.VMEM)


def call(body, name, outs, operands, specs=None, out_specs=None, scratch=()):
    return pl.pallas_call(
        body,
        out_shape=list(outs),
        in_specs=specs or [VMEM] * len(operands),
        out_specs=out_specs or [VMEM] * len(outs),
        scratch_shapes=list(scratch),
        compiler_params=pltpu.CompilerParams(vmem_limit_bytes=24 * 1024 * 1024),
        name=name,
    )(*operands)


def kept_columns(width, pair_rep, info, flat, gate, sent, w_proj, w_gate, w_out):
    devices = lax.axis_size("dap")
    rows, _, depth = pair_rep.shape
    hidden = w_out.shape[1]
    own = hidden // devices
    back_shape = jax.ShapeDtypeStruct((devices, 8, rows * own * width // 8), BF16)
    flat_shape = jax.ShapeDtypeStruct((rows * width, depth), BF16)
    gate_shape = jax.ShapeDtypeStruct((rows * width, depth), F32)
    sorted_shape = jax.ShapeDtypeStruct((4 * hidden, depth), BF16)

    apart = devices // GROUPS
    groups = [list(range(first, first + apart)) for first in range(0, devices, apart)]
    group_shape = jax.ShapeDtypeStruct((apart, 2 * own * GROUPS, rows * width), BF16)
    sums_shape = jax.ShapeDtypeStruct((devices, own * GROUPS, rows * width), BF16)

    def exchange(sent, within=None):
        return lax.all_to_all(
            sent, "dap", split_axis=0, concat_axis=0, axis_index_groups=within, tiled=True
        )

    sent = sent[:, :, : rows * width]
    came = exchange(sent)
    sent, weights = call(
        functools.partial(outgoing_kernel, rows, GROUPS),
        "outgoing",
        [back_shape, sorted_shape],
        (info, came, w_proj),
    )
    came = exchange(sent)
    flat, gate, sent = call(
        functools.partial(middle_kernel, rows),
        "finish_and_operands",
        [flat_shape, gate_shape, group_shape],
        (info, came, flat, gate, w_out, weights, w_gate),
    )
    came = exchange(sent, groups)
    sent = call(
        functools.partial(incoming_kernel, rows),
        "incoming",
        [sums_shape],
        (info, came),
    )[0]
    came = exchange(sent)
    return call(
        functools.partial(last_kernel, GROUPS),
        "finish",
        [jax.ShapeDtypeStruct(pair_rep.shape, BF16)],
        (info, pair_rep, came, flat, gate, w_out),
        scratch=[pltpu.VMEM(flat_shape.shape, BF16)],
    )[0]


def row_shards(pair_rep, chain_ids, crop_lengths, ln_in_gain, w_proj, w_gate, ln_out_gain, w_out):
    devices = lax.axis_size("dap")
    rows, count, depth = pair_rep.shape
    me = lax.axis_index("dap").reshape(1).astype(jnp.int32)
    ids = chain_ids.reshape(1, count)
    crops = crop_lengths.reshape(1, -1)
    widths = [count * share // 16 for share in SHARES]
    info_shape = jax.ShapeDtypeStruct((16, count), F32)
    flat_shape = jax.ShapeDtypeStruct((rows * count, depth), BF16)
    send_shape = jax.ShapeDtypeStruct((devices, w_proj.shape[2] // devices // 2, rows * count), BF16)
    gate_shape = jax.ShapeDtypeStruct(flat_shape.shape, F32)
    choice, info, flat, gate, sent = call(
        functools.partial(first_kernel, devices, widths),
        "first_operands",
        [
            pltpu.SMEM((1,), jnp.int32),
            info_shape,
            flat_shape,
            gate_shape,
            send_shape,
        ],
        [me]
        + [
            pltpu.with_memory_space_constraint(array, pltpu.HBM)
            for array in (ids, crops, ln_in_gain, ln_out_gain, w_proj, w_gate, pair_rep)
        ],
        specs=[SMEM] + [HBM] * 7,
        out_specs=[SMEM] + [VMEM] * 4,
        scratch=[
            pltpu.VMEM(ids.shape, jnp.int32),
            pltpu.VMEM(crops.shape, jnp.int32),
            pltpu.VMEM(ln_in_gain.shape, F32),
            pltpu.VMEM(ln_out_gain.shape, F32),
            pltpu.VMEM(w_proj.shape[1:], BF16),
            pltpu.VMEM(w_gate.shape[1:], BF16),
            pltpu.VMEM(pair_rep.shape, BF16),
            pltpu.VMEM(flat_shape.shape, BF16),
            pltpu.VMEM((w_proj.shape[2], depth), BF16),
            pltpu.SemaphoreType.DMA((7,)),
        ],
    )
    return lax.switch(
        choice[0],
        [functools.partial(kept_columns, some) for some in widths],
        pair_rep,
        info,
        flat,
        gate,
        sent,
        w_proj,
        w_gate,
        w_out,
    )


GROUPS = 2
SHARES = (11, 12, 13, 14, 16)


def solution(mesh):
    devices = mesh.shape["dap"]
    placed = (P("dap", "grp", None), P(), P(), P(), P(), P(), P(), P())

    def body(*arrays):
        rows, count, width = arrays[0].shape
        hidden = arrays[-1].shape[1]
        plain = (
            mesh.shape["grp"] == 1
            and rows * devices == count
            and count == 256
            and rows == 8
            and hidden == 4 * devices
        )
        return (row_shards if plain else shards)(*arrays)

    return jax.shard_map(
        body, mesh=mesh, in_specs=placed, out_specs=P("dap", "grp", None), check_vma=False
    )
```

```python
import functools

import jax
import jax.numpy as jnp
from jax import lax
from jax.experimental import pallas as pl
from jax.experimental.pallas import tpu as pltpu
from jax.sharding import PartitionSpec as P

epsilon_norm = 1e-05
F32 = jnp.float32
BF16 = jnp.bfloat16


def residue_valid(chain_ids, crop_lengths):
    count = chain_ids.shape[0]
    chains = jnp.arange(crop_lengths.shape[0], dtype=jnp.int32)
    member = (chain_ids[:, None] == chains[None, :]).astype(jnp.int32)
    counts = jnp.sum(member, axis=0)
    starts = jnp.cumsum(counts) - counts
    first = jnp.sum(member * starts[None, :], axis=1)
    limit = jnp.sum(member * crop_lengths[None, :], axis=1)
    place = jnp.arange(count, dtype=jnp.int32) - first
    return (place < limit).astype(jnp.float32)


def layer_norm(values, gain, axis):
    centre = jnp.mean(values, axis=axis, keepdims=True)
    spread = jnp.mean((values - centre) ** 2, axis=axis, keepdims=True)
    return (values - centre) * lax.rsqrt(spread + epsilon_norm) * gain


def column_rows(right_chan):
    return lax.all_to_all(right_chan, "grp", split_axis=1, concat_axis=2, tiled=True)


def update(pair_tile, pair_mask, ln_in, w_proj, w_gate, ln_out, w_out, outgoing):
    hidden = w_out.shape[0]
    normed = layer_norm(pair_tile.astype(jnp.float32), ln_in, 2).astype(jnp.bfloat16)
    projected = jnp.einsum("rqc,cf->frq", normed, w_proj, preferred_element_type=jnp.float32)
    gate_value = jax.nn.sigmoid(
        jnp.einsum("rqc,cd->rqd", normed, w_gate, preferred_element_type=jnp.float32)
    )
    left_op = (
        jax.nn.sigmoid(projected[:hidden]) * projected[hidden : 2 * hidden] * pair_mask
    ).astype(jnp.bfloat16)
    right_op = (
        jax.nn.sigmoid(projected[2 * hidden : 3 * hidden]) * projected[3 * hidden :] * pair_mask
    ).astype(jnp.bfloat16)
    left_chan, right_chan = (
        lax.all_to_all(left_op, "dap", split_axis=0, concat_axis=1, tiled=True),
        lax.all_to_all(right_op, "dap", split_axis=0, concat_axis=1, tiled=True),
    )
    if outgoing:
        right_rows = column_rows(right_chan)
        triangle = jnp.einsum(
            "hik,hjk->hij",
            lax.all_gather(left_chan, "grp", axis=2, tiled=True),
            right_rows,
            preferred_element_type=jnp.float32,
        )
    else:
        triangle = jnp.einsum(
            "hki,hkj->hij",
            lax.all_gather(left_chan, "grp", axis=2, tiled=True),
            right_chan,
            preferred_element_type=jnp.float32,
        )
    returned = lax.all_to_all(
        triangle.astype(jnp.bfloat16), "dap", split_axis=1, concat_axis=0, tiled=True
    )
    normed_product = layer_norm(returned.astype(jnp.float32), ln_out[:, None, None], 0).astype(
        jnp.bfloat16
    )
    update_term = jnp.einsum(
        "hrq,hd->rqd", normed_product, w_out, preferred_element_type=jnp.float32
    )
    return (pair_tile.astype(jnp.float32) + gate_value * update_term).astype(jnp.bfloat16)


def shards(pair_rep, chain_ids, crop_lengths, ln_in_gain, w_proj, w_gate, ln_out_gain, w_out):
    row_count = pair_rep.shape[0]
    column_count = pair_rep.shape[1]
    kept = residue_valid(chain_ids, crop_lengths)
    row_start = lax.axis_index("dap") * row_count
    column_start = lax.axis_index("grp") * column_count
    kept_rows = lax.dynamic_slice_in_dim(kept, row_start, row_count, 0)
    kept_columns = lax.dynamic_slice_in_dim(kept, column_start, column_count, 0)
    pair_mask = kept_rows[:, None] * kept_columns[None, :]
    pair_tile = pair_rep
    for layer_index, outgoing in ((0, True), (1, False)):
        pair_tile = update(
            pair_tile,
            pair_mask,
            ln_in_gain[layer_index],
            w_proj[layer_index],
            w_gate[layer_index],
            ln_out_gain[layer_index],
            w_out[layer_index],
            outgoing,
        )
    return pair_tile


def dot_nn(a, b):
    return lax.dot_general(a, b, (((1,), (0,)), ((), ())), preferred_element_type=F32)


def dot_nt(a, b):
    return lax.dot_general(a, b, (((1,), (1,)), ((), ())), preferred_element_type=F32)


def dot_tn(a, b):
    return lax.dot_general(a, b, (((0,), (0,)), ((), ())), preferred_element_type=F32)


def open_gate(half):
    return jnp.tanh(half) + 1.0


def halved(weights):
    return (weights.astype(F32) * 0.5).astype(BF16)


def one_hot(source, columns):
    place = lax.broadcasted_iota(jnp.int32, (source.shape[0], columns), 1)
    return jnp.where(place == source, 1.0, 0.0).astype(BF16)


def interleave(outer, inner):
    row = lax.broadcasted_iota(jnp.int32, (outer * inner, 1), 0)
    return one_hot((row % inner) * outer + row // inner, outer * inner)


def move(matrix, rows):
    return dot_nn(matrix, rows).astype(BF16)


def selection(slots, width):
    row = lax.broadcasted_iota(jnp.int32, (width, slots.shape[1]), 0).astype(F32)
    return jnp.where(row == slots, 1.0, 0.0).astype(BF16)


def kept_residues(ids, limits):
    place = lax.broadcasted_iota(jnp.int32, ids.shape, 1).astype(F32)
    kept = jnp.zeros(ids.shape, F32)
    for chain in range(limits.shape[1]):
        first = jnp.sum(jnp.where(ids < chain, 1.0, 0.0), axis=1, keepdims=True)
        limit = limits[:, chain : chain + 1].astype(F32)
        inside = jnp.where(ids == chain, 1.0, 0.0) * jnp.where(place - first < limit, 1.0, 0.0)
        kept = kept + inside
    return kept


def norm_rows(values, gain):
    centre = jnp.mean(values, axis=1, keepdims=True)
    apart = values - centre
    spread = jnp.mean(apart * apart, axis=1, keepdims=True)
    return (apart * lax.rsqrt(spread + epsilon_norm) * gain).astype(BF16)


def sort_projection(w_proj_ref, devices, sorted_ref):
    hidden = w_proj_ref.shape[1] // 4
    own = hidden // devices
    row = lax.broadcasted_iota(jnp.int32, (2 * hidden, 1), 0)
    side = (row % (2 * own)) // own
    order = one_hot(side * hidden + row // (2 * own) * own + row % own, 2 * hidden)
    for kind in range(2):
        sides = [
            w_proj_ref[:, block * hidden : (block + 1) * hidden] for block in (kind, kind + 2)
        ]
        rows = dot_nt(order, jnp.concatenate(sides, axis=1)) * 0.5
        sorted_ref[2 * hidden * kind : 2 * hidden * (kind + 1)] = rows.astype(BF16)


def project(normed, weights, w_gate, info_ref, gate_ref, send_ref, rows, width, start):
    span = normed.shape[0]
    half = weights.shape[0] // 2
    place = start + lax.broadcasted_iota(jnp.int32, (1, span), 1)
    mask = jnp.zeros((1, span), F32)
    for row in range(rows):
        if isinstance(width, int) and not start - width < row * width < start + span:
            continue
        inside = jnp.where(place >= row * width, 1.0, 0.0)
        inside = inside * jnp.where(place < (row + 1) * width, 1.0, 0.0)
        mask = mask + inside * info_ref[ROWS + row : ROWS + row + 1, 0:1]
    gate_ref[start : start + span] = open_gate(dot_nn(normed, w_gate))
    projected = dot_nt(weights, normed)
    operand = open_gate(projected[:half]) * projected[half:] * mask
    shape = send_ref.shape[:2] + (span,)
    send_ref[:, :, start : start + span] = operand.astype(BF16).reshape(shape)


def spans(total):
    start = 0
    while start < total:
        span = min(256, total - start)
        yield start, span
        start += span


LN_IN, LN_OUT, ROWS = 2, 4, 8


def gain_of(info_ref, row, width):
    return info_ref[row : row + 1, :width]


def first_kernel(
    devices,
    widths,
    me_ref,
    ids_hbm,
    crop_hbm,
    ln_in_hbm,
    ln_out_hbm,
    w_proj_hbm,
    w_gate_hbm,
    pair_hbm,
    choice_ref,
    info_ref,
    flat_ref,
    gate_ref,
    send_ref,
    ids_ref,
    crop_ref,
    ln_in_ref,
    ln_out_ref,
    w_proj_ref,
    w_gate_ref,
    pair_ref,
    normed_ref,
    weights_ref,
    arrived,
):
    moves = (
        (ids_hbm, ids_ref),
        (crop_hbm, crop_ref),
        (ln_in_hbm, ln_in_ref),
        (ln_out_hbm, ln_out_ref),
        (pair_hbm, pair_ref),
        (w_proj_hbm.at[0], w_proj_ref),
        (w_gate_hbm.at[0], w_gate_ref),
    )
    copies = [
        pltpu.make_async_copy(source, target, arrived.at[index])
        for index, (source, target) in enumerate(moves)
    ]
    for copy in copies:
        copy.start()
    rows, count, depth = pair_ref.shape
    flat_ref[...] = jnp.zeros(flat_ref.shape, BF16)
    normed_ref[...] = jnp.zeros(normed_ref.shape, BF16)
    info_ref[...] = jnp.zeros(info_ref.shape, F32)
    square = (count, count)
    up = lax.broadcasted_iota(jnp.int32, square, 0) < lax.broadcasted_iota(jnp.int32, square, 1)
    up = jnp.where(up, 1.0, 0.0).astype(BF16)
    by_row = interleave(rows, devices)
    for copy in copies[:4]:
        copy.wait()
    kept = kept_residues(ids_ref[...], crop_ref[...])
    total = jnp.sum(kept)
    choice = jnp.int32(0)
    width = jnp.int32(widths[0])
    for some, wider in zip(widths[:-1], widths[1:]):
        choice = choice + jnp.where(total > some, 1, 0).astype(jnp.int32)
        width = width + jnp.where(total > some, wider - some, 0).astype(jnp.int32)
    choice_ref[0] = choice
    place = lax.broadcasted_iota(jnp.int32, kept.shape, 1)
    for row in range(rows):
        own = jnp.where(place == me_ref[0] * rows + row, kept, 0.0)
        info_ref[ROWS + row : ROWS + row + 1] = jnp.broadcast_to(
            jnp.sum(own, axis=1, keepdims=True), kept.shape
        )
    rank = dot_nn(jnp.broadcast_to(kept, (8, count)).astype(BF16), up)[0:1]
    slots = jnp.where(kept > 0.0, rank, -1.0)
    info_ref[0:1] = slots
    info_ref[1:2] = dot_nt(jnp.broadcast_to(slots, (8, count)).astype(BF16), by_row)[0:1]
    info_ref[LN_IN : LN_IN + 2, :depth] = ln_in_ref[...]
    info_ref[LN_OUT : LN_OUT + 2, : ln_out_ref.shape[1]] = ln_out_ref[...]
    pick = selection(slots, count)
    for copy in copies[4:]:
        copy.wait()
    gain = ln_in_ref[0:1]
    lanes = [pair_ref[row] for row in range(rows)]
    lanes = lanes + [norm_rows(part.astype(F32), gain) for part in lanes]
    sort_projection(w_proj_ref, devices, weights_ref)
    packed = move(pick, jnp.concatenate(lanes, axis=1))
    for row in range(rows):
        here = pl.ds(pl.multiple_of(row * width, 16), count)
        flat_ref[here] = packed[:, row * depth : (row + 1) * depth]
        normed_ref[here] = packed[:, (rows + row) * depth : (rows + row + 1) * depth]
    w_gate = halved(w_gate_ref[...])
    for start, span in spans(rows * count):
        project(
            normed_ref[start : start + span],
            weights_ref[...],
            w_gate,
            info_ref,
            gate_ref,
            send_ref,
            rows,
            width,
            start,
        )


def channel_blocks(came_ref, rows, width):
    devices, channels, total = came_ref.shape
    came = move(
        interleave(channels, devices), came_ref[...].reshape(devices * channels, total)
    )
    blocks = []
    for channel in range(channels):
        span = slice(channel * devices, (channel + 1) * devices)
        parts = [came[span, row * width : (row + 1) * width] for row in range(rows)]
        blocks.append(jnp.concatenate(parts, axis=0))
    return blocks


def outgoing_kernel(rows, groups, info_ref, came_ref, w_proj_ref, send_ref, sorted_ref):
    devices, both, total = came_ref.shape
    own = both // 2
    width = total // rows
    pick = selection(info_ref[1:2], width)
    blocks = channel_blocks(came_ref, rows, width)
    products = [
        dot_nt(blocks[channel], move(pick, blocks[own + channel])).astype(BF16)
        for channel in range(own)
    ]
    low = rows * own // 8
    to_device = interleave(devices, 8)
    for offset in range(low):
        parts = []
        for channel in range(own):
            for high in range(rows // low):
                row = high * low + offset
                parts.append(products[channel][row * devices : (row + 1) * devices])
        sent = move(to_device, jnp.concatenate(parts, axis=0))
        send_ref[:, :, offset * width : (offset + 1) * width] = sent.reshape(devices, 8, width)
    sort_projection(w_proj_ref.at[1], devices // groups, sorted_ref)


def incoming_kernel(rows, info_ref, came_ref, send_ref):
    own = came_ref.shape[1] // 2
    devices = send_ref.shape[0]
    width = came_ref.shape[2] // rows
    pick = selection(info_ref[1:2], width)
    pick = dot_nt(interleave(1, rows * devices), pick).astype(BF16)
    blocks = channel_blocks(came_ref, rows, width)
    products = [
        dot_nn(dot_nt(pick, blocks[channel]).astype(BF16), blocks[own + channel]).astype(BF16)
        for channel in range(own)
    ]
    to_device = interleave(devices, own)
    for row in range(rows):
        span = slice(row * devices, (row + 1) * devices)
        sent = move(to_device, jnp.concatenate([product[span] for product in products], axis=0))
        send_ref[:, :, row * width : (row + 1) * width] = sent.reshape(devices, own, width)


def finish_parts(layer, groups, info_ref, came_ref, flat_ref, gate_ref, w_out_ref, use):
    devices, eight, lanes = came_ref.shape
    hidden = w_out_ref.shape[1]
    high = devices * eight // hidden // groups
    square = lax.broadcasted_iota(jnp.int32, (hidden, hidden), 0) == lax.broadcasted_iota(
        jnp.int32, (hidden, hidden), 1
    )
    gain = gain_of(info_ref, LN_OUT + layer, hidden)
    gain = jnp.sum(jnp.where(square, gain, 0.0), axis=1, keepdims=True)
    w_out = halved(w_out_ref[layer])
    for offset, span in spans(lanes):
        came = came_ref[:, :, offset : offset + span].reshape(devices * eight, span)
        if groups == 1:
            came = dot_nn(interleave(high, hidden), came)
        else:
            came = came.astype(F32)
            came = sum(came[hidden * group : hidden * (group + 1)] for group in range(groups))
        for part in range(high):
            block = came[part * hidden : (part + 1) * hidden]
            centre = jnp.mean(block, axis=0, keepdims=True)
            apart = block - centre
            spread = jnp.mean(apart * apart, axis=0, keepdims=True)
            normed = (apart * lax.rsqrt(spread + epsilon_norm) * gain).astype(BF16)
            term = dot_tn(normed, w_out)
            start = part * lanes + offset
            here = slice(start, start + span)
            use(start, (flat_ref[here].astype(F32) + gate_ref[here] * term).astype(BF16))


def middle_kernel(
    rows,
    info_ref,
    came_ref,
    flat_ref,
    gate_ref,
    w_out_ref,
    weights_ref,
    w_gate_ref,
    next_ref,
    next_gate_ref,
    send_ref,
):
    gain = gain_of(info_ref, LN_IN + 1, flat_ref.shape[1])
    width = next_ref.shape[0] // rows

    def use(start, fresh):
        next_ref[start : start + fresh.shape[0]] = fresh

    finish_parts(0, 1, info_ref, came_ref, flat_ref, gate_ref, w_out_ref, use)
    w_gate = halved(w_gate_ref[1])
    for start, span in spans(rows * width):
        project(
            norm_rows(next_ref[start : start + span].astype(F32), gain),
            weights_ref[...],
            w_gate,
            info_ref,
            next_gate_ref,
            send_ref,
            rows,
            width,
            start,
        )


def last_kernel(
    groups,
    info_ref,
    pair_ref,
    came_ref,
    flat_ref,
    gate_ref,
    w_out_ref,
    out_ref,
    next_ref,
):
    rows, count, depth = out_ref.shape
    width = flat_ref.shape[0] // rows

    def use(start, fresh):
        next_ref[start : start + fresh.shape[0]] = fresh

    finish_parts(1, groups, info_ref, came_ref, flat_ref, gate_ref, w_out_ref, use)
    pick = selection(info_ref[0:1], width)
    pick = dot_nt(interleave(1, count), pick).astype(BF16)
    lanes = [next_ref[row * width : (row + 1) * width] for row in range(rows)]
    lanes.append(jnp.ones((width, depth), BF16))
    spread = dot_nn(pick, jnp.concatenate(lanes, axis=1))
    kept = spread[:, rows * depth :] > 0.5
    for row in range(rows):
        fresh = spread[:, row * depth : (row + 1) * depth]
        out_ref[row] = jnp.where(kept, fresh, pair_ref[row].astype(F32)).astype(BF16)


SMEM = pl.BlockSpec(memory_space=pltpu.SMEM)
HBM = pl.BlockSpec(memory_space=pltpu.HBM)


VMEM = pl.BlockSpec(memory_space=pltpu.VMEM)


def call(body, name, outs, operands, specs=None, out_specs=None, scratch=()):
    return pl.pallas_call(
        body,
        out_shape=list(outs),
        in_specs=specs or [VMEM] * len(operands),
        out_specs=out_specs or [VMEM] * len(outs),
        scratch_shapes=list(scratch),
        compiler_params=pltpu.CompilerParams(vmem_limit_bytes=24 * 1024 * 1024),
        name=name,
    )(*operands)


def kept_columns(width, pair_rep, info, flat, gate, sent, w_proj, w_gate, w_out):
    devices = lax.axis_size("dap")
    rows, _, depth = pair_rep.shape
    hidden = w_out.shape[1]
    own = hidden // devices
    back_shape = jax.ShapeDtypeStruct((devices, 8, rows * own * width // 8), BF16)
    flat_shape = jax.ShapeDtypeStruct((rows * width, depth), BF16)
    gate_shape = jax.ShapeDtypeStruct((rows * width, depth), F32)
    sorted_shape = jax.ShapeDtypeStruct((4 * hidden, depth), BF16)

    apart = devices // GROUPS
    groups = [list(range(first, first + apart)) for first in range(0, devices, apart)]
    group_shape = jax.ShapeDtypeStruct((apart, 2 * own * GROUPS, rows * width), BF16)
    sums_shape = jax.ShapeDtypeStruct((devices, own * GROUPS, rows * width), BF16)

    def exchange(sent, within=None):
        return lax.all_to_all(
            sent, "dap", split_axis=0, concat_axis=0, axis_index_groups=within, tiled=True
        )

    sent = sent[:, :, : rows * width]
    came = exchange(sent)
    sent, weights = call(
        functools.partial(outgoing_kernel, rows, GROUPS),
        "outgoing",
        [back_shape, sorted_shape],
        (info, came, w_proj),
    )
    came = exchange(sent)
    flat, gate, sent = call(
        functools.partial(middle_kernel, rows),
        "finish_and_operands",
        [flat_shape, gate_shape, group_shape],
        (info, came, flat, gate, w_out, weights, w_gate),
    )
    came = exchange(sent, groups)
    sent = call(
        functools.partial(incoming_kernel, rows),
        "incoming",
        [sums_shape],
        (info, came),
    )[0]
    came = exchange(sent)
    return call(
        functools.partial(last_kernel, GROUPS),
        "finish",
        [jax.ShapeDtypeStruct(pair_rep.shape, BF16)],
        (info, pair_rep, came, flat, gate, w_out),
        scratch=[pltpu.VMEM(flat_shape.shape, BF16)],
    )[0]


def row_shards(pair_rep, chain_ids, crop_lengths, ln_in_gain, w_proj, w_gate, ln_out_gain, w_out):
    devices = lax.axis_size("dap")
    rows, count, depth = pair_rep.shape
    me = lax.axis_index("dap").reshape(1).astype(jnp.int32)
    ids = chain_ids.reshape(1, count)
    crops = crop_lengths.reshape(1, -1)
    widths = [count * share // 16 for share in SHARES]
    info_shape = jax.ShapeDtypeStruct((16, count), F32)
    flat_shape = jax.ShapeDtypeStruct((rows * count, depth), BF16)
    send_shape = jax.ShapeDtypeStruct((devices, w_proj.shape[2] // devices // 2, rows * count), BF16)
    gate_shape = jax.ShapeDtypeStruct(flat_shape.shape, F32)
    choice, info, flat, gate, sent = call(
        functools.partial(first_kernel, devices, widths),
        "first_operands",
        [
            pltpu.SMEM((1,), jnp.int32),
            info_shape,
            flat_shape,
            gate_shape,
            send_shape,
        ],
        [me]
        + [
            pltpu.with_memory_space_constraint(array, pltpu.HBM)
            for array in (ids, crops, ln_in_gain, ln_out_gain, w_proj, w_gate, pair_rep)
        ],
        specs=[SMEM] + [HBM] * 7,
        out_specs=[SMEM] + [VMEM] * 4,
        scratch=[
            pltpu.VMEM(ids.shape, jnp.int32),
            pltpu.VMEM(crops.shape, jnp.int32),
            pltpu.VMEM(ln_in_gain.shape, F32),
            pltpu.VMEM(ln_out_gain.shape, F32),
            pltpu.VMEM(w_proj.shape[1:], BF16),
            pltpu.VMEM(w_gate.shape[1:], BF16),
            pltpu.VMEM(pair_rep.shape, BF16),
            pltpu.VMEM(flat_shape.shape, BF16),
            pltpu.VMEM((w_proj.shape[2], depth), BF16),
            pltpu.SemaphoreType.DMA((7,)),
        ],
    )
    return lax.switch(
        choice[0],
        [functools.partial(kept_columns, some) for some in widths],
        pair_rep,
        info,
        flat,
        gate,
        sent,
        w_proj,
        w_gate,
        w_out,
    )


GROUPS = 2
SHARES = (11, 12, 13, 14, 16)


def solution(mesh):
    devices = mesh.shape["dap"]
    placed = (P("dap", "grp", None), P(), P(), P(), P(), P(), P(), P())

    def body(*arrays):
        rows, count, width = arrays[0].shape
        hidden = arrays[-1].shape[1]
        plain = (
            mesh.shape["grp"] == 1
            and rows * devices == count
            and count == 256
            and rows == 8
            and hidden == 4 * devices
        )
        return (row_shards if plain else shards)(*arrays)

    return jax.shard_map(
        body, mesh=mesh, in_specs=placed, out_specs=P("dap", "grp", None), check_vma=False
    )
```

```python
import functools

import jax
import jax.numpy as jnp
from jax import lax
from jax.experimental import pallas as pl
from jax.experimental.pallas import tpu as pltpu
from jax.sharding import PartitionSpec as P

epsilon_norm = 1e-05
F32 = jnp.float32
BF16 = jnp.bfloat16


def residue_valid(chain_ids, crop_lengths):
    count = chain_ids.shape[0]
    chains = jnp.arange(crop_lengths.shape[0], dtype=jnp.int32)
    member = (chain_ids[:, None] == chains[None, :]).astype(jnp.int32)
    counts = jnp.sum(member, axis=0)
    starts = jnp.cumsum(counts) - counts
    first = jnp.sum(member * starts[None, :], axis=1)
    limit = jnp.sum(member * crop_lengths[None, :], axis=1)
    place = jnp.arange(count, dtype=jnp.int32) - first
    return (place < limit).astype(jnp.float32)


def layer_norm(values, gain, axis):
    centre = jnp.mean(values, axis=axis, keepdims=True)
    spread = jnp.mean((values - centre) ** 2, axis=axis, keepdims=True)
    return (values - centre) * lax.rsqrt(spread + epsilon_norm) * gain


def column_rows(right_chan):
    return lax.all_to_all(right_chan, "grp", split_axis=1, concat_axis=2, tiled=True)


def update(pair_tile, pair_mask, ln_in, w_proj, w_gate, ln_out, w_out, outgoing):
    hidden = w_out.shape[0]
    normed = layer_norm(pair_tile.astype(jnp.float32), ln_in, 2).astype(jnp.bfloat16)
    projected = jnp.einsum("rqc,cf->frq", normed, w_proj, preferred_element_type=jnp.float32)
    gate_value = jax.nn.sigmoid(
        jnp.einsum("rqc,cd->rqd", normed, w_gate, preferred_element_type=jnp.float32)
    )
    left_op = (
        jax.nn.sigmoid(projected[:hidden]) * projected[hidden : 2 * hidden] * pair_mask
    ).astype(jnp.bfloat16)
    right_op = (
        jax.nn.sigmoid(projected[2 * hidden : 3 * hidden]) * projected[3 * hidden :] * pair_mask
    ).astype(jnp.bfloat16)
    left_chan, right_chan = (
        lax.all_to_all(left_op, "dap", split_axis=0, concat_axis=1, tiled=True),
        lax.all_to_all(right_op, "dap", split_axis=0, concat_axis=1, tiled=True),
    )
    if outgoing:
        right_rows = column_rows(right_chan)
        triangle = jnp.einsum(
            "hik,hjk->hij",
            lax.all_gather(left_chan, "grp", axis=2, tiled=True),
            right_rows,
            preferred_element_type=jnp.float32,
        )
    else:
        triangle = jnp.einsum(
            "hki,hkj->hij",
            lax.all_gather(left_chan, "grp", axis=2, tiled=True),
            right_chan,
            preferred_element_type=jnp.float32,
        )
    returned = lax.all_to_all(
        triangle.astype(jnp.bfloat16), "dap", split_axis=1, concat_axis=0, tiled=True
    )
    normed_product = layer_norm(returned.astype(jnp.float32), ln_out[:, None, None], 0).astype(
        jnp.bfloat16
    )
    update_term = jnp.einsum(
        "hrq,hd->rqd", normed_product, w_out, preferred_element_type=jnp.float32
    )
    return (pair_tile.astype(jnp.float32) + gate_value * update_term).astype(jnp.bfloat16)


def shards(pair_rep, chain_ids, crop_lengths, ln_in_gain, w_proj, w_gate, ln_out_gain, w_out):
    row_count = pair_rep.shape[0]
    column_count = pair_rep.shape[1]
    kept = residue_valid(chain_ids, crop_lengths)
    row_start = lax.axis_index("dap") * row_count
    column_start = lax.axis_index("grp") * column_count
    kept_rows = lax.dynamic_slice_in_dim(kept, row_start, row_count, 0)
    kept_columns = lax.dynamic_slice_in_dim(kept, column_start, column_count, 0)
    pair_mask = kept_rows[:, None] * kept_columns[None, :]
    pair_tile = pair_rep
    for layer_index, outgoing in ((0, True), (1, False)):
        pair_tile = update(
            pair_tile,
            pair_mask,
            ln_in_gain[layer_index],
            w_proj[layer_index],
            w_gate[layer_index],
            ln_out_gain[layer_index],
            w_out[layer_index],
            outgoing,
        )
    return pair_tile


def dot_nn(a, b):
    return lax.dot_general(a, b, (((1,), (0,)), ((), ())), preferred_element_type=F32)


def dot_nt(a, b):
    return lax.dot_general(a, b, (((1,), (1,)), ((), ())), preferred_element_type=F32)


def dot_tn(a, b):
    return lax.dot_general(a, b, (((0,), (0,)), ((), ())), preferred_element_type=F32)


def open_gate(half):
    return jnp.tanh(half) + 1.0


def halved(weights):
    return (weights.astype(F32) * 0.5).astype(BF16)


def one_hot(source, columns):
    place = lax.broadcasted_iota(jnp.int32, (source.shape[0], columns), 1)
    return jnp.where(place == source, 1.0, 0.0).astype(BF16)


def interleave(outer, inner):
    row = lax.broadcasted_iota(jnp.int32, (outer * inner, 1), 0)
    return one_hot((row % inner) * outer + row // inner, outer * inner)


def move(matrix, rows):
    return dot_nn(matrix, rows).astype(BF16)


def selection(slots, width):
    row = lax.broadcasted_iota(jnp.int32, (width, slots.shape[1]), 0).astype(F32)
    return jnp.where(row == slots, 1.0, 0.0).astype(BF16)


def kept_residues(ids, limits):
    place = lax.broadcasted_iota(jnp.int32, ids.shape, 1).astype(F32)
    kept = jnp.zeros(ids.shape, F32)
    for chain in range(limits.shape[1]):
        first = jnp.sum(jnp.where(ids < chain, 1.0, 0.0), axis=1, keepdims=True)
        limit = limits[:, chain : chain + 1].astype(F32)
        inside = jnp.where(ids == chain, 1.0, 0.0) * jnp.where(place - first < limit, 1.0, 0.0)
        kept = kept + inside
    return kept


def norm_rows(values, gain):
    centre = jnp.mean(values, axis=1, keepdims=True)
    apart = values - centre
    spread = jnp.mean(apart * apart, axis=1, keepdims=True)
    return (apart * lax.rsqrt(spread + epsilon_norm) * gain).astype(BF16)


def sort_projection(w_proj_ref, devices, sorted_ref):
    hidden = w_proj_ref.shape[1] // 4
    own = hidden // devices
    row = lax.broadcasted_iota(jnp.int32, (2 * hidden, 1), 0)
    side = (row % (2 * own)) // own
    order = one_hot(side * hidden + row // (2 * own) * own + row % own, 2 * hidden)
    for kind in range(2):
        sides = [
            w_proj_ref[:, block * hidden : (block + 1) * hidden] for block in (kind, kind + 2)
        ]
        rows = dot_nt(order, jnp.concatenate(sides, axis=1)) * 0.5
        sorted_ref[2 * hidden * kind : 2 * hidden * (kind + 1)] = rows.astype(BF16)


def project(normed, weights, info_ref, send_ref, rows, width, start):
    span = normed.shape[0]
    half = weights.shape[0] // 2
    place = start + lax.broadcasted_iota(jnp.int32, (1, span), 1)
    mask = jnp.zeros((1, span), F32)
    for row in range(rows):
        if isinstance(width, int) and not start - width < row * width < start + span:
            continue
        inside = jnp.where(place >= row * width, 1.0, 0.0)
        inside = inside * jnp.where(place < (row + 1) * width, 1.0, 0.0)
        mask = mask + inside * info_ref[ROWS + row : ROWS + row + 1, 0:1]
    projected = dot_nt(weights, normed)
    operand = open_gate(projected[:half]) * projected[half:] * mask
    shape = send_ref.shape[:2] + (span,)
    send_ref[:, :, start : start + span] = operand.astype(BF16).reshape(shape)


def spans(total):
    start = 0
    while start < total:
        span = min(256, total - start)
        yield start, span
        start += span


LN_IN, LN_OUT, ROWS = 2, 4, 8


def gain_of(info_ref, row, width):
    return info_ref[row : row + 1, :width]


def first_kernel(
    devices,
    widths,
    me_ref,
    ids_hbm,
    crop_hbm,
    ln_in_hbm,
    ln_out_hbm,
    w_proj_hbm,
    pair_hbm,
    choice_ref,
    info_ref,
    flat_ref,
    normed_ref,
    send_ref,
    ids_ref,
    crop_ref,
    ln_in_ref,
    ln_out_ref,
    w_proj_ref,
    pair_ref,
    weights_ref,
    arrived,
):
    moves = (
        (ids_hbm, ids_ref),
        (crop_hbm, crop_ref),
        (ln_in_hbm, ln_in_ref),
        (ln_out_hbm, ln_out_ref),
        (pair_hbm, pair_ref),
        (w_proj_hbm.at[0], w_proj_ref),
    )
    copies = [
        pltpu.make_async_copy(source, target, arrived.at[index])
        for index, (source, target) in enumerate(moves)
    ]
    for copy in copies:
        copy.start()
    rows, count, depth = pair_ref.shape
    flat_ref[...] = jnp.zeros(flat_ref.shape, BF16)
    normed_ref[...] = jnp.zeros(normed_ref.shape, BF16)
    info_ref[...] = jnp.zeros(info_ref.shape, F32)
    square = (count, count)
    up = lax.broadcasted_iota(jnp.int32, square, 0) < lax.broadcasted_iota(jnp.int32, square, 1)
    up = jnp.where(up, 1.0, 0.0).astype(BF16)
    by_row = interleave(rows, devices)
    for copy in copies[:4]:
        copy.wait()
    kept = kept_residues(ids_ref[...], crop_ref[...])
    total = jnp.sum(kept)
    choice = jnp.int32(0)
    width = jnp.int32(widths[0])
    for some, wider in zip(widths[:-1], widths[1:]):
        choice = choice + jnp.where(total > some, 1, 0).astype(jnp.int32)
        width = width + jnp.where(total > some, wider - some, 0).astype(jnp.int32)
    choice_ref[0] = choice
    place = lax.broadcasted_iota(jnp.int32, kept.shape, 1)
    for row in range(rows):
        own = jnp.where(place == me_ref[0] * rows + row, kept, 0.0)
        info_ref[ROWS + row : ROWS + row + 1] = jnp.broadcast_to(
            jnp.sum(own, axis=1, keepdims=True), kept.shape
        )
    rank = dot_nn(jnp.broadcast_to(kept, (8, count)).astype(BF16), up)[0:1]
    slots = jnp.where(kept > 0.0, rank, -1.0)
    info_ref[0:1] = slots
    info_ref[1:2] = dot_nt(jnp.broadcast_to(slots, (8, count)).astype(BF16), by_row)[0:1]
    info_ref[LN_IN : LN_IN + 2, :depth] = ln_in_ref[...]
    info_ref[LN_OUT : LN_OUT + 2, : ln_out_ref.shape[1]] = ln_out_ref[...]
    pick = selection(slots, count)
    for copy in copies[4:]:
        copy.wait()
    gain = ln_in_ref[0:1]
    lanes = [pair_ref[row] for row in range(rows)]
    lanes = lanes + [norm_rows(part.astype(F32), gain) for part in lanes]
    sort_projection(w_proj_ref, devices, weights_ref)
    packed = move(pick, jnp.concatenate(lanes, axis=1))
    for row in range(rows):
        here = pl.ds(pl.multiple_of(row * width, 16), count)
        flat_ref[here] = packed[:, row * depth : (row + 1) * depth]
        normed_ref[here] = packed[:, (rows + row) * depth : (rows + row + 1) * depth]
    for start, span in spans(rows * count):
        project(
            normed_ref[start : start + span],
            weights_ref[...],
            info_ref,
            send_ref,
            rows,
            width,
            start,
        )


def channel_blocks(came_ref, rows, width):
    devices, channels, total = came_ref.shape
    came = move(
        interleave(channels, devices), came_ref[...].reshape(devices * channels, total)
    )
    blocks = []
    for channel in range(channels):
        span = slice(channel * devices, (channel + 1) * devices)
        parts = [came[span, row * width : (row + 1) * width] for row in range(rows)]
        blocks.append(jnp.concatenate(parts, axis=0))
    return blocks


def outgoing_kernel(rows, groups, info_ref, came_ref, w_proj_ref, send_ref, sorted_ref):
    devices, both, total = came_ref.shape
    own = both // 2
    width = total // rows
    pick = selection(info_ref[1:2], width)
    blocks = channel_blocks(came_ref, rows, width)
    products = [
        dot_nt(blocks[channel], move(pick, blocks[own + channel])).astype(BF16)
        for channel in range(own)
    ]
    low = rows * own // 8
    to_device = interleave(devices, 8)
    for offset in range(low):
        parts = []
        for channel in range(own):
            for high in range(rows // low):
                row = high * low + offset
                parts.append(products[channel][row * devices : (row + 1) * devices])
        sent = move(to_device, jnp.concatenate(parts, axis=0))
        send_ref[:, :, offset * width : (offset + 1) * width] = sent.reshape(devices, 8, width)
    sort_projection(w_proj_ref.at[1], devices // groups, sorted_ref)


def incoming_kernel(rows, info_ref, came_ref, send_ref):
    own = came_ref.shape[1] // 2
    devices = send_ref.shape[0]
    width = came_ref.shape[2] // rows
    pick = selection(info_ref[1:2], width)
    pick = dot_nt(interleave(1, rows * devices), pick).astype(BF16)
    blocks = channel_blocks(came_ref, rows, width)
    products = [
        dot_nn(dot_nt(pick, blocks[channel]).astype(BF16), blocks[own + channel]).astype(BF16)
        for channel in range(own)
    ]
    to_device = interleave(devices, own)
    for row in range(rows):
        span = slice(row * devices, (row + 1) * devices)
        sent = move(to_device, jnp.concatenate([product[span] for product in products], axis=0))
        send_ref[:, :, row * width : (row + 1) * width] = sent.reshape(devices, own, width)


def finish_parts(layer, groups, info_ref, came_ref, flat_ref, normed_ref, w_gate_ref, w_out_ref, use):
    devices, eight, lanes = came_ref.shape
    hidden = w_out_ref.shape[1]
    high = devices * eight // hidden // groups
    square = lax.broadcasted_iota(jnp.int32, (hidden, hidden), 0) == lax.broadcasted_iota(
        jnp.int32, (hidden, hidden), 1
    )
    gain = gain_of(info_ref, LN_OUT + layer, hidden)
    gain = jnp.sum(jnp.where(square, gain, 0.0), axis=1, keepdims=True)
    w_gate = halved(w_gate_ref[layer])
    w_out = halved(w_out_ref[layer])
    for offset, span in spans(lanes):
        came = came_ref[:, :, offset : offset + span].reshape(devices * eight, span)
        if groups == 1:
            came = dot_nn(interleave(high, hidden), came)
        else:
            came = came.astype(F32)
            came = sum(came[hidden * group : hidden * (group + 1)] for group in range(groups))
        for part in range(high):
            block = came[part * hidden : (part + 1) * hidden]
            centre = jnp.mean(block, axis=0, keepdims=True)
            apart = block - centre
            spread = jnp.mean(apart * apart, axis=0, keepdims=True)
            normed = (apart * lax.rsqrt(spread + epsilon_norm) * gain).astype(BF16)
            term = dot_tn(normed, w_out)
            start = part * lanes + offset
            here = slice(start, start + span)
            gate = open_gate(dot_nn(normed_ref[here], w_gate))
            use(start, (flat_ref[here].astype(F32) + gate * term).astype(BF16))


def middle_kernel(
    rows,
    info_ref,
    came_ref,
    flat_ref,
    normed_ref,
    w_gate_ref,
    w_out_ref,
    weights_ref,
    next_ref,
    next_normed_ref,
    send_ref,
):
    gain = gain_of(info_ref, LN_IN + 1, flat_ref.shape[1])
    width = next_ref.shape[0] // rows

    def use(start, fresh):
        next_ref[start : start + fresh.shape[0]] = fresh

    finish_parts(0, 1, info_ref, came_ref, flat_ref, normed_ref, w_gate_ref, w_out_ref, use)
    for start, span in spans(rows * width):
        normed = norm_rows(next_ref[start : start + span].astype(F32), gain)
        next_normed_ref[start : start + span] = normed
        project(
            normed,
            weights_ref[...],
            info_ref,
            send_ref,
            rows,
            width,
            start,
        )


def last_kernel(
    groups,
    info_ref,
    pair_ref,
    came_ref,
    flat_ref,
    normed_ref,
    w_gate_ref,
    w_out_ref,
    out_ref,
    next_ref,
):
    rows, count, depth = out_ref.shape
    width = flat_ref.shape[0] // rows

    def use(start, fresh):
        next_ref[start : start + fresh.shape[0]] = fresh

    finish_parts(1, groups, info_ref, came_ref, flat_ref, normed_ref, w_gate_ref, w_out_ref, use)
    pick = selection(info_ref[0:1], width)
    pick = dot_nt(interleave(1, count), pick).astype(BF16)
    lanes = [next_ref[row * width : (row + 1) * width] for row in range(rows)]
    lanes.append(jnp.ones((width, depth), BF16))
    spread = dot_nn(pick, jnp.concatenate(lanes, axis=1))
    kept = spread[:, rows * depth :] > 0.5
    for row in range(rows):
        fresh = spread[:, row * depth : (row + 1) * depth]
        out_ref[row] = jnp.where(kept, fresh, pair_ref[row].astype(F32)).astype(BF16)


SMEM = pl.BlockSpec(memory_space=pltpu.SMEM)
HBM = pl.BlockSpec(memory_space=pltpu.HBM)


VMEM = pl.BlockSpec(memory_space=pltpu.VMEM)


def call(body, name, outs, operands, specs=None, out_specs=None, scratch=()):
    return pl.pallas_call(
        body,
        out_shape=list(outs),
        in_specs=specs or [VMEM] * len(operands),
        out_specs=out_specs or [VMEM] * len(outs),
        scratch_shapes=list(scratch),
        compiler_params=pltpu.CompilerParams(vmem_limit_bytes=24 * 1024 * 1024),
        name=name,
    )(*operands)


def kept_columns(width, pair_rep, info, flat, normed, sent, w_proj, w_gate, w_out):
    devices = lax.axis_size("dap")
    rows, _, depth = pair_rep.shape
    hidden = w_out.shape[1]
    own = hidden // devices
    back_shape = jax.ShapeDtypeStruct((devices, 8, rows * own * width // 8), BF16)
    flat_shape = jax.ShapeDtypeStruct((rows * width, depth), BF16)
    sorted_shape = jax.ShapeDtypeStruct((4 * hidden, depth), BF16)

    apart = devices // GROUPS
    groups = [list(range(first, first + apart)) for first in range(0, devices, apart)]
    group_shape = jax.ShapeDtypeStruct((apart, 2 * own * GROUPS, rows * width), BF16)
    sums_shape = jax.ShapeDtypeStruct((devices, own * GROUPS, rows * width), BF16)

    def exchange(sent, within=None):
        return lax.all_to_all(
            sent, "dap", split_axis=0, concat_axis=0, axis_index_groups=within, tiled=True
        )

    sent = sent[:, :, : rows * width]
    came = exchange(sent)
    sent, weights = call(
        functools.partial(outgoing_kernel, rows, GROUPS),
        "outgoing",
        [back_shape, sorted_shape],
        (info, came, w_proj),
    )
    came = exchange(sent)
    flat, normed, sent = call(
        functools.partial(middle_kernel, rows),
        "finish_and_operands",
        [flat_shape, flat_shape, group_shape],
        (info, came, flat, normed, w_gate, w_out, weights),
    )
    came = exchange(sent, groups)
    sent = call(
        functools.partial(incoming_kernel, rows),
        "incoming",
        [sums_shape],
        (info, came),
    )[0]
    came = exchange(sent)
    return call(
        functools.partial(last_kernel, GROUPS),
        "finish",
        [jax.ShapeDtypeStruct(pair_rep.shape, BF16)],
        (info, pair_rep, came, flat, normed, w_gate, w_out),
        scratch=[pltpu.VMEM(flat_shape.shape, BF16)],
    )[0]


def row_shards(pair_rep, chain_ids, crop_lengths, ln_in_gain, w_proj, w_gate, ln_out_gain, w_out):
    devices = lax.axis_size("dap")
    rows, count, depth = pair_rep.shape
    me = lax.axis_index("dap").reshape(1).astype(jnp.int32)
    ids = chain_ids.reshape(1, count)
    crops = crop_lengths.reshape(1, -1)
    widths = [count * share // 16 for share in SHARES]
    info_shape = jax.ShapeDtypeStruct((16, count), F32)
    flat_shape = jax.ShapeDtypeStruct((rows * count, depth), BF16)
    send_shape = jax.ShapeDtypeStruct((devices, w_proj.shape[2] // devices // 2, rows * count), BF16)
    choice, info, flat, normed, sent = call(
        functools.partial(first_kernel, devices, widths),
        "first_operands",
        [
            pltpu.SMEM((1,), jnp.int32),
            info_shape,
            flat_shape,
            flat_shape,
            send_shape,
        ],
        [me]
        + [
            pltpu.with_memory_space_constraint(array, pltpu.HBM)
            for array in (ids, crops, ln_in_gain, ln_out_gain, w_proj, pair_rep)
        ],
        specs=[SMEM] + [HBM] * 6,
        out_specs=[SMEM] + [VMEM] * 4,
        scratch=[
            pltpu.VMEM(ids.shape, jnp.int32),
            pltpu.VMEM(crops.shape, jnp.int32),
            pltpu.VMEM(ln_in_gain.shape, F32),
            pltpu.VMEM(ln_out_gain.shape, F32),
            pltpu.VMEM(w_proj.shape[1:], BF16),
            pltpu.VMEM(pair_rep.shape, BF16),
            pltpu.VMEM((w_proj.shape[2], depth), BF16),
            pltpu.SemaphoreType.DMA((6,)),
        ],
    )
    return lax.switch(
        choice[0],
        [functools.partial(kept_columns, some) for some in widths],
        pair_rep,
        info,
        flat,
        normed,
        sent,
        w_proj,
        w_gate,
        w_out,
    )


GROUPS = 2
SHARES = (11, 12, 13, 14, 16)


def solution(mesh):
    devices = mesh.shape["dap"]
    placed = (P("dap", "grp", None), P(), P(), P(), P(), P(), P(), P())

    def body(*arrays):
        rows, count, width = arrays[0].shape
        hidden = arrays[-1].shape[1]
        plain = (
            mesh.shape["grp"] == 1
            and rows * devices == count
            and count == 256
            and rows == 8
            and hidden == 4 * devices
        )
        return (row_shards if plain else shards)(*arrays)

    return jax.shard_map(
        body, mesh=mesh, in_specs=placed, out_specs=P("dap", "grp", None), check_vma=False
    )
```

```python
import functools

import jax
import jax.numpy as jnp
from jax import lax
from jax.experimental import pallas as pl
from jax.experimental.pallas import tpu as pltpu
from jax.sharding import PartitionSpec as P

epsilon_norm = 1e-05
F32 = jnp.float32
BF16 = jnp.bfloat16


def residue_valid(chain_ids, crop_lengths):
    count = chain_ids.shape[0]
    chains = jnp.arange(crop_lengths.shape[0], dtype=jnp.int32)
    member = (chain_ids[:, None] == chains[None, :]).astype(jnp.int32)
    counts = jnp.sum(member, axis=0)
    starts = jnp.cumsum(counts) - counts
    first = jnp.sum(member * starts[None, :], axis=1)
    limit = jnp.sum(member * crop_lengths[None, :], axis=1)
    place = jnp.arange(count, dtype=jnp.int32) - first
    return (place < limit).astype(jnp.float32)


def layer_norm(values, gain, axis):
    centre = jnp.mean(values, axis=axis, keepdims=True)
    spread = jnp.mean((values - centre) ** 2, axis=axis, keepdims=True)
    return (values - centre) * lax.rsqrt(spread + epsilon_norm) * gain


def column_rows(right_chan):
    return lax.all_to_all(right_chan, "grp", split_axis=1, concat_axis=2, tiled=True)


def update(pair_tile, pair_mask, ln_in, w_proj, w_gate, ln_out, w_out, outgoing):
    hidden = w_out.shape[0]
    normed = layer_norm(pair_tile.astype(jnp.float32), ln_in, 2).astype(jnp.bfloat16)
    projected = jnp.einsum("rqc,cf->frq", normed, w_proj, preferred_element_type=jnp.float32)
    gate_value = jax.nn.sigmoid(
        jnp.einsum("rqc,cd->rqd", normed, w_gate, preferred_element_type=jnp.float32)
    )
    left_op = (
        jax.nn.sigmoid(projected[:hidden]) * projected[hidden : 2 * hidden] * pair_mask
    ).astype(jnp.bfloat16)
    right_op = (
        jax.nn.sigmoid(projected[2 * hidden : 3 * hidden]) * projected[3 * hidden :] * pair_mask
    ).astype(jnp.bfloat16)
    left_chan, right_chan = (
        lax.all_to_all(left_op, "dap", split_axis=0, concat_axis=1, tiled=True),
        lax.all_to_all(right_op, "dap", split_axis=0, concat_axis=1, tiled=True),
    )
    if outgoing:
        right_rows = column_rows(right_chan)
        triangle = jnp.einsum(
            "hik,hjk->hij",
            lax.all_gather(left_chan, "grp", axis=2, tiled=True),
            right_rows,
            preferred_element_type=jnp.float32,
        )
    else:
        triangle = jnp.einsum(
            "hki,hkj->hij",
            lax.all_gather(left_chan, "grp", axis=2, tiled=True),
            right_chan,
            preferred_element_type=jnp.float32,
        )
    returned = lax.all_to_all(
        triangle.astype(jnp.bfloat16), "dap", split_axis=1, concat_axis=0, tiled=True
    )
    normed_product = layer_norm(returned.astype(jnp.float32), ln_out[:, None, None], 0).astype(
        jnp.bfloat16
    )
    update_term = jnp.einsum(
        "hrq,hd->rqd", normed_product, w_out, preferred_element_type=jnp.float32
    )
    return (pair_tile.astype(jnp.float32) + gate_value * update_term).astype(jnp.bfloat16)


def shards(pair_rep, chain_ids, crop_lengths, ln_in_gain, w_proj, w_gate, ln_out_gain, w_out):
    row_count = pair_rep.shape[0]
    column_count = pair_rep.shape[1]
    kept = residue_valid(chain_ids, crop_lengths)
    row_start = lax.axis_index("dap") * row_count
    column_start = lax.axis_index("grp") * column_count
    kept_rows = lax.dynamic_slice_in_dim(kept, row_start, row_count, 0)
    kept_columns = lax.dynamic_slice_in_dim(kept, column_start, column_count, 0)
    pair_mask = kept_rows[:, None] * kept_columns[None, :]
    pair_tile = pair_rep
    for layer_index, outgoing in ((0, True), (1, False)):
        pair_tile = update(
            pair_tile,
            pair_mask,
            ln_in_gain[layer_index],
            w_proj[layer_index],
            w_gate[layer_index],
            ln_out_gain[layer_index],
            w_out[layer_index],
            outgoing,
        )
    return pair_tile


def dot_nn(a, b):
    return lax.dot_general(a, b, (((1,), (0,)), ((), ())), preferred_element_type=F32)


def dot_nt(a, b):
    return lax.dot_general(a, b, (((1,), (1,)), ((), ())), preferred_element_type=F32)


def dot_tn(a, b):
    return lax.dot_general(a, b, (((0,), (0,)), ((), ())), preferred_element_type=F32)


def open_gate(half):
    return jnp.tanh(half) + 1.0


def halved(weights):
    return (weights.astype(F32) * 0.5).astype(BF16)


def one_hot(source, columns):
    place = lax.broadcasted_iota(jnp.int32, (source.shape[0], columns), 1)
    return jnp.where(place == source, 1.0, 0.0).astype(BF16)


def interleave(outer, inner):
    row = lax.broadcasted_iota(jnp.int32, (outer * inner, 1), 0)
    return one_hot((row % inner) * outer + row // inner, outer * inner)


def move(matrix, rows):
    return dot_nn(matrix, rows).astype(BF16)


def selection(slots, width):
    row = lax.broadcasted_iota(jnp.int32, (width, slots.shape[1]), 0).astype(F32)
    return jnp.where(row == slots, 1.0, 0.0).astype(BF16)


def kept_residues(ids, limits):
    place = lax.broadcasted_iota(jnp.int32, ids.shape, 1).astype(F32)
    kept = jnp.zeros(ids.shape, F32)
    for chain in range(limits.shape[1]):
        first = jnp.sum(jnp.where(ids < chain, 1.0, 0.0), axis=1, keepdims=True)
        limit = limits[:, chain : chain + 1].astype(F32)
        inside = jnp.where(ids == chain, 1.0, 0.0) * jnp.where(place - first < limit, 1.0, 0.0)
        kept = kept + inside
    return kept


def norm_rows(values, gain):
    centre = jnp.mean(values, axis=1, keepdims=True)
    apart = values - centre
    spread = jnp.mean(apart * apart, axis=1, keepdims=True)
    return (apart * lax.rsqrt(spread + epsilon_norm) * gain).astype(BF16)


def sort_projection(w_proj_ref, devices, sorted_ref):
    hidden = w_proj_ref.shape[1] // 4
    own = hidden // devices
    row = lax.broadcasted_iota(jnp.int32, (2 * hidden, 1), 0)
    side = (row % (2 * own)) // own
    order = one_hot(side * hidden + row // (2 * own) * own + row % own, 2 * hidden)
    for kind in range(2):
        sides = [
            w_proj_ref[:, block * hidden : (block + 1) * hidden] for block in (kind, kind + 2)
        ]
        rows = dot_nt(order, jnp.concatenate(sides, axis=1)) * 0.5
        sorted_ref[2 * hidden * kind : 2 * hidden * (kind + 1)] = rows.astype(BF16)


def project(normed, weights, w_gate, info_ref, gate_ref, send_ref, rows, width, start):
    span = normed.shape[0]
    half = weights.shape[0] // 2
    place = start + lax.broadcasted_iota(jnp.int32, (1, span), 1)
    mask = jnp.zeros((1, span), F32)
    for row in range(rows):
        if isinstance(width, int) and not start - width < row * width < start + span:
            continue
        inside = jnp.where(place >= row * width, 1.0, 0.0)
        inside = inside * jnp.where(place < (row + 1) * width, 1.0, 0.0)
        mask = mask + inside * info_ref[ROWS + row : ROWS + row + 1, 0:1]
    gate_ref[start : start + span] = open_gate(dot_nn(normed, w_gate))
    projected = dot_nt(weights, normed)
    operand = open_gate(projected[:half]) * projected[half:] * mask
    shape = send_ref.shape[:2] + (span,)
    send_ref[:, :, start : start + span] = operand.astype(BF16).reshape(shape)


def spans(total):
    start = 0
    while start < total:
        span = min(256, total - start)
        yield start, span
        start += span


LN_IN, LN_OUT, ROWS = 2, 4, 8


def gain_of(info_ref, row, width):
    return info_ref[row : row + 1, :width]


def first_kernel(
    devices,
    widths,
    me_ref,
    ids_hbm,
    crop_hbm,
    ln_in_hbm,
    ln_out_hbm,
    w_proj_hbm,
    w_gate_hbm,
    pair_hbm,
    choice_ref,
    info_ref,
    flat_ref,
    gate_ref,
    send_ref,
    ids_ref,
    crop_ref,
    ln_in_ref,
    ln_out_ref,
    w_proj_ref,
    w_gate_ref,
    pair_ref,
    normed_ref,
    weights_ref,
    arrived,
):
    moves = (
        (ids_hbm, ids_ref),
        (crop_hbm, crop_ref),
        (ln_in_hbm, ln_in_ref),
        (ln_out_hbm, ln_out_ref),
        (pair_hbm, pair_ref),
        (w_proj_hbm.at[0], w_proj_ref),
        (w_gate_hbm.at[0], w_gate_ref),
    )
    copies = [
        pltpu.make_async_copy(source, target, arrived.at[index])
        for index, (source, target) in enumerate(moves)
    ]
    for copy in copies:
        copy.start()
    rows, count, depth = pair_ref.shape
    flat_ref[...] = jnp.zeros(flat_ref.shape, BF16)
    normed_ref[...] = jnp.zeros(normed_ref.shape, BF16)
    info_ref[...] = jnp.zeros(info_ref.shape, F32)
    square = (count, count)
    up = lax.broadcasted_iota(jnp.int32, square, 0) < lax.broadcasted_iota(jnp.int32, square, 1)
    up = jnp.where(up, 1.0, 0.0).astype(BF16)
    by_row = interleave(rows, devices)
    for copy in copies[:4]:
        copy.wait()
    kept = kept_residues(ids_ref[...], crop_ref[...])
    total = jnp.sum(kept)
    choice = jnp.int32(0)
    width = jnp.int32(widths[0])
    for some, wider in zip(widths[:-1], widths[1:]):
        choice = choice + jnp.where(total > some, 1, 0).astype(jnp.int32)
        width = width + jnp.where(total > some, wider - some, 0).astype(jnp.int32)
    choice_ref[0] = choice
    place = lax.broadcasted_iota(jnp.int32, kept.shape, 1)
    for row in range(rows):
        own = jnp.where(place == me_ref[0] * rows + row, kept, 0.0)
        info_ref[ROWS + row : ROWS + row + 1] = jnp.broadcast_to(
            jnp.sum(own, axis=1, keepdims=True), kept.shape
        )
    rank = dot_nn(jnp.broadcast_to(kept, (8, count)).astype(BF16), up)[0:1]
    slots = jnp.where(kept > 0.0, rank, -1.0)
    info_ref[0:1] = slots
    info_ref[1:2] = dot_nt(jnp.broadcast_to(slots, (8, count)).astype(BF16), by_row)[0:1]
    info_ref[LN_IN : LN_IN + 2, :depth] = ln_in_ref[...]
    info_ref[LN_OUT : LN_OUT + 2, : ln_out_ref.shape[1]] = ln_out_ref[...]
    pick = selection(slots, count)
    for copy in copies[4:]:
        copy.wait()
    gain = ln_in_ref[0:1]
    lanes = [pair_ref[row] for row in range(rows)]
    lanes = lanes + [norm_rows(part.astype(F32), gain) for part in lanes]
    sort_projection(w_proj_ref, devices, weights_ref)
    packed = move(pick, jnp.concatenate(lanes, axis=1))
    for row in range(rows):
        here = pl.ds(pl.multiple_of(row * width, 16), count)
        flat_ref[here] = packed[:, row * depth : (row + 1) * depth]
        normed_ref[here] = packed[:, (rows + row) * depth : (rows + row + 1) * depth]
    w_gate = halved(w_gate_ref[...])
    for start, span in spans(rows * count):
        project(
            normed_ref[start : start + span],
            weights_ref[...],
            w_gate,
            info_ref,
            gate_ref,
            send_ref,
            rows,
            width,
            start,
        )


def channel_blocks(came_ref, rows, width):
    devices, channels, total = came_ref.shape
    came = move(
        interleave(channels, devices), came_ref[...].reshape(devices * channels, total)
    )
    blocks = []
    for channel in range(channels):
        span = slice(channel * devices, (channel + 1) * devices)
        parts = [came[span, row * width : (row + 1) * width] for row in range(rows)]
        blocks.append(jnp.concatenate(parts, axis=0))
    return blocks


def outgoing_kernel(rows, groups, info_ref, came_ref, w_proj_ref, send_ref, sorted_ref):
    devices, both, total = came_ref.shape
    own = both // 2
    width = total // rows
    pick = selection(info_ref[1:2], width)
    blocks = channel_blocks(came_ref, rows, width)
    products = [
        dot_nt(blocks[channel], move(pick, blocks[own + channel])).astype(BF16)
        for channel in range(own)
    ]
    low = rows * own // 8
    to_device = interleave(devices, 8)
    for offset in range(low):
        parts = []
        for channel in range(own):
            for high in range(rows // low):
                row = high * low + offset
                parts.append(products[channel][row * devices : (row + 1) * devices])
        sent = move(to_device, jnp.concatenate(parts, axis=0))
        send_ref[:, :, offset * width : (offset + 1) * width] = sent.reshape(devices, 8, width)
    sort_projection(w_proj_ref.at[1], devices // groups, sorted_ref)


def incoming_kernel(rows, info_ref, came_ref, send_ref):
    own = came_ref.shape[1] // 2
    devices = send_ref.shape[0]
    width = came_ref.shape[2] // rows
    pick = selection(info_ref[1:2], width)
    pick = dot_nt(interleave(1, rows * devices), pick).astype(BF16)
    blocks = channel_blocks(came_ref, rows, width)
    products = [
        dot_nn(dot_nt(pick, blocks[channel]).astype(BF16), blocks[own + channel]).astype(BF16)
        for channel in range(own)
    ]
    to_device = interleave(devices, own)
    for row in range(rows):
        span = slice(row * devices, (row + 1) * devices)
        sent = move(to_device, jnp.concatenate([product[span] for product in products], axis=0))
        send_ref[:, :, row * width : (row + 1) * width] = sent.reshape(devices, own, width)


def finish_parts(layer, groups, info_ref, came_ref, flat_ref, gate_ref, w_out_ref, use):
    devices, eight, lanes = came_ref.shape
    hidden = w_out_ref.shape[1]
    high = devices * eight // hidden // groups
    square = lax.broadcasted_iota(jnp.int32, (hidden, hidden), 0) == lax.broadcasted_iota(
        jnp.int32, (hidden, hidden), 1
    )
    gain = gain_of(info_ref, LN_OUT + layer, hidden)
    gain = jnp.sum(jnp.where(square, gain, 0.0), axis=1, keepdims=True)
    w_out = halved(w_out_ref[layer])
    for offset, span in spans(lanes):
        came = came_ref[:, :, offset : offset + span].reshape(devices * eight, span)
        if groups == 1:
            came = dot_nn(interleave(high, hidden), came)
        else:
            came = came.astype(F32)
            came = sum(came[hidden * group : hidden * (group + 1)] for group in range(groups))
        for part in range(high):
            block = came[part * hidden : (part + 1) * hidden]
            centre = jnp.mean(block, axis=0, keepdims=True)
            apart = block - centre
            spread = jnp.mean(apart * apart, axis=0, keepdims=True)
            normed = (apart * lax.rsqrt(spread + epsilon_norm) * gain).astype(BF16)
            term = dot_tn(normed, w_out)
            start = part * lanes + offset
            here = slice(start, start + span)
            use(start, (flat_ref[here].astype(F32) + gate_ref[here] * term).astype(BF16))


def middle_kernel(
    rows,
    info_ref,
    came_ref,
    flat_ref,
    gate_ref,
    w_out_ref,
    weights_ref,
    w_gate_ref,
    next_ref,
    next_gate_ref,
    send_ref,
):
    gain = gain_of(info_ref, LN_IN + 1, flat_ref.shape[1])
    width = next_ref.shape[0] // rows

    def use(start, fresh):
        next_ref[start : start + fresh.shape[0]] = fresh

    finish_parts(0, 1, info_ref, came_ref, flat_ref, gate_ref, w_out_ref, use)
    w_gate = halved(w_gate_ref[1])
    for start, span in spans(rows * width):
        project(
            norm_rows(next_ref[start : start + span].astype(F32), gain),
            weights_ref[...],
            w_gate,
            info_ref,
            next_gate_ref,
            send_ref,
            rows,
            width,
            start,
        )


def last_kernel(
    groups,
    info_ref,
    pair_ref,
    came_ref,
    flat_ref,
    gate_ref,
    w_out_ref,
    out_ref,
    next_ref,
):
    rows, count, depth = out_ref.shape
    width = flat_ref.shape[0] // rows

    def use(start, fresh):
        next_ref[start : start + fresh.shape[0]] = fresh

    finish_parts(1, groups, info_ref, came_ref, flat_ref, gate_ref, w_out_ref, use)
    pick = selection(info_ref[0:1], width)
    pick = dot_nt(interleave(1, count), pick).astype(BF16)
    lanes = [next_ref[row * width : (row + 1) * width] for row in range(rows)]
    lanes.append(jnp.ones((width, depth), BF16))
    spread = dot_nn(pick, jnp.concatenate(lanes, axis=1))
    kept = spread[:, rows * depth :] > 0.5
    for row in range(rows):
        fresh = spread[:, row * depth : (row + 1) * depth]
        out_ref[row] = jnp.where(kept, fresh, pair_ref[row].astype(F32)).astype(BF16)


SMEM = pl.BlockSpec(memory_space=pltpu.SMEM)
HBM = pl.BlockSpec(memory_space=pltpu.HBM)


VMEM = pl.BlockSpec(memory_space=pltpu.VMEM)


def call(body, name, outs, operands, specs=None, out_specs=None, scratch=()):
    return pl.pallas_call(
        body,
        out_shape=list(outs),
        in_specs=specs or [VMEM] * len(operands),
        out_specs=out_specs or [VMEM] * len(outs),
        scratch_shapes=list(scratch),
        compiler_params=pltpu.CompilerParams(vmem_limit_bytes=24 * 1024 * 1024),
        name=name,
    )(*operands)


def kept_columns(width, pair_rep, info, flat, gate, sent, w_proj, w_gate, w_out):
    devices = lax.axis_size("dap")
    rows, _, depth = pair_rep.shape
    hidden = w_out.shape[1]
    own = hidden // devices
    back_shape = jax.ShapeDtypeStruct((devices, 8, rows * own * width // 8), BF16)
    flat_shape = jax.ShapeDtypeStruct((rows * width, depth), BF16)
    gate_shape = jax.ShapeDtypeStruct((rows * width, depth), F32)
    sorted_shape = jax.ShapeDtypeStruct((4 * hidden, depth), BF16)

    apart = devices // GROUPS
    groups = [list(range(first, first + apart)) for first in range(0, devices, apart)]
    group_shape = jax.ShapeDtypeStruct((apart, 2 * own * GROUPS, rows * width), BF16)
    sums_shape = jax.ShapeDtypeStruct((devices, own * GROUPS, rows * width), BF16)

    def exchange(sent, within=None):
        return lax.all_to_all(
            sent, "dap", split_axis=0, concat_axis=0, axis_index_groups=within, tiled=True
        )

    sent = sent[:, :, : rows * width]
    came = exchange(sent)
    sent, weights = call(
        functools.partial(outgoing_kernel, rows, GROUPS),
        "outgoing",
        [back_shape, sorted_shape],
        (info, came, w_proj),
    )
    came = exchange(sent)
    flat, gate, sent = call(
        functools.partial(middle_kernel, rows),
        "finish_and_operands",
        [flat_shape, gate_shape, group_shape],
        (info, came, flat, gate, w_out, weights, w_gate),
    )
    came = exchange(sent, groups)
    sent = call(
        functools.partial(incoming_kernel, rows),
        "incoming",
        [sums_shape],
        (info, came),
    )[0]
    came = exchange(sent)
    return call(
        functools.partial(last_kernel, GROUPS),
        "finish",
        [jax.ShapeDtypeStruct(pair_rep.shape, BF16)],
        (info, pair_rep, came, flat, gate, w_out),
        scratch=[pltpu.VMEM(flat_shape.shape, BF16)],
    )[0]


def row_shards(pair_rep, chain_ids, crop_lengths, ln_in_gain, w_proj, w_gate, ln_out_gain, w_out):
    devices = lax.axis_size("dap")
    rows, count, depth = pair_rep.shape
    me = lax.axis_index("dap").reshape(1).astype(jnp.int32)
    ids = chain_ids.reshape(1, count)
    crops = crop_lengths.reshape(1, -1)
    widths = [count * share // 16 for share in SHARES]
    info_shape = jax.ShapeDtypeStruct((16, count), F32)
    flat_shape = jax.ShapeDtypeStruct((rows * count, depth), BF16)
    send_shape = jax.ShapeDtypeStruct((devices, w_proj.shape[2] // devices // 2, rows * count), BF16)
    gate_shape = jax.ShapeDtypeStruct(flat_shape.shape, F32)
    choice, info, flat, gate, sent = call(
        functools.partial(first_kernel, devices, widths),
        "first_operands",
        [
            pltpu.SMEM((1,), jnp.int32),
            info_shape,
            flat_shape,
            gate_shape,
            send_shape,
        ],
        [me]
        + [
            pltpu.with_memory_space_constraint(array, pltpu.HBM)
            for array in (ids, crops, ln_in_gain, ln_out_gain, w_proj, w_gate, pair_rep)
        ],
        specs=[SMEM] + [HBM] * 7,
        out_specs=[SMEM] + [VMEM] * 4,
        scratch=[
            pltpu.VMEM(ids.shape, jnp.int32),
            pltpu.VMEM(crops.shape, jnp.int32),
            pltpu.VMEM(ln_in_gain.shape, F32),
            pltpu.VMEM(ln_out_gain.shape, F32),
            pltpu.VMEM(w_proj.shape[1:], BF16),
            pltpu.VMEM(w_gate.shape[1:], BF16),
            pltpu.VMEM(pair_rep.shape, BF16),
            pltpu.VMEM(flat_shape.shape, BF16),
            pltpu.VMEM((w_proj.shape[2], depth), BF16),
            pltpu.SemaphoreType.DMA((7,)),
        ],
    )
    return lax.switch(
        choice[0],
        [functools.partial(kept_columns, some) for some in widths],
        pair_rep,
        info,
        flat,
        gate,
        sent,
        w_proj,
        w_gate,
        w_out,
    )


GROUPS = 2
SHARES = (12, 13, 14, 15, 16)


def solution(mesh):
    devices = mesh.shape["dap"]
    placed = (P("dap", "grp", None), P(), P(), P(), P(), P(), P(), P())

    def body(*arrays):
        rows, count, width = arrays[0].shape
        hidden = arrays[-1].shape[1]
        plain = (
            mesh.shape["grp"] == 1
            and rows * devices == count
            and count == 256
            and rows == 8
            and hidden == 4 * devices
        )
        return (row_shards if plain else shards)(*arrays)

    return jax.shard_map(
        body, mesh=mesh, in_specs=placed, out_specs=P("dap", "grp", None), check_vma=False
    )
```
